256 devices in a mesh: gx: 32 (over x, z), gy: 8 (over y, core).
Axes of the slice: x: 4, y: 4, z: 8, core: 2. Of those that a mesh axis runs over, the one named last changes fastest.
Arguments:
- right_sides: float32 [2, 512, 512, 128], P(None, 'gx', 'gy'), may hold values from -24 to 24, as said below
- diagonal: float32 [512, 512, 128], P('gx', 'gy'), may hold values from 0.5 to 2
- velocity: float32 [3, 512, 512, 128], P(None, 'gx', 'gy'), may hold values from -0.6 to 0.6
Outputs:
- orthonormal: float32 [10, 512, 512, 128], P(None, 'gx', 'gy')
- triangle: float32 [10, 10], replicated
- update: float32 [2, 512, 512, 128], P(None, 'gx', 'gy')
The draws below stay inside these ranges and needn't reach their ends.
Inputs may be any that keep to these rules, and one draw needn't show every extreme that they name: `right_sides`: 2 right-hand sides.
All inputs are finite; a program needn't handle non-finite values.
Results may differ from the reference program's by a relative error of at most 0.0004.
Values sent between devices are 32-bit elements; how exact they have to be, the bound alone decides.
No kernel may reach another device: no remote copies, remote signals or barrier semaphores. Data moves between devices by JAX's collectives and lax.ppermute only.
A program may use at most 128 MiB of HBM per device.

```python
import math
import jax
import jax.numpy as jnp
from jax import lax

S = 4
RHS = 2
COLS = 10
NX = 512
NY = 512
NZ = 128


def draw_right_sides(key, part):
    key = jax.random.fold_in(key, 5)
    first, second = jax.random.split(key, 2)
    shape = (RHS, NX, NY, NZ)
    along = jnp.arange(NX, dtype=jnp.float32) / NX
    ramp = jnp.exp(math.log(3.0) * along)[None, :, None, None]
    rough = jnp.clip(jax.random.normal(first, shape, jnp.float32), -4.0, 4.0)
    scales = jnp.exp(jax.random.uniform(second, shape, jnp.float32, 0.0, math.log(10.0)))
    values = rough * scales * ramp / 5.0
    return values.astype(jnp.float32)


def block_scale(own_key, extent, shards, smallest, high):
    level, own = 1.0, jax.random.fold_in(own_key, 6)
    for dim, shards_of in shards:
        draws = jnp.exp(jax.random.uniform(jax.random.fold_in(own, dim), (shards_of,), jnp.float32, smallest / len(shards), high / len(shards)))
        level = level * jnp.repeat(draws, extent[dim] // shards_of).reshape([-1 if axis == dim else 1 for axis in range(len(extent))])
    return level


def setup_inputs(seed: int = 0) -> dict:
    arg_keys = jax.random.split(jax.random.key(seed), 4)
    right_sides = draw_right_sides(jax.random.fold_in(arg_keys[3], 71), 0)
    diagonal = jnp.clip(0.5 + 1.5 * jax.random.uniform(arg_keys[1], (NX, NY, NZ), jnp.float32) ** block_scale(arg_keys[1], (NX, NY, NZ), ((0, 32), (1, 8)), -0.2, 0.2), 0.5, 2.0)
    velocity = jnp.clip(jax.random.uniform(arg_keys[2], (3, NX, NY, NZ), jnp.float32, -0.6, 0.6) * block_scale(arg_keys[2], (3, NX, NY, NZ), ((1, 32), (2, 8)), -0.4, 0.0), -0.6, 0.6)
    return dict(right_sides=right_sides, diagonal=diagonal, velocity=velocity)


def combine(padded, velocity, diagonal):
    summed = (1.0 + velocity[0]) * padded[:, :-2, 1:-1, 1:-1] + (1.0 - velocity[0]) * padded[:, 2:, 1:-1, 1:-1]
    summed = summed + (1.0 + velocity[1]) * padded[:, 1:-1, :-2, 1:-1] + (1.0 - velocity[1]) * padded[:, 1:-1, 2:, 1:-1]
    summed = summed + (1.0 + velocity[2]) * padded[:, 1:-1, 1:-1, :-2] + (1.0 - velocity[2]) * padded[:, 1:-1, 1:-1, 2:]
    return summed / (6.0 + diagonal)

def spread(field, velocity, diagonal):
    return combine(jnp.pad(field, ((0, 0), (1, 1), (1, 1), (1, 1))), velocity, diagonal)

def orthonormalize(columns):
    count = columns.shape[0]
    vectors = []
    factor = jnp.zeros((count, count), jnp.float32)
    for column in range(count):
        current = columns[column]
        for earlier in range(column):
            weight = jnp.sum(vectors[earlier] * current)
            current = current - weight * vectors[earlier]
            factor = factor.at[earlier, column].set(weight)
        length = jnp.sqrt(jnp.sum(current * current))
        factor = factor.at[column, column].set(length)
        vectors.append(current / length)
    return (jnp.stack(vectors), factor)

def back_substitute(upper, target):
    count = upper.shape[0]
    rows = [None] * count
    for index in reversed(range(count)):
        value = target[index]
        for later in range(index + 1, count):
            value = value - upper[index, later] * rows[later]
        rows[index] = value / upper[index, index]
    return jnp.stack(rows)

def least_squares(triangle):
    image = triangle[:, :RHS * S] - triangle[:, RHS:]
    basis_m, upper = orthonormalize(image.T)
    target = jnp.dot(basis_m, triangle[:, :RHS], precision=lax.Precision.HIGHEST)
    return back_substitute(upper, target)

def reference(right_sides, diagonal, velocity):
    current = right_sides
    degrees = [current]
    for degree in range(S):
        current = spread(current, velocity, diagonal)
        degrees.append(current)
    basis = jnp.stack(degrees).reshape(COLS, NX * NY * NZ)
    factor_q, factor_r = jnp.linalg.qr(basis.T)
    signs = jnp.sign(jnp.diagonal(factor_r))
    scale = math.sqrt(NX * NY * NZ)
    triangle = signs[:, None] * factor_r / scale
    orthonormal = ((factor_q * signs[None, :]).T * scale).reshape(COLS, NX, NY, NZ)
    coefficients = least_squares(triangle)
    update = jnp.dot(coefficients.T, basis[:RHS * S], precision=lax.Precision.HIGHEST).reshape(RHS, NX, NY, NZ)
    return (orthonormal, triangle, update)
```

```python
import functools
import math

import jax
import jax.numpy as jnp
from jax import lax
from jax.experimental import pallas as pl
from jax.experimental.pallas import tpu as pltpu
from jax.sharding import PartitionSpec as P

S = 4
RHS = 2
COLS = 10
YP = 16
VMEM_LIMIT = 56 * 1024 * 1024

F32 = jnp.float32
FIELD_CORNER = [(dx, dy) for dx in (1, 2, 3) for dy in (1, 2, 3) if dx + dy <= 4]
COEF_CORNER = [(dx, dy) for dx in (1, 2) for dy in (1, 2) if dx + dy <= 3]
CORNER_ROWS = RHS * len(FIELD_CORNER) + 4 * len(COEF_CORNER)


def slot(i, k):
    return (8 * k if k < 8 else 64 + 16 * (k - 8)) + i


def run_copies(copies):
    for copy in copies:
        copy.start()
    for copy in copies:
        copy.wait()


def pack_x_kernel(X, rhs, vel, diag, low, high, sems):
    copies = []
    for out, at4, at3 in ((high, X - 4, X - 3), (low, 0, 0)):
        for f in range(RHS):
            copies.append((rhs.at[f, pl.ds(at4, 4)], out.at[pl.ds(4 * f, 4)]))
        for c in range(3):
            copies.append((vel.at[c, pl.ds(at3, 3)], out.at[pl.ds(8 + 3 * c, 3)]))
        copies.append((diag.at[pl.ds(at3, 3)], out.at[pl.ds(17, 3)]))
    run_copies([pltpu.make_async_copy(s, d, sems.at[i]) for i, (s, d) in enumerate(copies)])


def pack_y_kernel(X, Y, rhs, vel, diag, low, high, c_ll, c_lh, c_hl, c_hh, stage, sems):
    copies = []
    for out, at in ((high, Y - 8), (low, 0)):
        copies.append((rhs.at[:, :, pl.ds(at, 8)], out.at[pl.ds(0, 2)]))
        copies.append((vel.at[:, :, pl.ds(at, 8)], out.at[pl.ds(2, 3)]))
        copies.append((diag.at[:, pl.ds(at, 8)], out.at[5]))
    for n, (ax, ay) in enumerate(((0, 0), (0, Y - 8), (X - 3, 0), (X - 3, Y - 8))):
        copies.append((rhs.at[:, pl.ds(ax, 3), pl.ds(ay, 8)], stage.at[n, pl.ds(0, 2)]))
        copies.append((vel.at[:, pl.ds(ax, 3), pl.ds(ay, 8)], stage.at[n, pl.ds(2, 3)]))
        copies.append((diag.at[pl.ds(ax, 3), pl.ds(ay, 8)], stage.at[n, 5]))
    run_copies([pltpu.make_async_copy(s, d, sems.at[i]) for i, (s, d) in enumerate(copies)])
    for n, out in enumerate((c_ll, c_lh, c_hl, c_hh)):
        row = 0
        for f in range(6):
            for dx, dy in FIELD_CORNER if f < 2 else COEF_CORNER:
                x = dx - 1 if n < 2 else 3 - dx
                y = dy - 1 if n % 2 == 0 else 8 - dy
                out[row : row + 1, :] = stage[n, f, x, y : y + 1, :]
                row += 1


def total(x):
    return jnp.sum(jnp.sum(x, axis=0, keepdims=True), axis=1, keepdims=True)


def fold8(x):
    rows = x.shape[0]
    parts = [x[8 * i : 8 * i + 8] for i in range(rows // 8)]
    while len(parts) > 1:
        parts = [a + b for a, b in zip(parts[::2], parts[1::2])] + (
            [parts[-1]] if len(parts) % 2 else []
        )
    return parts[0]


def main_kernel(
    X, Y, rhs, vel, diag, xl, xh, yl, yh, c_ll, c_lh, c_hl, c_hh,
    basis, packed, V, V4, U, A, Q, sems, out_sems,
):
    gx, gy = lax.axis_index("gx"), lax.axis_index("gy")
    nx, ny = lax.axis_size("gx"), lax.axis_size("gy")
    XE, YE = X + 8, Y + 2 * YP
    own_x, own_y = pl.ds(4, X), pl.ds(YP, Y)
    copies = [
        (rhs, V.at[0, :, own_x, own_y]),
        (vel, U.at[pl.ds(0, 3), own_x, own_y]),
        (diag, U.at[3, own_x, own_y]),
        (yl.at[pl.ds(0, 2)], V.at[0, :, own_x, pl.ds(YP - 8, 8)]),
        (yl.at[pl.ds(2, 4)], U.at[:, own_x, pl.ds(YP - 8, 8)]),
        (yh.at[pl.ds(0, 2)], V.at[0, :, own_x, pl.ds(YP + Y, 8)]),
        (yh.at[pl.ds(2, 4)], U.at[:, own_x, pl.ds(YP + Y, 8)]),
    ]
    for got, at4, at3 in ((xl, 0, 1), (xh, X + 4, X + 4)):
        for f in range(RHS):
            copies.append((got.at[pl.ds(4 * f, 4)], V.at[0, f, pl.ds(at4, 4), own_y]))
        for c in range(4):
            copies.append((got.at[pl.ds(8 + 3 * c, 3)], U.at[c, pl.ds(at3, 3), own_y]))
    run_copies([pltpu.make_async_copy(s, d, sems.at[i]) for i, (s, d) in enumerate(copies)])
    for n, got in enumerate((c_ll, c_lh, c_hl, c_hh)):
        row = 0
        for f in range(6):
            for dx, dy in FIELD_CORNER if f < 2 else COEF_CORNER:
                x = 4 - dx if n < 2 else X + 3 + dx
                y = YP - dy if n % 2 == 0 else YP + Y - 1 + dy
                value = got[row : row + 1, :]
                if f < 2:
                    V[0, f, x, y : y + 1, :] = value
                else:
                    U[f - 2, x, y : y + 1, :] = value
                row += 1

    WIDE = Y + 16
    inner = pl.ds(YP - 8, WIDE)
    yi = lax.broadcasted_iota(jnp.int32, (WIDE, 128), 0)
    zi = lax.broadcasted_iota(jnp.int32, (WIDE, 128), 1)
    y_in = ((yi >= 8) | (gy > 0)) & ((yi < Y + 8) | (gy < ny - 1))

    def coefficients(x, carry):
        x_in = ((x >= 4) | (gx > 0)) & ((x < X + 4) | (gx < nx - 1))
        g = jnp.where(y_in & x_in, 1.0 / (6.0 + U[3, x, inner, :]), 0.0)
        for c in range(3):
            ug = U[c, x, inner, :] * g
            plus, minus = g + ug, g - ug
            if c == 2:
                plus = jnp.where(zi == 0, 0.0, plus)
                minus = jnp.where(zi == 127, 0.0, minus)
            A[2 * c, x, inner, :] = plus
            A[2 * c + 1, x, inner, :] = minus
        return carry

    lax.fori_loop(1, XE - 1, coefficients, 0)

    def step(source, store, first, last, begin, rows, chunk):
        def row(x, carry):
            for at in range(begin, begin + rows, chunk):
                here = pl.ds(at, chunk)
                a = [A[c, x, here, :] for c in range(6)]
                for f in range(RHS):
                    centre = source[f, x, here, :]
                    value = a[0] * source[f, x - 1, here, :] + a[1] * source[f, x + 1, here, :]
                    value += a[2] * source[f, x, pl.ds(at - 1, chunk), :]
                    value += a[3] * source[f, x, pl.ds(at + 1, chunk), :]
                    value += a[4] * pltpu.roll(centre, 1, 1)
                    value += a[5] * pltpu.roll(centre, 127, 1)
                    store(f, x, at, chunk, value)
            return carry

        lax.fori_loop(first, last, row, 0)

    outs = []

    def send(k, source):
        copy = pltpu.make_async_copy(source, basis.at[pl.ds(2 * (k - 1), 2)], out_sems.at[k - 1])
        copy.start()
        outs.append(copy)

    for k in range(1, S):

        def store(f, x, at, chunk, value, k=k):
            V[k, f, x, pl.ds(at, chunk), :] = value

        step(V.at[k - 1], store, k, XE - k, YP - 8, WIDE, 40)
        send(k, V.at[k, :, own_x, own_y])

    def store4(f, x, at, chunk, value):
        V4[f, x - 4, pl.ds(at - YP, chunk), :] = value

    step(V.at[S - 1], store4, 4, X + 4, YP, Y, 32)
    send(S, V4)

    def original(k, x, at, size):
        if k >= 8:
            return V4[k - 8, x, pl.ds(at, size), :]
        return V[k // 2, k % 2, x + 4, pl.ds(YP + at, size), :]

    CH = 32
    zero = jnp.zeros((8, 128), F32)

    def first_dots(x, accs):
        accs = list(accs)
        for at in range(0, Y, CH):
            q = original(0, x, at, CH)
            for k in range(COLS):
                accs[k] = accs[k] + fold8(q * original(k, x, at, CH))
        return tuple(accs)

    accs = lax.fori_loop(0, X, first_dots, (zero,) * COLS)
    lane = lax.broadcasted_iota(jnp.int32, (1, 128), 1)
    line = jnp.zeros((1, 128), F32)
    for j in range(COLS):
        dots = [total(a) for a in accs]
        norm2 = dots[0]
        live = norm2 > 0.0
        safe = jnp.where(live, norm2, 1.0)
        length = jnp.sqrt(safe)
        inv = jnp.where(live, 1.0 / length, 0.0)
        for k in range(j, COLS):
            entry = dots[k - j] * inv
            line = jnp.where(lane == slot(j, k), entry, line)
        if j == COLS - 1:
            break
        inv2 = inv * inv
        alphas = [jnp.broadcast_to(d * inv2, (8, 128)) for d in dots[1:]]

        def get(k, x, at, size, j=j):
            if j == 0 or k == 0:
                return original(k, x, at, size)
            return Q[k - 1, x, pl.ds(at, size), :]

        def sweep(x, accs, j=j, get=get, alphas=alphas):
            accs = list(accs)
            for at in range(0, Y, CH):
                q = get(j, x, at, CH)
                after = None
                for k in range(j + 1, COLS):
                    alpha = jnp.concatenate([alphas[k - j - 1]] * (CH // 8), axis=0)
                    value = get(k, x, at, CH) - alpha * q
                    Q[k - 1, x, pl.ds(at, CH), :] = value
                    if k == j + 1:
                        after = value
                    accs[k - j - 1] = accs[k - j - 1] + fold8(after * value)
            return tuple(accs)

        accs = lax.fori_loop(0, X, sweep, (zero,) * (COLS - 1 - j))
    packed[...] = jnp.broadcast_to(line, packed.shape)
    for copy in outs:
        copy.wait()


def fold_lanes(x):
    parts = [x[:, i : i + 128] for i in range(0, x.shape[1], 128)]
    return functools.reduce(lambda a, b: a + b, parts)


def merged_factor(gathered):
    g = gathered.T
    cols = []
    for k in range(COLS):
        if k < 8:
            cols.append([g[8 * k : 8 * k + 8]])
        else:
            at = 64 + 16 * (k - 8)
            cols.append([g[at : at + 8], g[at + 8 : at + 16]])
    R = {}
    for j in range(COLS):
        dots = []
        for k in range(j, COLS):
            p = fold_lanes(cols[j][0] * cols[k][0])
            if j >= 8:
                p = p + fold_lanes(cols[j][1] * cols[k][1])
            dots.append(total(p))
        inv = 1.0 / jnp.sqrt(dots[0])
        for k in range(j, COLS):
            R[j, k] = dots[k - j] * inv
        inv2 = inv * inv
        for k in range(j + 1, COLS):
            alpha = dots[k - j] * inv2
            for part in range(len(cols[j])):
                cols[k][part] = cols[k][part] - alpha * cols[j][part]
    return R


def inverse(R):
    T = {}
    recip = [1.0 / R[j, j] for j in range(COLS)]
    for j in range(COLS):
        T[j, j] = recip[j]
        for i in range(j):
            s = T[i, i] * R[i, j]
            for k in range(i + 1, j):
                s = s + T[i, k] * R[k, j]
            T[i, j] = -s * recip[j]
    return T


def least_squares(R):
    n = RHS * S
    cols = []
    for c in range(n):
        col = []
        for i in range(c + RHS + 1):
            minus = R[i, c + RHS]
            col.append(R[i, c] - minus if i <= c else -minus)
        cols.append(col)
    upper, target = {}, {}
    recips = []

    def dot(a, b):
        terms = [x * y for x, y in zip(a, b)]
        while len(terms) > 1:
            terms = [x + y for x, y in zip(terms[::2], terms[1::2])] + (
                [terms[-1]] if len(terms) % 2 else []
            )
        return terms[0]

    for j in range(n):
        inv = 1.0 / jnp.sqrt(dot(cols[j], cols[j]))
        recips.append(inv)
        q = [v * inv for v in cols[j]]
        for c in range(j + 1, n):
            w = dot(q, cols[c])
            upper[j, c] = w
            for i in range(len(q)):
                cols[c][i] = cols[c][i] - w * q[i]
        for e in range(RHS):
            target[j, e] = dot(q, [R[i, e] for i in range(e + 1)])
    coef = {}
    for e in range(RHS):
        for j in reversed(range(n)):
            value = target[j, e]
            for later in range(j + 1, n):
                value = value - upper[j, later] * coef[later, e]
            coef[j, e] = value * recips[j]
    return coef


def final_kernel(
    X, Y, scale, gathered, rhs, basis, ortho, triangle, update,
    B, O, W, in_sems, out_sems,
):
    loads = [
        pltpu.make_async_copy(rhs, B.at[pl.ds(0, 2)], in_sems.at[0]),
        pltpu.make_async_copy(basis, B.at[pl.ds(2, 8)], in_sems.at[1]),
    ]
    for copy in loads:
        copy.start()
    R = merged_factor(gathered[...])
    row = lax.broadcasted_iota(jnp.int32, (16, 128), 0)
    lane = lax.broadcasted_iota(jnp.int32, (16, 128), 1)
    tri = jnp.zeros((16, 128), F32)
    for (i, j), value in R.items():
        tri = jnp.where((row == i) & (lane == j), value * (1.0 / scale), tri)
    triangle[...] = tri[:COLS, :COLS]
    T = inverse(R)
    weights = {}
    for n, ((i, j), value) in enumerate(T.items()):
        weights[i, j] = n
        W[n] = jnp.broadcast_to(value * scale, (8, 128))
    coef = least_squares(R)
    base = len(weights)
    for n, ((k, e), value) in enumerate(coef.items()):
        weights[k, COLS + e] = base + n
        W[base + n] = jnp.broadcast_to(value, (8, 128))
    for copy in loads:
        copy.wait()

    CH = 32
    XB = 2
    outs = []
    for block in range(X // XB):

        def rows(i, carry, block=block):
            x = block * XB + i
            for at in range(0, Y, CH):
                b = [B[k, x, pl.ds(at, CH), :] for k in range(COLS)]
                for j in range(COLS + RHS):
                    value = None
                    for k in range(j + 1 if j < COLS else RHS * S):
                        w = jnp.concatenate([W[weights[k, j]]] * (CH // 8), axis=0)
                        value = w * b[k] if value is None else value + w * b[k]
                    O[j, x, pl.ds(at, CH), :] = value
            return carry

        lax.fori_loop(0, XB, rows, 0)
        here = pl.ds(block * XB, XB)
        for copy in (
            pltpu.make_async_copy(
                O.at[pl.ds(0, COLS), here], ortho.at[:, here], out_sems.at[2 * block]
            ),
            pltpu.make_async_copy(
                O.at[pl.ds(COLS, RHS), here], update.at[:, here], out_sems.at[2 * block + 1]
            ),
        ):
            copy.start()
            outs.append(copy)
    for copy in outs:
        copy.wait()


ANY = pl.BlockSpec(memory_space=pl.ANY)
VMEM = pl.BlockSpec(memory_space=pltpu.VMEM)
PARAMS = pltpu.CompilerParams(vmem_limit_bytes=VMEM_LIMIT)


def body(right_sides, diagonal, velocity):
    _, X, Y, Z = right_sides.shape
    nx, ny = lax.axis_size("gx"), lax.axis_size("gy")
    devices = nx * ny
    scale = math.sqrt(X * Y * Z * devices)
    shape = lambda *s: jax.ShapeDtypeStruct(s, F32)
    inputs = (right_sides, velocity, diagonal)

    x_low, x_high = pl.pallas_call(
        functools.partial(pack_x_kernel, X),
        out_shape=(shape(20, Y, Z),) * 2,
        in_specs=[ANY] * 3,
        out_specs=[VMEM] * 2,
        scratch_shapes=[pltpu.SemaphoreType.DMA((12,))],
        compiler_params=PARAMS,
        name="pack_x",
    )(*inputs)

    def shift(value, dx, dy):
        pairs = []
        for i in range(nx):
            for j in range(ny):
                if 0 <= i + dx < nx and 0 <= j + dy < ny:
                    pairs.append((i * ny + j, (i + dx) * ny + j + dy))
        return lax.ppermute(value, ("gx", "gy"), pairs)

    xl = shift(x_high, 1, 0)
    xh = shift(x_low, -1, 0)
    y_low, y_high, c_ll, c_lh, c_hl, c_hh = pl.pallas_call(
        functools.partial(pack_y_kernel, X, Y),
        out_shape=(shape(6, X, 8, Z),) * 2 + (shape(CORNER_ROWS, Z),) * 4,
        in_specs=[ANY] * 3,
        out_specs=[VMEM] * 6,
        scratch_shapes=[pltpu.VMEM((4, 6, 3, 8, Z), F32), pltpu.SemaphoreType.DMA((18,))],
        compiler_params=PARAMS,
        name="pack_y",
    )(*inputs)
    yl = shift(y_high, 0, 1)
    yh = shift(y_low, 0, -1)
    corners = (shift(c_hh, 1, 1), shift(c_hl, 1, -1), shift(c_lh, -1, 1), shift(c_ll, -1, -1))

    XE, YE = X + 8, Y + 2 * YP
    basis, packed = pl.pallas_call(
        functools.partial(main_kernel, X, Y),
        out_shape=(shape(8, X, Y, Z), shape(devices, 128)),
        in_specs=[ANY] * 7 + [VMEM] * 4,
        out_specs=[ANY, VMEM],
        scratch_shapes=[
            pltpu.VMEM((S, RHS, XE, YE, Z), F32),
            pltpu.VMEM((RHS, X, Y, Z), F32),
            pltpu.VMEM((4, XE, YE, Z), F32),
            pltpu.VMEM((6, XE, YE, Z), F32),
            pltpu.VMEM((COLS - 1, X, Y, Z), F32),
            pltpu.SemaphoreType.DMA((19,)),
            pltpu.SemaphoreType.DMA((4,)),
        ],
        compiler_params=PARAMS,
        name="powers",
    )(*inputs, xl, xh, yl, yh, *corners)

    gathered = lax.all_to_all(packed, ("gx", "gy"), 0, 0, tiled=True)

    ortho, triangle, update = pl.pallas_call(
        functools.partial(final_kernel, X, Y, scale),
        out_shape=(shape(COLS, X, Y, Z), shape(COLS, COLS), shape(RHS, X, Y, Z)),
        in_specs=[VMEM, ANY, ANY],
        out_specs=[ANY, VMEM, ANY],
        scratch_shapes=[
            pltpu.VMEM((COLS, X, Y, Z), F32),
            pltpu.VMEM((COLS + RHS, X, Y, Z), F32),
            pltpu.VMEM((71, 8, 128), F32),
            pltpu.SemaphoreType.DMA((2,)),
            pltpu.SemaphoreType.DMA((X,)),
        ],
        compiler_params=PARAMS,
        name="combine",
    )(gathered, right_sides, basis)
    return ortho, triangle, update


def solution(mesh):
    return jax.shard_map(
        body,
        mesh=mesh,
        in_specs=(P(None, "gx", "gy", None), P("gx", "gy", None), P(None, "gx", "gy", None)),
        out_specs=(P(None, "gx", "gy", None), P(), P(None, "gx", "gy", None)),
        check_vma=False,
    )
```

```python
import functools
import math

import jax
import jax.numpy as jnp
from jax import lax
from jax.experimental import pallas as pl
from jax.experimental.pallas import tpu as pltpu
from jax.sharding import PartitionSpec as P

S = 4
RHS = 2
COLS = 10
YP = 16

F32 = jnp.float32
FIELD_CORNER = [(dx, dy) for dx in (1, 2, 3) for dy in (1, 2, 3) if dx + dy <= 4]
COEF_CORNER = [(dx, dy) for dx in (1, 2) for dy in (1, 2) if dx + dy <= 3]
CORNER_ROWS = RHS * len(FIELD_CORNER) + 4 * len(COEF_CORNER)


def slot(i, k):
    return (8 * k if k < 8 else 64 + 16 * (k - 8)) + i


def run_copies(copies):
    for copy in copies:
        copy.start()
    for copy in copies:
        copy.wait()


def pack_x_kernel(X, rhs, vel, diag, low, high, sems):
    copies = []
    for out, at4, at3 in ((high, X - 4, X - 3), (low, 0, 0)):
        for f in range(RHS):
            copies.append((rhs.at[f, pl.ds(at4, 4)], out.at[pl.ds(4 * f, 4)]))
        for c in range(3):
            copies.append((vel.at[c, pl.ds(at3, 3)], out.at[pl.ds(8 + 3 * c, 3)]))
        copies.append((diag.at[pl.ds(at3, 3)], out.at[pl.ds(17, 3)]))
    run_copies([pltpu.make_async_copy(s, d, sems.at[i]) for i, (s, d) in enumerate(copies)])


def pack_y_kernel(Y, rhs, vel, diag, low, high, sems):
    copies = []
    for out, at in ((high, Y - 8), (low, 0)):
        copies.append((rhs.at[:, :, pl.ds(at, 8)], out.at[pl.ds(0, 2)]))
        copies.append((vel.at[:, :, pl.ds(at, 8)], out.at[pl.ds(2, 3)]))
        copies.append((diag.at[:, pl.ds(at, 8)], out.at[5]))
    run_copies([pltpu.make_async_copy(s, d, sems.at[i]) for i, (s, d) in enumerate(copies)])


def load_kernel(X, Y, rhs, vel, diag, V, U, sems):
    own_x, own_y = pl.ds(4, X), pl.ds(YP, Y)
    copies = [
        (rhs, V.at[0, :, own_x, own_y]),
        (vel, U.at[pl.ds(0, 3), own_x, own_y]),
        (diag, U.at[3, own_x, own_y]),
    ]
    run_copies([pltpu.make_async_copy(s, d, sems.at[i]) for i, (s, d) in enumerate(copies)])


def corner_cells(X, Y, low, own):
    cells = []
    for y_low in (True, False):
        for f in range(6):
            for dx, dy in FIELD_CORNER if f < 2 else COEF_CORNER:
                if own:
                    x = 3 + dx if low else X + 4 - dx
                else:
                    x = 4 - dx if low else X + 3 + dx
                cells.append((f, x, YP - dy if y_low else YP + Y - 1 + dy))
    return cells


def place_y_kernel(X, Y, yl, yh, V_in, U_in, V, U, low, high):
    for got, at in ((yl, YP - 8), (yh, YP + Y)):
        for x in range(X):
            for f in range(2):
                V[0, f, 4 + x, at : at + 8, :] = got[f, x]
            for c in range(4):
                U[c, 4 + x, at : at + 8, :] = got[2 + c, x]
    for out, is_low in ((low, True), (high, False)):
        for row, (f, x, y) in enumerate(corner_cells(X, Y, is_low, True)):
            out[row : row + 1, :] = (
                V[0, f, x, y : y + 1, :] if f < 2 else U[f - 2, x, y : y + 1, :]
            )


def total(x):
    return jnp.sum(jnp.sum(x, axis=0, keepdims=True), axis=1, keepdims=True)


def fold8(x):
    rows = x.shape[0]
    parts = [x[8 * i : 8 * i + 8] for i in range(rows // 8)]
    while len(parts) > 1:
        parts = [a + b for a, b in zip(parts[::2], parts[1::2])] + (
            [parts[-1]] if len(parts) % 2 else []
        )
    return parts[0]


def coefficient_rows(X, Y, U, A, rows):
    gx, gy = lax.axis_index("gx"), lax.axis_index("gy")
    nx, ny = lax.axis_size("gx"), lax.axis_size("gy")
    WIDE = Y + 16
    inner = pl.ds(YP - 8, WIDE)
    yi = lax.broadcasted_iota(jnp.int32, (WIDE, 128), 0)
    zi = lax.broadcasted_iota(jnp.int32, (WIDE, 128), 1)
    y_in = ((yi >= 8) | (gy > 0)) & ((yi < Y + 8) | (gy < ny - 1))

    def one(x):
        x_in = ((x >= 4) | (gx > 0)) & ((x < X + 4) | (gx < nx - 1))
        g = jnp.where(y_in & x_in, 1.0 / (6.0 + U[3, x, inner, :]), 0.0)
        for c in range(3):
            ug = U[c, x, inner, :] * g
            plus, minus = g + ug, g - ug
            if c == 2:
                plus = jnp.where(zi == 0, 0.0, plus)
                minus = jnp.where(zi == 127, 0.0, minus)
            A[2 * c, x, inner, :] = plus
            A[2 * c + 1, x, inner, :] = minus

    for_rows(rows, one, 2)


def for_rows(rows, body, unroll):
    def run(i, carry):
        for first, last in rows:
            body(first + i)
        return carry

    lax.fori_loop(0, rows[0][1] - rows[0][0], run, 0, unroll=unroll)


def power_rows(Y, V, V4, A, k, rows, unroll):
    begin, size = (YP, Y) if k == S else (YP - 8, Y + 16)
    here = pl.ds(begin, size)

    def one(x):
        a = [A[c, x, here, :] for c in range(6)]
        for f in range(RHS):
            centre = V[k - 1, f, x, here, :]
            value = a[4] * pltpu.roll(centre, 1, 1) + a[5] * pltpu.roll(centre, 127, 1)
            value += a[0] * V[k - 1, f, x - 1, here, :] + a[1] * V[k - 1, f, x + 1, here, :]
            value += a[2] * V[k - 1, f, x, pl.ds(begin - 1, size), :]
            value += a[3] * V[k - 1, f, x, pl.ds(begin + 1, size), :]
            if k == S:
                V4[f, x - 4] = value
            else:
                V[k, f, x, here, :] = value

    for_rows(rows, one, unroll)


def basis_rows(V, V4, k, x, at, size):
    if k >= RHS * S:
        return V4[k - RHS * S, x, pl.ds(at, size), :]
    return V[k // RHS, k % RHS, x + 4, pl.ds(YP + at, size), :]


def local_factor(Y, V, V4, Q, rows):
    CH = 32
    zero = jnp.zeros((8, 128), F32)

    def first_dots(i, accs):
        accs = list(accs)
        for first, _ in rows:
            x = first + i
            for at in range(0, Y, CH):
                q = basis_rows(V, V4, 0, x, at, CH)
                for k in range(COLS):
                    accs[k] = accs[k] + fold8(q * basis_rows(V, V4, k, x, at, CH))
        return tuple(accs)

    count = rows[0][1] - rows[0][0]
    accs = lax.fori_loop(0, count, first_dots, (zero,) * COLS)
    lane = lax.broadcasted_iota(jnp.int32, (1, 128), 1)
    line = jnp.zeros((1, 128), F32)
    for j in range(COLS):
        dots = [total(a) for a in accs]
        live = dots[0] > 0.0
        length = jnp.sqrt(jnp.where(live, dots[0], 1.0))
        inv = jnp.where(live, 1.0 / length, 0.0)
        for k in range(j, COLS):
            line = jnp.where(lane == slot(j, k), dots[k - j] * inv, line)
        if j == COLS - 1:
            return line
        inv2 = inv * inv
        alphas = [jnp.broadcast_to(d * inv2, (8, 128)) for d in dots[1:]]

        def get(k, x, at, size, j=j):
            if j == 0 or k == 0:
                return basis_rows(V, V4, k, x, at, size)
            return Q[k - 1, x, pl.ds(at, size), :]

        def sweep(i, accs, j=j, get=get, alphas=alphas):
            accs = list(accs)
            for first, _ in rows:
                x = first + i
                for at in range(0, Y, CH):
                    q = get(j, x, at, CH)
                    after = None
                    for k in range(j + 1, COLS):
                        alpha = jnp.concatenate([alphas[k - j - 1]] * (CH // 8), axis=0)
                        value = get(k, x, at, CH) - alpha * q
                        Q[k - 1, x, pl.ds(at, CH), :] = value
                        if k == j + 1:
                            after = value
                        accs[k - j - 1] = accs[k - j - 1] + fold8(after * value)
            return tuple(accs)

        accs = lax.fori_loop(0, count, sweep, (zero,) * (COLS - 1 - j))


def inner_kernel(X, Y, V_in, U, V, V4, A, line, Q):
    coefficient_rows(X, Y, U, A, [(4, X + 4)])
    for k in range(1, S + 1):
        power_rows(Y, V, V4, A, k, [(4 + k, X + 4 - k)], 4)
    line[...] = local_factor(Y, V, V4, Q, [(4, X // 2), (X // 2, X - 4)])


def outer_kernel(X, Y, xl, xh, cl, ch, inner_line, V_in, V4_in, A_in, U_in, V, V4, A, U, packed, Q):
    own_y = slice(YP, YP + Y)
    for got, at4, at3 in ((xl, 0, 1), (xh, X + 4, X + 4)):
        for i in range(4):
            for f in range(RHS):
                V[0, f, at4 + i, own_y, :] = got[4 * f + i]
        for i in range(3):
            for c in range(4):
                U[c, at3 + i, own_y, :] = got[8 + 3 * c + i]
    for got, is_low in ((cl, True), (ch, False)):
        for row, (f, x, y) in enumerate(corner_cells(X, Y, is_low, False)):
            if f < 2:
                V[0, f, x, y : y + 1, :] = got[row : row + 1, :]
            else:
                U[f - 2, x, y : y + 1, :] = got[row : row + 1, :]
    coefficient_rows(X, Y, U, A, [(1, 4), (X + 4, X + 7)])
    for k in range(1, S + 1):
        power_rows(Y, V, V4, A, k, [(k, k + 4), (X + 4 - k, X + 8 - k)], 2)
    line = local_factor(Y, V, V4, Q, [(0, 4), (X - 4, X)])
    row = lax.broadcasted_iota(jnp.int32, (8, 128), 0)
    both = jnp.where(row % 2 == 0, inner_line[...], line)
    packed[...] = jnp.concatenate([both] * (packed.shape[0] // 8), axis=0)


def fold_lanes(x):
    parts = [x[:, i : i + 128] for i in range(0, x.shape[1], 128)]
    return functools.reduce(lambda a, b: a + b, parts)


def merged_factor(gathered):
    g = gathered.T
    cols = []
    for k in range(COLS):
        if k < 8:
            cols.append([g[8 * k : 8 * k + 8]])
        else:
            at = 64 + 16 * (k - 8)
            cols.append([g[at : at + 8], g[at + 8 : at + 16]])
    R = {}
    for j in range(COLS):
        dots = []
        for k in range(j, COLS):
            p = fold_lanes(cols[j][0] * cols[k][0])
            if j >= 8:
                p = p + fold_lanes(cols[j][1] * cols[k][1])
            dots.append(total(p))
        inv = 1.0 / jnp.sqrt(dots[0])
        for k in range(j, COLS):
            R[j, k] = dots[k - j] * inv
        inv2 = inv * inv
        for k in range(j + 1, COLS):
            alpha = dots[k - j] * inv2
            for part in range(len(cols[j])):
                cols[k][part] = cols[k][part] - alpha * cols[j][part]
    return R


def inverse(R):
    T = {}
    recip = [1.0 / R[j, j] for j in range(COLS)]
    for j in range(COLS):
        T[j, j] = recip[j]
        for i in range(j):
            s = T[i, i] * R[i, j]
            for k in range(i + 1, j):
                s = s + T[i, k] * R[k, j]
            T[i, j] = -s * recip[j]
    return T


def least_squares(R):
    n = RHS * S
    cols = []
    for c in range(n):
        col = []
        for i in range(c + RHS + 1):
            minus = R[i, c + RHS]
            col.append(R[i, c] - minus if i <= c else -minus)
        cols.append(col)
    upper, target = {}, {}
    recips = []

    def dot(a, b):
        terms = [x * y for x, y in zip(a, b)]
        while len(terms) > 1:
            terms = [x + y for x, y in zip(terms[::2], terms[1::2])] + (
                [terms[-1]] if len(terms) % 2 else []
            )
        return terms[0]

    for j in range(n):
        inv = 1.0 / jnp.sqrt(dot(cols[j], cols[j]))
        recips.append(inv)
        q = [v * inv for v in cols[j]]
        for c in range(j + 1, n):
            w = dot(q, cols[c])
            upper[j, c] = w
            for i in range(len(q)):
                cols[c][i] = cols[c][i] - w * q[i]
        for e in range(RHS):
            target[j, e] = dot(q, [R[i, e] for i in range(e + 1)])
    coef = {}
    for e in range(RHS):
        for j in reversed(range(n)):
            value = target[j, e]
            for later in range(j + 1, n):
                value = value - upper[j, later] * coef[later, e]
            coef[j, e] = value * recips[j]
    return coef


def final_kernel(
    X, Y, scale, gathered, V, V4, ortho, triangle, update, O, W, out_sems
):
    R = merged_factor(gathered[...])
    row = lax.broadcasted_iota(jnp.int32, (16, 128), 0)
    lane = lax.broadcasted_iota(jnp.int32, (16, 128), 1)
    tri = jnp.zeros((16, 128), F32)
    for (i, j), value in R.items():
        tri = jnp.where((row == i) & (lane == j), value * (1.0 / scale), tri)
    triangle[...] = tri[:COLS, :COLS]
    T = inverse(R)
    weights = {}
    for n, ((i, j), value) in enumerate(T.items()):
        weights[i, j] = n
        W[n] = jnp.broadcast_to(value * scale, (8, 128))
    coef = least_squares(R)
    base = len(weights)
    for n, ((k, e), value) in enumerate(coef.items()):
        weights[k, COLS + e] = base + n
        W[base + n] = jnp.broadcast_to(value, (8, 128))

    CH = 32
    XB = 2
    outs = []
    for block in range(X // XB):

        def rows(i, carry, block=block):
            x = block * XB + i
            for at in range(0, Y, CH):
                b = [basis_rows(V, V4, k, x, at, CH) for k in range(COLS)]
                for j in range(COLS + RHS):
                    value = None
                    for k in range(j + 1 if j < COLS else RHS * S):
                        w = jnp.concatenate([W[weights[k, j]]] * (CH // 8), axis=0)
                        value = w * b[k] if value is None else value + w * b[k]
                    O[j, x, pl.ds(at, CH), :] = value
            return carry

        lax.fori_loop(0, XB, rows, 0)
        here = pl.ds(block * XB, XB)
        for copy in (
            pltpu.make_async_copy(
                O.at[pl.ds(0, COLS), here], ortho.at[:, here], out_sems.at[2 * block]
            ),
            pltpu.make_async_copy(
                O.at[pl.ds(COLS, RHS), here], update.at[:, here], out_sems.at[2 * block + 1]
            ),
        ):
            copy.start()
            outs.append(copy)
    for copy in outs:
        copy.wait()


ANY = pl.BlockSpec(memory_space=pl.ANY)
VMEM = pl.BlockSpec(memory_space=pltpu.VMEM)
MIB = 1024 * 1024
PIN, BLOCK, FAR = range(3)


def call(kernel, name, inputs, outputs, scratch=(), aliases={}, limit=4):
    pin = lambda a: pltpu.with_memory_space_constraint(a, pltpu.VMEM)
    spec = lambda place: ANY if place == FAR else VMEM
    return pl.pallas_call(
        kernel,
        out_shape=tuple(
            pltpu.VMEM(o, F32) if place == PIN else jax.ShapeDtypeStruct(o, F32)
            for o, place in outputs
        ),
        in_specs=[spec(place) for _, place in inputs],
        out_specs=tuple(spec(place) for _, place in outputs),
        scratch_shapes=list(scratch),
        input_output_aliases=aliases,
        compiler_params=pltpu.CompilerParams(vmem_limit_bytes=limit * MIB),
        name=name,
    )(*(pin(a) if place == PIN else a for a, place in inputs))


def body(right_sides, diagonal, velocity):
    _, X, Y, Z = right_sides.shape
    nx, ny = lax.axis_size("gx"), lax.axis_size("gy")
    devices = nx * ny
    scale = math.sqrt(X * Y * Z * devices)
    XE, YE = X + 8, Y + 2 * YP
    inputs = [(right_sides, FAR), (velocity, FAR), (diagonal, FAR)]
    dma = pltpu.SemaphoreType.DMA

    def shift(value, axis, by):
        size = lax.axis_size(axis)
        return lax.ppermute(
            value, axis, [(i, i + by) for i in range(size) if 0 <= i + by < size]
        )

    slab = ((20, Y, Z), PIN)
    x_low, x_high = call(
        functools.partial(pack_x_kernel, X), "pack_x", inputs, [slab, slab], [dma((12,))]
    )
    xl, xh = shift(x_high, "gx", 1), shift(x_low, "gx", -1)
    slab = ((6, X, 8, Z), PIN)
    y_low, y_high = call(
        functools.partial(pack_y_kernel, Y), "pack_y", inputs, [slab, slab], [dma((6,))]
    )
    yl, yh = shift(y_high, "gy", 1), shift(y_low, "gy", -1)
    v_shape, u_shape = ((S, RHS, XE, YE, Z), PIN), ((4, XE, YE, Z), PIN)
    V, U = call(
        functools.partial(load_kernel, X, Y), "load", inputs, [v_shape, u_shape], [dma((3,))]
    )
    strip = ((2 * CORNER_ROWS, Z), PIN)
    V, U, c_low, c_high = call(
        functools.partial(place_y_kernel, X, Y),
        "place_y",
        [(yl, PIN), (yh, PIN), (V, PIN), (U, PIN)],
        [v_shape, u_shape, strip, strip],
        aliases={2: 0, 3: 1},
    )
    cl, ch = shift(c_high, "gx", 1), shift(c_low, "gx", -1)
    v4_shape, a_shape = ((RHS, X, Y, Z), PIN), ((6, XE, YE, Z), PIN)
    work = pltpu.VMEM((COLS - 1, X, Y, Z), F32)
    V, V4, A, line = call(
        functools.partial(inner_kernel, X, Y),
        "inner",
        [(V, PIN), (U, PIN)],
        [v_shape, v4_shape, a_shape, ((1, 128), PIN)],
        [work],
        aliases={0: 0},
        limit=8,
    )
    V, V4, A, U, packed = call(
        functools.partial(outer_kernel, X, Y),
        "outer",
        [(a, PIN) for a in (xl, xh, cl, ch, line, V, V4, A, U)],
        [v_shape, v4_shape, a_shape, u_shape, ((2 * devices, 128), BLOCK)],
        [work],
        aliases={5: 0, 6: 1, 7: 2, 8: 3},
        limit=8,
    )
    gathered = lax.all_to_all(packed, ("gx", "gy"), 0, 0, tiled=True)
    out = [((COLS, X, Y, Z), FAR), ((COLS, COLS), BLOCK), ((RHS, X, Y, Z), FAR)]
    ortho, triangle, update = call(
        functools.partial(final_kernel, X, Y, scale),
        "combine",
        [(gathered, BLOCK), (V, PIN), (V4, PIN)],
        out,
        [
            pltpu.VMEM((COLS + RHS, X, Y, Z), F32),
            pltpu.VMEM((71, 8, 128), F32),
            dma((X,)),
        ],
        limit=10,
    )
    return ortho, triangle, update


def solution(mesh):
    return jax.shard_map(
        body,
        mesh=mesh,
        in_specs=(P(None, "gx", "gy", None), P("gx", "gy", None), P(None, "gx", "gy", None)),
        out_specs=(P(None, "gx", "gy", None), P(), P(None, "gx", "gy", None)),
        check_vma=False,
    )
```

```python
import functools
import math

import jax
import jax.numpy as jnp
from jax import lax
from jax.experimental import pallas as pl
from jax.experimental.pallas import tpu as pltpu
from jax.sharding import PartitionSpec as P

S = 4
RHS = 2
COLS = 10
YP = 16

F32 = jnp.float32
FIELD_CORNER = [(dx, dy) for dx in (1, 2, 3) for dy in (1, 2, 3) if dx + dy <= 4]
COEF_CORNER = [(dx, dy) for dx in (1, 2) for dy in (1, 2) if dx + dy <= 3]
CORNER_ROWS = RHS * len(FIELD_CORNER) + 4 * len(COEF_CORNER)


def slot(i, k):
    return (8 * k if k < 8 else 64 + 16 * (k - 8)) + i


def run_copies(copies):
    for copy in copies:
        copy.start()
    for copy in copies:
        copy.wait()


def toward_high(axis, pairing):
    return lax.axis_index(axis) % 2 == pairing


def pack_x_kernel(X, rhs, vel, diag, first, second, sems):
    copies = []
    for pairing, out in enumerate((first, second)):
        high = toward_high("gx", pairing)
        at4, at3 = jnp.where(high, X - 4, 0), jnp.where(high, X - 3, 0)
        for f in range(RHS):
            copies.append((rhs.at[f, pl.ds(at4, 4)], out.at[pl.ds(4 * f, 4)]))
        for c in range(3):
            copies.append((vel.at[c, pl.ds(at3, 3)], out.at[pl.ds(8 + 3 * c, 3)]))
        copies.append((diag.at[pl.ds(at3, 3)], out.at[pl.ds(17, 3)]))
    run_copies([pltpu.make_async_copy(s, d, sems.at[i]) for i, (s, d) in enumerate(copies)])


def pack_y_kernel(Y, rhs, vel, diag, first, second, sems):
    copies = []
    for pairing, out in enumerate((first, second)):
        at = pl.ds(pl.multiple_of(jnp.where(toward_high("gy", pairing), Y - 8, 0), 8), 8)
        copies.append((rhs.at[:, :, at], out.at[pl.ds(0, 2)]))
        copies.append((vel.at[:, :, at], out.at[pl.ds(2, 3)]))
        copies.append((diag.at[:, at], out.at[5]))
    run_copies([pltpu.make_async_copy(s, d, sems.at[i]) for i, (s, d) in enumerate(copies)])


def load_kernel(X, Y, rhs, vel, diag, V, U, sems):
    own_x, own_y = pl.ds(4, X), pl.ds(YP, Y)
    copies = [
        (rhs, V.at[0, :, own_x, own_y]),
        (vel, U.at[pl.ds(0, 3), own_x, own_y]),
        (diag, U.at[3, own_x, own_y]),
    ]
    run_copies([pltpu.make_async_copy(s, d, sems.at[i]) for i, (s, d) in enumerate(copies)])


def corner_cells(X, Y, high, own):
    cells = []
    for y_low in (True, False):
        for f in range(6):
            for dx, dy in FIELD_CORNER if f < 2 else COEF_CORNER:
                if own:
                    x = jnp.where(high, X + 4 - dx, 3 + dx)
                else:
                    x = jnp.where(high, X + 3 + dx, 4 - dx)
                cells.append((f, x, YP - dy if y_low else YP + Y - 1 + dy))
    return cells


def place_y_kernel(X, Y, y0, y1, V_in, U_in, V, U, first, second):
    for pairing, got in enumerate((y0, y1)):
        at = jnp.where(toward_high("gy", pairing), YP + Y, YP - 8)
        here = pl.ds(pl.multiple_of(at, 8), 8)
        for x in range(X):
            for f in range(2):
                V[0, f, 4 + x, here, :] = got[f, x]
            for c in range(4):
                U[c, 4 + x, here, :] = got[2 + c, x]
    for pairing, out in enumerate((first, second)):
        cells = corner_cells(X, Y, toward_high("gx", pairing), True)
        for row, (f, x, y) in enumerate(cells):
            out[row : row + 1, :] = (
                V[0, f, x, y : y + 1, :] if f < 2 else U[f - 2, x, y : y + 1, :]
            )


def total(x):
    return jnp.sum(jnp.sum(x, axis=0, keepdims=True), axis=1, keepdims=True)


def fold8(x):
    rows = x.shape[0]
    parts = [x[8 * i : 8 * i + 8] for i in range(rows // 8)]
    while len(parts) > 1:
        parts = [a + b for a, b in zip(parts[::2], parts[1::2])] + (
            [parts[-1]] if len(parts) % 2 else []
        )
    return parts[0]


def coefficient_rows(X, Y, U, A, rows):
    gx, gy = lax.axis_index("gx"), lax.axis_index("gy")
    nx, ny = lax.axis_size("gx"), lax.axis_size("gy")
    WIDE = Y + 16
    inner = pl.ds(YP - 8, WIDE)
    yi = lax.broadcasted_iota(jnp.int32, (WIDE, 128), 0)
    zi = lax.broadcasted_iota(jnp.int32, (WIDE, 128), 1)
    y_in = ((yi >= 8) | (gy > 0)) & ((yi < Y + 8) | (gy < ny - 1))

    def one(x):
        x_in = ((x >= 4) | (gx > 0)) & ((x < X + 4) | (gx < nx - 1))
        g = jnp.where(y_in & x_in, 1.0 / (6.0 + U[3, x, inner, :]), 0.0)
        for c in range(3):
            ug = U[c, x, inner, :] * g
            plus, minus = g + ug, g - ug
            if c == 2:
                plus = jnp.where(zi == 0, 0.0, plus)
                minus = jnp.where(zi == 127, 0.0, minus)
            A[2 * c, x, inner, :] = plus
            A[2 * c + 1, x, inner, :] = minus

    for_rows(rows, one, 2)


def for_rows(rows, body, unroll):
    def run(i, carry):
        for first, last in rows:
            body(first + i)
        return carry

    lax.fori_loop(0, rows[0][1] - rows[0][0], run, 0, unroll=unroll)


def power_rows(Y, V, V4, A, k, rows, unroll):
    begin, size = (YP, Y) if k == S else (YP - 8, Y + 16)
    here = pl.ds(begin, size)

    def one(x):
        a = [A[c, x, here, :] for c in range(6)]
        for f in range(RHS):
            centre = V[k - 1, f, x, here, :]
            value = a[4] * pltpu.roll(centre, 1, 1) + a[5] * pltpu.roll(centre, 127, 1)
            value += a[0] * V[k - 1, f, x - 1, here, :] + a[1] * V[k - 1, f, x + 1, here, :]
            value += a[2] * V[k - 1, f, x, pl.ds(begin - 1, size), :]
            value += a[3] * V[k - 1, f, x, pl.ds(begin + 1, size), :]
            if k == S:
                V4[f, x - 4] = value
            else:
                V[k, f, x, here, :] = value

    for_rows(rows, one, unroll)


def basis_rows(V, V4, k, x, at, size):
    if k >= RHS * S:
        return V4[k - RHS * S, x, pl.ds(at, size), :]
    return V[k // RHS, k % RHS, x + 4, pl.ds(YP + at, size), :]


def local_factor(Y, V, V4, Q, rows):
    CH = 32
    zero = jnp.zeros((8, 128), F32)

    def first_dots(i, accs):
        accs = list(accs)
        for first, _ in rows:
            x = first + i
            for at in range(0, Y, CH):
                q = basis_rows(V, V4, 0, x, at, CH)
                for k in range(COLS):
                    accs[k] = accs[k] + fold8(q * basis_rows(V, V4, k, x, at, CH))
        return tuple(accs)

    count = rows[0][1] - rows[0][0]
    accs = lax.fori_loop(0, count, first_dots, (zero,) * COLS)
    lane = lax.broadcasted_iota(jnp.int32, (1, 128), 1)
    line = jnp.zeros((1, 128), F32)
    for j in range(COLS):
        dots = [total(a) for a in accs]
        live = dots[0] > 0.0
        length = jnp.sqrt(jnp.where(live, dots[0], 1.0))
        inv = jnp.where(live, 1.0 / length, 0.0)
        for k in range(j, COLS):
            line = jnp.where(lane == slot(j, k), dots[k - j] * inv, line)
        if j == COLS - 1:
            return line
        inv2 = inv * inv
        alphas = [jnp.broadcast_to(d * inv2, (8, 128)) for d in dots[1:]]

        def get(k, x, at, size, j=j):
            if j == 0 or k == 0:
                return basis_rows(V, V4, k, x, at, size)
            return Q[k - 1, x, pl.ds(at, size), :]

        def sweep(i, accs, j=j, get=get, alphas=alphas):
            accs = list(accs)
            for first, _ in rows:
                x = first + i
                for at in range(0, Y, CH):
                    q = get(j, x, at, CH)
                    after = None
                    for k in range(j + 1, COLS):
                        alpha = jnp.concatenate([alphas[k - j - 1]] * (CH // 8), axis=0)
                        value = get(k, x, at, CH) - alpha * q
                        Q[k - 1, x, pl.ds(at, CH), :] = value
                        if k == j + 1:
                            after = value
                        accs[k - j - 1] = accs[k - j - 1] + fold8(after * value)
            return tuple(accs)

        accs = lax.fori_loop(0, count, sweep, (zero,) * (COLS - 1 - j))


def inner_kernel(X, Y, V_in, U, V, V4, A, line, Q):
    coefficient_rows(X, Y, U, A, [(4, X + 4)])
    for k in range(1, S + 1):
        power_rows(Y, V, V4, A, k, [(4 + k, X + 4 - k)], 4)
    line[...] = local_factor(Y, V, V4, Q, [(4, X // 2), (X // 2, X - 4)])


def outer_kernel(X, Y, x0, x1, c0, c1, inner_line, V_in, V4_in, A_in, U_in, V, V4, A, U, packed, Q):
    own_y = slice(YP, YP + Y)
    for pairing, (got, corner) in enumerate(((x0, c0), (x1, c1))):
        high = toward_high("gx", pairing)
        at4, at3 = jnp.where(high, X + 4, 0), jnp.where(high, X + 4, 1)
        for i in range(4):
            for f in range(RHS):
                V[0, f, at4 + i, own_y, :] = got[4 * f + i]
        for i in range(3):
            for c in range(4):
                U[c, at3 + i, own_y, :] = got[8 + 3 * c + i]
        for row, (f, x, y) in enumerate(corner_cells(X, Y, high, False)):
            if f < 2:
                V[0, f, x, y : y + 1, :] = corner[row : row + 1, :]
            else:
                U[f - 2, x, y : y + 1, :] = corner[row : row + 1, :]
    coefficient_rows(X, Y, U, A, [(1, 4), (X + 4, X + 7)])
    for k in range(1, S + 1):
        power_rows(Y, V, V4, A, k, [(k, k + 4), (X + 4 - k, X + 8 - k)], 2)
    line = local_factor(Y, V, V4, Q, [(0, 4), (X - 4, X)])
    row = lax.broadcasted_iota(jnp.int32, (8, 128), 0)
    both = jnp.where(row % 2 == 0, inner_line[...], line)
    packed[...] = jnp.concatenate([both] * (packed.shape[0] // 8), axis=0)


def fold_lanes(x):
    parts = [x[:, i : i + 128] for i in range(0, x.shape[1], 128)]
    return functools.reduce(lambda a, b: a + b, parts)


def merged_factor(gathered):
    g = gathered.T
    cols = []
    for k in range(COLS):
        if k < 8:
            cols.append([g[8 * k : 8 * k + 8]])
        else:
            at = 64 + 16 * (k - 8)
            cols.append([g[at : at + 8], g[at + 8 : at + 16]])
    R = {}
    for j in range(COLS):
        dots = []
        for k in range(j, COLS):
            p = fold_lanes(cols[j][0] * cols[k][0])
            if j >= 8:
                p = p + fold_lanes(cols[j][1] * cols[k][1])
            dots.append(total(p))
        inv = 1.0 / jnp.sqrt(dots[0])
        for k in range(j, COLS):
            R[j, k] = dots[k - j] * inv
        inv2 = inv * inv
        for k in range(j + 1, COLS):
            alpha = dots[k - j] * inv2
            for part in range(len(cols[j])):
                cols[k][part] = cols[k][part] - alpha * cols[j][part]
    return R


def inverse(R):
    T = {}
    recip = [1.0 / R[j, j] for j in range(COLS)]
    for j in range(COLS):
        T[j, j] = recip[j]
        for i in range(j):
            s = T[i, i] * R[i, j]
            for k in range(i + 1, j):
                s = s + T[i, k] * R[k, j]
            T[i, j] = -s * recip[j]
    return T


def least_squares(R):
    n = RHS * S
    cols = []
    for c in range(n):
        col = []
        for i in range(c + RHS + 1):
            minus = R[i, c + RHS]
            col.append(R[i, c] - minus if i <= c else -minus)
        cols.append(col)
    upper, target = {}, {}
    recips = []

    def dot(a, b):
        terms = [x * y for x, y in zip(a, b)]
        while len(terms) > 1:
            terms = [x + y for x, y in zip(terms[::2], terms[1::2])] + (
                [terms[-1]] if len(terms) % 2 else []
            )
        return terms[0]

    for j in range(n):
        inv = 1.0 / jnp.sqrt(dot(cols[j], cols[j]))
        recips.append(inv)
        q = [v * inv for v in cols[j]]
        for c in range(j + 1, n):
            w = dot(q, cols[c])
            upper[j, c] = w
            for i in range(len(q)):
                cols[c][i] = cols[c][i] - w * q[i]
        for e in range(RHS):
            target[j, e] = dot(q, [R[i, e] for i in range(e + 1)])
    coef = {}
    for e in range(RHS):
        for j in reversed(range(n)):
            value = target[j, e]
            for later in range(j + 1, n):
                value = value - upper[j, later] * coef[later, e]
            coef[j, e] = value * recips[j]
    return coef


def final_kernel(
    X, Y, scale, gathered, V, V4, ortho, triangle, update, O, W, out_sems
):
    R = merged_factor(gathered[...])
    row = lax.broadcasted_iota(jnp.int32, (16, 128), 0)
    lane = lax.broadcasted_iota(jnp.int32, (16, 128), 1)
    tri = jnp.zeros((16, 128), F32)
    for (i, j), value in R.items():
        tri = jnp.where((row == i) & (lane == j), value * (1.0 / scale), tri)
    triangle[...] = tri[:COLS, :COLS]
    T = inverse(R)
    weights = {}
    for n, ((i, j), value) in enumerate(T.items()):
        weights[i, j] = n
        W[n] = jnp.broadcast_to(value * scale, (8, 128))
    coef = least_squares(R)
    base = len(weights)
    for n, ((k, e), value) in enumerate(coef.items()):
        weights[k, COLS + e] = base + n
        W[base + n] = jnp.broadcast_to(value, (8, 128))

    CH = 32
    XB = 2
    outs = []
    for block in range(X // XB):

        def rows(i, carry, block=block):
            x = block * XB + i
            for at in range(0, Y, CH):
                b = [basis_rows(V, V4, k, x, at, CH) for k in range(COLS)]
                for j in range(COLS + RHS):
                    value = None
                    for k in range(j + 1 if j < COLS else RHS * S):
                        w = jnp.concatenate([W[weights[k, j]]] * (CH // 8), axis=0)
                        value = w * b[k] if value is None else value + w * b[k]
                    O[j, x, pl.ds(at, CH), :] = value
            return carry

        lax.fori_loop(0, XB, rows, 0)
        here = pl.ds(block * XB, XB)
        for copy in (
            pltpu.make_async_copy(
                O.at[pl.ds(0, COLS), here], ortho.at[:, here], out_sems.at[2 * block]
            ),
            pltpu.make_async_copy(
                O.at[pl.ds(COLS, RHS), here], update.at[:, here], out_sems.at[2 * block + 1]
            ),
        ):
            copy.start()
            outs.append(copy)
    for copy in outs:
        copy.wait()


ANY = pl.BlockSpec(memory_space=pl.ANY)
VMEM = pl.BlockSpec(memory_space=pltpu.VMEM)
MIB = 1024 * 1024
PIN, BLOCK, FAR = range(3)


def call(kernel, name, inputs, outputs, scratch=(), aliases={}, limit=4):
    pin = lambda a: pltpu.with_memory_space_constraint(a, pltpu.VMEM)
    spec = lambda place: ANY if place == FAR else VMEM
    return pl.pallas_call(
        kernel,
        out_shape=tuple(
            pltpu.VMEM(o, F32) if place == PIN else jax.ShapeDtypeStruct(o, F32)
            for o, place in outputs
        ),
        in_specs=[spec(place) for _, place in inputs],
        out_specs=tuple(spec(place) for _, place in outputs),
        scratch_shapes=list(scratch),
        input_output_aliases=aliases,
        compiler_params=pltpu.CompilerParams(vmem_limit_bytes=limit * MIB),
        name=name,
    )(*(pin(a) if place == PIN else a for a, place in inputs))


def body(right_sides, diagonal, velocity):
    _, X, Y, Z = right_sides.shape
    nx, ny = lax.axis_size("gx"), lax.axis_size("gy")
    devices = nx * ny
    scale = math.sqrt(X * Y * Z * devices)
    XE, YE = X + 8, Y + 2 * YP
    inputs = [
        (pltpu.with_memory_space_constraint(a, pltpu.HBM), FAR)
        for a in (right_sides, velocity, diagonal)
    ]
    dma = pltpu.SemaphoreType.DMA

    def swap(value, axis, pairing):
        size = lax.axis_size(axis)
        pairs = [(i, i + 1) for i in range(pairing, size - 1, 2)]
        return lax.ppermute(value, axis, pairs + [(j, i) for i, j in pairs])

    slab = ((20, Y, Z), PIN)
    x0, x1 = call(
        functools.partial(pack_x_kernel, X), "pack_x", inputs, [slab, slab], [dma((12,))]
    )
    x0, x1 = swap(x0, "gx", 0), swap(x1, "gx", 1)
    slab = ((6, X, 8, Z), PIN)
    y0, y1 = call(
        functools.partial(pack_y_kernel, Y), "pack_y", inputs, [slab, slab], [dma((6,))]
    )
    y1, y0 = swap(y1, "gy", 1), swap(y0, "gy", 0)
    v_shape, u_shape = ((S, RHS, XE, YE, Z), PIN), ((4, XE, YE, Z), PIN)
    V, U = call(
        functools.partial(load_kernel, X, Y), "load", inputs, [v_shape, u_shape], [dma((3,))]
    )
    strip = ((2 * CORNER_ROWS, Z), PIN)
    V, U, c0, c1 = call(
        functools.partial(place_y_kernel, X, Y),
        "place_y",
        [(y0, PIN), (y1, PIN), (V, PIN), (U, PIN)],
        [v_shape, u_shape, strip, strip],
        aliases={2: 0, 3: 1},
    )
    c0, c1 = swap(c0, "gx", 0), swap(c1, "gx", 1)
    v4_shape, a_shape = ((RHS, X, Y, Z), PIN), ((6, XE, YE, Z), PIN)
    work = pltpu.VMEM((COLS - 1, X, Y, Z), F32)
    V, V4, A, line = call(
        functools.partial(inner_kernel, X, Y),
        "inner",
        [(V, PIN), (U, PIN)],
        [v_shape, v4_shape, a_shape, ((1, 128), PIN)],
        [work],
        aliases={0: 0},
        limit=8,
    )
    V, V4, A, U, packed = call(
        functools.partial(outer_kernel, X, Y),
        "outer",
        [(a, PIN) for a in (x0, x1, c0, c1, line, V, V4, A, U)],
        [v_shape, v4_shape, a_shape, u_shape, ((2 * devices, 128), BLOCK)],
        [work],
        aliases={5: 0, 6: 1, 7: 2, 8: 3},
        limit=8,
    )
    gathered = lax.all_to_all(packed, ("gx", "gy"), 0, 0, tiled=True)
    out = [((COLS, X, Y, Z), FAR), ((COLS, COLS), BLOCK), ((RHS, X, Y, Z), FAR)]
    ortho, triangle, update = call(
        functools.partial(final_kernel, X, Y, scale),
        "combine",
        [(gathered, BLOCK), (V, PIN), (V4, PIN)],
        out,
        [
            pltpu.VMEM((COLS + RHS, X, Y, Z), F32),
            pltpu.VMEM((71, 8, 128), F32),
            dma((X,)),
        ],
        limit=10,
    )
    return ortho, triangle, update


def solution(mesh):
    return jax.shard_map(
        body,
        mesh=mesh,
        in_specs=(P(None, "gx", "gy", None), P("gx", "gy", None), P(None, "gx", "gy", None)),
        out_specs=(P(None, "gx", "gy", None), P(), P(None, "gx", "gy", None)),
        check_vma=False,
    )
```

```python
import functools
import math

import jax
import jax.numpy as jnp
from jax import lax
from jax.experimental import pallas as pl
from jax.experimental.pallas import tpu as pltpu
from jax.sharding import PartitionSpec as P

S = 4
RHS = 2
COLS = 10
YP = 16

F32 = jnp.float32
FIELD_CORNER = [(dx, dy) for dx in (1, 2, 3) for dy in (1, 2, 3) if dx + dy <= 4]
COEF_CORNER = [(dx, dy) for dx in (1, 2) for dy in (1, 2) if dx + dy <= 3]
CORNER_ROWS = RHS * len(FIELD_CORNER) + 4 * len(COEF_CORNER)


def slot(i, k):
    return (8 * k if k < 8 else 64 + 16 * (k - 8)) + i


def toward_high(axis, pairing):
    return lax.axis_index(axis) % 2 == pairing


def pack_kernel(X, Y, rhs, vel, diag, x0, x1, y0, y1, V, U, sems):
    own_x, own_y = pl.ds(4, X), pl.ds(YP, Y)
    copies = [
        (rhs, V.at[0, :, own_x, own_y]),
        (vel, U.at[pl.ds(0, 3), own_x, own_y]),
        (diag, U.at[3, own_x, own_y]),
    ]
    for pairing, out in enumerate((x0, x1)):
        high = toward_high("gx", pairing)
        at4, at3 = jnp.where(high, X - 4, 0), jnp.where(high, X - 3, 0)
        for f in range(RHS):
            copies.append((rhs.at[f, pl.ds(at4, 4)], out.at[pl.ds(4 * f, 4)]))
        for c in range(3):
            copies.append((vel.at[c, pl.ds(at3, 3)], out.at[pl.ds(8 + 3 * c, 3)]))
        copies.append((diag.at[pl.ds(at3, 3)], out.at[pl.ds(17, 3)]))
    copies = [pltpu.make_async_copy(s, d, sems.at[i]) for i, (s, d) in enumerate(copies)]
    for copy in copies:
        copy.start()
    for copy in copies[:3]:
        copy.wait()
    first_high = toward_high("gy", 0)
    for f in range(6):
        for x in range(X):
            field = V.at[0, f, 4 + x] if f < 2 else U.at[f - 2, 4 + x]
            low, high = field[YP : YP + 4, :], field[YP + Y - 4 : YP + Y, :]
            at = 4 * (f * X + x)
            y0[at : at + 4, :] = jnp.where(first_high, high, low)
            y1[at : at + 4, :] = jnp.where(first_high, low, high)
    for copy in copies[3:]:
        copy.wait()


def corner_cells(X, Y, high, own):
    cells = []
    for y_low in (True, False):
        for f in range(6):
            for dx, dy in FIELD_CORNER if f < 2 else COEF_CORNER:
                if own:
                    x = jnp.where(high, X + 4 - dx, 3 + dx)
                else:
                    x = jnp.where(high, X + 3 + dx, 4 - dx)
                cells.append((f, x, YP - dy if y_low else YP + Y - 1 + dy))
    return cells


def place_y_kernel(X, Y, y0, y1, V_in, U_in, V, U, first, second):
    first_high = toward_high("gy", 0)
    for f in range(6):
        for x in range(X):
            at = 4 * (f * X + x)
            a, b = y0[at : at + 4, :], y1[at : at + 4, :]
            field = V.at[0, f, 4 + x] if f < 2 else U.at[f - 2, 4 + x]
            field[YP - 4 : YP, :] = jnp.where(first_high, b, a)
            field[YP + Y : YP + Y + 4, :] = jnp.where(first_high, a, b)
    for pairing, out in enumerate((first, second)):
        cells = corner_cells(X, Y, toward_high("gx", pairing), True)
        for row, (f, x, y) in enumerate(cells):
            out[row : row + 1, :] = (
                V[0, f, x, y : y + 1, :] if f < 2 else U[f - 2, x, y : y + 1, :]
            )


def total(x):
    return jnp.sum(jnp.sum(x, axis=0, keepdims=True), axis=1, keepdims=True)


def fold8(x):
    rows = x.shape[0]
    parts = [x[8 * i : 8 * i + 8] for i in range(rows // 8)]
    while len(parts) > 1:
        parts = [a + b for a, b in zip(parts[::2], parts[1::2])] + (
            [parts[-1]] if len(parts) % 2 else []
        )
    return parts[0]


def coefficient_rows(X, Y, U, A, rows):
    gx, gy = lax.axis_index("gx"), lax.axis_index("gy")
    nx, ny = lax.axis_size("gx"), lax.axis_size("gy")
    WIDE = Y + 16
    inner = pl.ds(YP - 8, WIDE)
    yi = lax.broadcasted_iota(jnp.int32, (WIDE, 128), 0)
    zi = lax.broadcasted_iota(jnp.int32, (WIDE, 128), 1)
    y_in = ((yi >= 8) | (gy > 0)) & ((yi < Y + 8) | (gy < ny - 1))

    def one(x):
        x_in = ((x >= 4) | (gx > 0)) & ((x < X + 4) | (gx < nx - 1))
        g = jnp.where(y_in & x_in, 1.0 / (6.0 + U[3, x, inner, :]), 0.0)
        for c in range(3):
            ug = U[c, x, inner, :] * g
            plus, minus = g + ug, g - ug
            if c == 2:
                plus = jnp.where(zi == 0, 0.0, plus)
                minus = jnp.where(zi == 127, 0.0, minus)
            A[2 * c, x, inner, :] = plus
            A[2 * c + 1, x, inner, :] = minus

    for_rows(rows, one, 2)


def for_rows(rows, body, unroll):
    def run(i, carry):
        for first, last in rows:
            body(first + i)
        return carry

    lax.fori_loop(0, rows[0][1] - rows[0][0], run, 0, unroll=unroll)


def power_rows(Y, V, V4, A, k, rows, unroll):
    begin, size = (YP, Y) if k == S else (YP - 8, Y + 16)
    here = pl.ds(begin, size)

    def one(x):
        a = [A[c, x, here, :] for c in range(6)]
        for f in range(RHS):
            centre = V[k - 1, f, x, here, :]
            value = a[4] * pltpu.roll(centre, 1, 1) + a[5] * pltpu.roll(centre, 127, 1)
            value += a[0] * V[k - 1, f, x - 1, here, :] + a[1] * V[k - 1, f, x + 1, here, :]
            value += a[2] * V[k - 1, f, x, pl.ds(begin - 1, size), :]
            value += a[3] * V[k - 1, f, x, pl.ds(begin + 1, size), :]
            if k == S:
                V4[f, x - 4] = value
            else:
                V[k, f, x, here, :] = value

    for_rows(rows, one, unroll)


def basis_rows(V, V4, k, x, at, size):
    if k >= RHS * S:
        return V4[k - RHS * S, x, pl.ds(at, size), :]
    return V[k // RHS, k % RHS, x + 4, pl.ds(YP + at, size), :]


def local_factor(Y, V, V4, Q, rows):
    CH = 32
    zero = jnp.zeros((8, 128), F32)

    def first_dots(i, accs):
        accs = list(accs)
        for first, _ in rows:
            x = first + i
            for at in range(0, Y, CH):
                q = basis_rows(V, V4, 0, x, at, CH)
                for k in range(COLS):
                    accs[k] = accs[k] + fold8(q * basis_rows(V, V4, k, x, at, CH))
        return tuple(accs)

    count = rows[0][1] - rows[0][0]
    accs = lax.fori_loop(0, count, first_dots, (zero,) * COLS, unroll=4)
    lane = lax.broadcasted_iota(jnp.int32, (1, 128), 1)
    line = jnp.zeros((1, 128), F32)
    for j in range(COLS):
        dots = [total(a) for a in accs]
        live = dots[0] > 0.0
        length = jnp.sqrt(jnp.where(live, dots[0], 1.0))
        inv = jnp.where(live, 1.0 / length, 0.0)
        for k in range(j, COLS):
            line = jnp.where(lane == slot(j, k), dots[k - j] * inv, line)
        if j == COLS - 1:
            return line
        recip = 1.0 / jnp.where(live, dots[0], 1.0)
        alphas = [jnp.broadcast_to(d * recip, (8, 128)) for d in dots[1:]]

        def get(k, x, at, size, j=j):
            if j == 0 or k == 0:
                return basis_rows(V, V4, k, x, at, size)
            return Q[k - 1, x, pl.ds(at, size), :]

        def sweep(i, accs, j=j, get=get, alphas=alphas):
            accs = list(accs)
            for first, _ in rows:
                x = first + i
                for at in range(0, Y, CH):
                    q = get(j, x, at, CH)
                    after = None
                    for k in range(j + 1, COLS):
                        alpha = jnp.concatenate([alphas[k - j - 1]] * (CH // 8), axis=0)
                        value = get(k, x, at, CH) - alpha * q
                        Q[k - 1, x, pl.ds(at, CH), :] = value
                        if k == j + 1:
                            after = value
                        accs[k - j - 1] = accs[k - j - 1] + fold8(after * value)
            return tuple(accs)

        accs = lax.fori_loop(0, count, sweep, (zero,) * (COLS - 1 - j), unroll=4)


def inner_kernel(X, Y, V_in, U, V, V4, A, line, Q):
    coefficient_rows(X, Y, U, A, [(4, X + 4)])
    for k in range(1, S + 1):
        power_rows(Y, V, V4, A, k, [(4 + k, X + 4 - k)], 4)
    line[...] = local_factor(Y, V, V4, Q, [(4, X // 2), (X // 2, X - 4)])


def outer_kernel(X, Y, x0, x1, c0, c1, inner_line, V_in, V4_in, A_in, U_in, V, V4, A, U, packed, Q):
    own_y = slice(YP, YP + Y)
    for pairing, (got, corner) in enumerate(((x0, c0), (x1, c1))):
        high = toward_high("gx", pairing)
        at4, at3 = jnp.where(high, X + 4, 0), jnp.where(high, X + 4, 1)
        for i in range(4):
            for f in range(RHS):
                V[0, f, at4 + i, own_y, :] = got[4 * f + i]
        for i in range(3):
            for c in range(4):
                U[c, at3 + i, own_y, :] = got[8 + 3 * c + i]
        for row, (f, x, y) in enumerate(corner_cells(X, Y, high, False)):
            if f < 2:
                V[0, f, x, y : y + 1, :] = corner[row : row + 1, :]
            else:
                U[f - 2, x, y : y + 1, :] = corner[row : row + 1, :]
    coefficient_rows(X, Y, U, A, [(1, 4), (X + 4, X + 7)])
    for k in range(1, S + 1):
        power_rows(Y, V, V4, A, k, [(k, k + 4), (X + 4 - k, X + 8 - k)], 2)
    line = local_factor(Y, V, V4, Q, [(0, 4), (X - 4, X)])
    row = lax.broadcasted_iota(jnp.int32, (8, 128), 0)
    both = jnp.where(row % 2 == 0, inner_line[...], line)
    packed[...] = jnp.concatenate([both] * (packed.shape[0] // 8), axis=0)


def fold_lanes(x):
    parts = [x[:, i : i + 128] for i in range(0, x.shape[1], 128)]
    return functools.reduce(lambda a, b: a + b, parts)


def merged_factor(gathered):
    g = gathered.T
    cols = []
    for k in range(COLS):
        if k < 8:
            cols.append([g[8 * k : 8 * k + 8]])
        else:
            at = 64 + 16 * (k - 8)
            cols.append([g[at : at + 8], g[at + 8 : at + 16]])
    R = {}
    for j in range(COLS):
        dots = []
        for k in range(j, COLS):
            p = fold_lanes(cols[j][0] * cols[k][0])
            if j >= 8:
                p = p + fold_lanes(cols[j][1] * cols[k][1])
            dots.append(total(p))
        inv = 1.0 / jnp.sqrt(dots[0])
        for k in range(j, COLS):
            R[j, k] = dots[k - j] * inv
        inv2 = inv * inv
        for k in range(j + 1, COLS):
            alpha = dots[k - j] * inv2
            for part in range(len(cols[j])):
                cols[k][part] = cols[k][part] - alpha * cols[j][part]
    return R


def inverse(R):
    T = {}
    recip = [1.0 / R[j, j] for j in range(COLS)]
    for j in range(COLS):
        T[j, j] = recip[j]
        for i in range(j):
            s = T[i, i] * R[i, j]
            for k in range(i + 1, j):
                s = s + T[i, k] * R[k, j]
            T[i, j] = -s * recip[j]
    return T


def least_squares(R):
    n = RHS * S
    cols = []
    for c in range(n):
        col = []
        for i in range(c + RHS + 1):
            minus = R[i, c + RHS]
            col.append(R[i, c] - minus if i <= c else -minus)
        cols.append(col)
    upper, target = {}, {}
    recips = []

    def dot(a, b):
        terms = [x * y for x, y in zip(a, b)]
        while len(terms) > 1:
            terms = [x + y for x, y in zip(terms[::2], terms[1::2])] + (
                [terms[-1]] if len(terms) % 2 else []
            )
        return terms[0]

    for j in range(n):
        inv = 1.0 / jnp.sqrt(dot(cols[j], cols[j]))
        recips.append(inv)
        q = [v * inv for v in cols[j]]
        for c in range(j + 1, n):
            w = dot(q, cols[c])
            upper[j, c] = w
            for i in range(len(q)):
                cols[c][i] = cols[c][i] - w * q[i]
        for e in range(RHS):
            target[j, e] = dot(q, [R[i, e] for i in range(e + 1)])
    coef = {}
    for e in range(RHS):
        for j in reversed(range(n)):
            value = target[j, e]
            for later in range(j + 1, n):
                value = value - upper[j, later] * coef[later, e]
            coef[j, e] = value * recips[j]
    return coef


def final_kernel(
    X, Y, scale, gathered, V, V4, ortho, triangle, update, O, W, out_sems
):
    R = merged_factor(gathered[...])
    row = lax.broadcasted_iota(jnp.int32, (16, 128), 0)
    lane = lax.broadcasted_iota(jnp.int32, (16, 128), 1)
    tri = jnp.zeros((16, 128), F32)
    for (i, j), value in R.items():
        tri = jnp.where((row == i) & (lane == j), value * (1.0 / scale), tri)
    triangle[...] = tri[:COLS, :COLS]
    T = inverse(R)
    weights = {}
    for n, ((i, j), value) in enumerate(T.items()):
        weights[i, j] = n
        W[n] = jnp.broadcast_to(value * scale, (8, 128))
    coef = least_squares(R)
    base = len(weights)
    for n, ((k, e), value) in enumerate(coef.items()):
        weights[k, COLS + e] = base + n
        W[base + n] = jnp.broadcast_to(value, (8, 128))

    CH = 32
    XB = 2
    outs = []
    for block in range(X // XB):

        def rows(i, carry, block=block):
            x = block * XB + i
            for at in range(0, Y, CH):
                b = [basis_rows(V, V4, k, x, at, CH) for k in range(COLS)]
                for j in range(COLS + RHS):
                    value = None
                    for k in range(j + 1 if j < COLS else RHS * S):
                        w = jnp.concatenate([W[weights[k, j]]] * (CH // 8), axis=0)
                        value = w * b[k] if value is None else value + w * b[k]
                    O[j, x, pl.ds(at, CH), :] = value
            return carry

        lax.fori_loop(0, XB, rows, 0)
        here = pl.ds(block * XB, XB)
        for copy in (
            pltpu.make_async_copy(
                O.at[pl.ds(0, COLS), here], ortho.at[:, here], out_sems.at[2 * block]
            ),
            pltpu.make_async_copy(
                O.at[pl.ds(COLS, RHS), here], update.at[:, here], out_sems.at[2 * block + 1]
            ),
        ):
            copy.start()
            outs.append(copy)
    for copy in outs:
        copy.wait()


ANY = pl.BlockSpec(memory_space=pl.ANY)
VMEM = pl.BlockSpec(memory_space=pltpu.VMEM)
MIB = 1024 * 1024
PIN, BLOCK, FAR = range(3)


def call(kernel, name, inputs, outputs, scratch=(), aliases={}, limit=4):
    pin = lambda a: pltpu.with_memory_space_constraint(a, pltpu.VMEM)
    spec = lambda place: ANY if place == FAR else VMEM
    return pl.pallas_call(
        kernel,
        out_shape=tuple(
            pltpu.VMEM(o, F32) if place == PIN else jax.ShapeDtypeStruct(o, F32)
            for o, place in outputs
        ),
        in_specs=[spec(place) for _, place in inputs],
        out_specs=tuple(spec(place) for _, place in outputs),
        scratch_shapes=list(scratch),
        input_output_aliases=aliases,
        compiler_params=pltpu.CompilerParams(vmem_limit_bytes=limit * MIB),
        name=name,
    )(*(pin(a) if place == PIN else a for a, place in inputs))


def body(right_sides, diagonal, velocity):
    _, X, Y, Z = right_sides.shape
    nx, ny = lax.axis_size("gx"), lax.axis_size("gy")
    devices = nx * ny
    scale = math.sqrt(X * Y * Z * devices)
    XE, YE = X + 8, Y + 2 * YP
    inputs = [
        (pltpu.with_memory_space_constraint(a, pltpu.HBM), FAR)
        for a in (right_sides, velocity, diagonal)
    ]
    dma = pltpu.SemaphoreType.DMA

    def swap(value, axis, pairing):
        size = lax.axis_size(axis)
        pairs = [(i, i + 1) for i in range(pairing, size - 1, 2)]
        return lax.ppermute(value, axis, pairs + [(j, i) for i, j in pairs])

    v_shape, u_shape = ((S, RHS, XE, YE, Z), PIN), ((4, XE, YE, Z), PIN)
    x_slab, y_slab = ((20, Y, Z), PIN), ((24 * X, Z), PIN)
    x0, x1, y0, y1, V, U = call(
        functools.partial(pack_kernel, X, Y),
        "pack",
        inputs,
        [x_slab, x_slab, y_slab, y_slab, v_shape, u_shape],
        [dma((15,))],
    )
    x0, x1 = swap(x0, "gx", 0), swap(x1, "gx", 1)
    y1, y0 = swap(y1, "gy", 1), swap(y0, "gy", 0)
    strip = ((2 * CORNER_ROWS, Z), PIN)
    V, U, c0, c1 = call(
        functools.partial(place_y_kernel, X, Y),
        "place_y",
        [(y0, PIN), (y1, PIN), (V, PIN), (U, PIN)],
        [v_shape, u_shape, strip, strip],
        aliases={2: 0, 3: 1},
    )
    c0, c1 = swap(c0, "gx", 0), swap(c1, "gx", 1)
    v4_shape, a_shape = ((RHS, X, Y, Z), PIN), ((6, XE, YE, Z), PIN)
    work = pltpu.VMEM((COLS - 1, X, Y, Z), F32)
    V, V4, A, line = call(
        functools.partial(inner_kernel, X, Y),
        "inner",
        [(V, PIN), (U, PIN)],
        [v_shape, v4_shape, a_shape, ((1, 128), PIN)],
        [work],
        aliases={0: 0},
        limit=8,
    )
    V, V4, A, U, packed = call(
        functools.partial(outer_kernel, X, Y),
        "outer",
        [(a, PIN) for a in (x0, x1, c0, c1, line, V, V4, A, U)],
        [v_shape, v4_shape, a_shape, u_shape, ((2 * devices, 128), BLOCK)],
        [work],
        aliases={5: 0, 6: 1, 7: 2, 8: 3},
        limit=8,
    )
    gathered = lax.all_to_all(packed, ("gx", "gy"), 0, 0, tiled=True)
    out = [((COLS, X, Y, Z), FAR), ((COLS, COLS), BLOCK), ((RHS, X, Y, Z), FAR)]
    ortho, triangle, update = call(
        functools.partial(final_kernel, X, Y, scale),
        "combine",
        [(gathered, BLOCK), (V, PIN), (V4, PIN)],
        out,
        [
            pltpu.VMEM((COLS + RHS, X, Y, Z), F32),
            pltpu.VMEM((71, 8, 128), F32),
            dma((X,)),
        ],
        limit=10,
    )
    return ortho, triangle, update


def solution(mesh):
    return jax.shard_map(
        body,
        mesh=mesh,
        in_specs=(P(None, "gx", "gy", None), P("gx", "gy", None), P(None, "gx", "gy", None)),
        out_specs=(P(None, "gx", "gy", None), P(), P(None, "gx", "gy", None)),
        check_vma=False,
    )
```

```python
import functools
import math

import jax
import jax.numpy as jnp
from jax import lax
from jax.experimental import pallas as pl
from jax.experimental.pallas import tpu as pltpu
from jax.sharding import PartitionSpec as P

S = 4
RHS = 2
COLS = 10
YP = 16

F32 = jnp.float32
FIELD_CORNER = [(dx, dy) for dx in (1, 2, 3) for dy in (1, 2, 3) if dx + dy <= 4]
COEF_CORNER = [(dx, dy) for dx in (1, 2) for dy in (1, 2) if dx + dy <= 3]
CORNER_ROWS = RHS * len(FIELD_CORNER) + 4 * len(COEF_CORNER)


def slot(leaf, i, k):
    if i >= 8:
        return 104 + 3 * leaf + (k - 8) + (i - 8)
    if k >= 8:
        return 72 + 16 * leaf + 8 * (k - 8) + i
    if k == 7:
        return 56 + 8 * leaf + i
    return 8 * (6 - k) + 7 - k + i if leaf else 8 * k + i


def unpack(g, leaf):
    row = lax.broadcasted_iota(jnp.int32, (8, g.shape[1]), 0)

    def rows(first, count):
        group = g[8 * (first // 8) : 8 * (first // 8) + 8]
        if first % 8:
            group = pltpu.roll(group, 8 - first % 8, 0)
        return group if count == 8 else jnp.where(row < count, group, 0.0)

    cols = []
    for k in range(COLS):
        parts = [rows(slot(leaf, 0, k), min(k + 1, 8))]
        if k >= 8:
            parts.append(rows(slot(leaf, 8, k), k - 7))
        cols.append(parts)
    return cols


def toward_high(axis, pairing):
    return lax.axis_index(axis) % 2 == pairing


def pack_kernel(X, Y, rhs, vel, diag, x0, x1, y0, y1, V, U, sems):
    own_x, own_y = pl.ds(4, X), pl.ds(YP, Y)
    copies = [
        (rhs, V.at[0, :, own_x, own_y]),
        (vel, U.at[pl.ds(0, 3), own_x, own_y]),
        (diag, U.at[3, own_x, own_y]),
    ]
    copies = [pltpu.make_async_copy(s, d, sems.at[i]) for i, (s, d) in enumerate(copies)]
    for copy in copies:
        copy.start()
    for copy in copies:
        copy.wait()
    for pairing, out in enumerate((x0, x1)):
        high = toward_high("gx", pairing)
        at4, at3 = jnp.where(high, X, 4), jnp.where(high, X + 1, 4)
        for i in range(4):
            for f in range(RHS):
                out[4 * f + i] = V[0, f, at4 + i, YP : YP + Y, :]
        for i in range(3):
            for c in range(4):
                out[8 + 3 * c + i] = U[c, at3 + i, YP : YP + Y, :]
    first_high = toward_high("gy", 0)
    for f in range(6):
        for x in range(X):
            field = V.at[0, f, 4 + x] if f < 2 else U.at[f - 2, 4 + x]
            low, high = field[YP : YP + 4, :], field[YP + Y - 4 : YP + Y, :]
            at = 4 * (f * X + x)
            y0[at : at + 4, :] = jnp.where(first_high, high, low)
            y1[at : at + 4, :] = jnp.where(first_high, low, high)


def corner_cells(X, Y, high, own):
    cells = []
    for y_low in (True, False):
        for f in range(6):
            for dx, dy in FIELD_CORNER if f < 2 else COEF_CORNER:
                if own:
                    x = jnp.where(high, X + 4 - dx, 3 + dx)
                else:
                    x = jnp.where(high, X + 3 + dx, 4 - dx)
                cells.append((f, x, YP - dy if y_low else YP + Y - 1 + dy))
    return cells


def place_y_kernel(X, Y, y0, y1, V_in, U_in, V, U, first, second):
    first_high = toward_high("gy", 0)
    for f in range(6):
        for x in range(X):
            at = 4 * (f * X + x)
            a, b = y0[at : at + 4, :], y1[at : at + 4, :]
            field = V.at[0, f, 4 + x] if f < 2 else U.at[f - 2, 4 + x]
            field[YP - 4 : YP, :] = jnp.where(first_high, b, a)
            field[YP + Y : YP + Y + 4, :] = jnp.where(first_high, a, b)
    for pairing, out in enumerate((first, second)):
        cells = corner_cells(X, Y, toward_high("gx", pairing), True)
        for row, (f, x, y) in enumerate(cells):
            out[row : row + 1, :] = (
                V[0, f, x, y : y + 1, :] if f < 2 else U[f - 2, x, y : y + 1, :]
            )


def total(x):
    return jnp.sum(jnp.sum(x, axis=0, keepdims=True), axis=1, keepdims=True)


def fold8(x):
    rows = x.shape[0]
    parts = [x[8 * i : 8 * i + 8] for i in range(rows // 8)]
    while len(parts) > 1:
        parts = [a + b for a, b in zip(parts[::2], parts[1::2])] + (
            [parts[-1]] if len(parts) % 2 else []
        )
    return parts[0]


def coefficient_rows(X, Y, U, A, rows, begin, size):
    gx, gy = lax.axis_index("gx"), lax.axis_index("gy")
    nx, ny = lax.axis_size("gx"), lax.axis_size("gy")
    here = pl.ds(begin, size)
    yi = begin + lax.broadcasted_iota(jnp.int32, (size, 128), 0)
    zi = lax.broadcasted_iota(jnp.int32, (size, 128), 1)
    y_in = ((yi >= YP) | (gy > 0)) & ((yi < Y + YP) | (gy < ny - 1))

    def one(x):
        x_in = ((x >= 4) | (gx > 0)) & ((x < X + 4) | (gx < nx - 1))
        g = jnp.where(y_in & x_in, 1.0 / (6.0 + U[3, x, here, :]), 0.0)
        for c in range(3):
            ug = U[c, x, here, :] * g
            plus, minus = g + ug, g - ug
            if c == 2:
                plus = jnp.where(zi == 0, 0.0, plus)
                minus = jnp.where(zi == 127, 0.0, minus)
            A[2 * c, x, here, :] = plus
            A[2 * c + 1, x, here, :] = minus

    for_rows(rows, one, 2)


def for_rows(rows, body, unroll):
    def run(i, carry):
        for first, last in rows:
            body(first + i)
        return carry

    lax.fori_loop(0, rows[0][1] - rows[0][0], run, 0, unroll=unroll)


def power_rows(V, V4, A, k, rows, pieces, unroll):
    def one(x):
        for begin, size in pieces:
            here = pl.ds(begin, size)
            a = [A[c, x, here, :] for c in range(6)]
            for f in range(RHS):
                centre = V[k - 1, f, x, here, :]
                value = a[4] * pltpu.roll(centre, 1, 1) + a[5] * pltpu.roll(centre, 127, 1)
                value += a[0] * V[k - 1, f, x - 1, here, :] + a[1] * V[k - 1, f, x + 1, here, :]
                value += a[2] * V[k - 1, f, x, pl.ds(begin - 1, size), :]
                value += a[3] * V[k - 1, f, x, pl.ds(begin + 1, size), :]
                if k == S:
                    V4[f, x - 4, pl.ds(begin - YP, size), :] = value
                else:
                    V[k, f, x, here, :] = value

    for_rows(rows, one, unroll)


def basis_rows(V, V4, k, x, at, size):
    if k >= RHS * S:
        return V4[k - RHS * S, x, pl.ds(at, size), :]
    return V[k // RHS, k % RHS, x + 4, pl.ds(YP + at, size), :]


def local_factor(V, V4, Q, leaf, count, pieces):
    zero = jnp.zeros((8, 128), F32)

    def first_dots(i, accs):
        accs = list(accs)
        for row, at, size in pieces:
            x = row + i
            q = basis_rows(V, V4, 0, x, at, size)
            for k in range(COLS):
                accs[k] = accs[k] + fold8(q * basis_rows(V, V4, k, x, at, size))
        return tuple(accs)

    accs = lax.fori_loop(0, count, first_dots, (zero,) * COLS, unroll=4)
    lane = lax.broadcasted_iota(jnp.int32, (1, 128), 1)
    line = jnp.zeros((1, 128), F32)
    for j in range(COLS):
        dots = [total(a) for a in accs]
        live = dots[0] > 0.0
        length = jnp.sqrt(jnp.where(live, dots[0], 1.0))
        inv = jnp.where(live, 1.0 / length, 0.0)
        for k in range(j, COLS):
            line = jnp.where(lane == slot(leaf, j, k), dots[k - j] * inv, line)
        if j == COLS - 1:
            return line
        recip = 1.0 / jnp.where(live, dots[0], 1.0)
        alphas = [jnp.broadcast_to(d * recip, (8, 128)) for d in dots[1:]]

        def get(k, x, at, size, j=j):
            if j == 0 or k == 0:
                return basis_rows(V, V4, k, x, at, size)
            return Q[k - 1, x, pl.ds(at, size), :]

        def sweep(i, accs, j=j, get=get, alphas=alphas):
            accs = list(accs)
            for row, at, size in pieces:
                x = row + i
                q = get(j, x, at, size)
                after = None
                for k in range(j + 1, COLS):
                    alpha = jnp.concatenate([alphas[k - j - 1]] * (size // 8), axis=0)
                    value = get(k, x, at, size) - alpha * q
                    Q[k - 1, x, pl.ds(at, size), :] = value
                    if k == j + 1:
                        after = value
                    accs[k - j - 1] = accs[k - j - 1] + fold8(after * value)
            return tuple(accs)

        accs = lax.fori_loop(0, count, sweep, (zero,) * (COLS - 1 - j), unroll=4)


def inner_kernel(X, Y, V_in, U, V, V4, A, line, Q):
    coefficient_rows(X, Y, U, A, [(4, X + 4)], YP, Y)
    for k in range(1, S + 1):
        power_rows(V, V4, A, k, [(4 + k, X + 4 - k)], [(YP, Y)], 4)
    half = (Y - 16) // 2
    pieces = [(row, at, half) for row in (4, X // 2) for at in (8, 8 + half)]
    line[...] = local_factor(V, V4, Q, 0, X // 2 - 4, pieces)


def edge_kernel(X, Y, U, V_in, V4_in, A_in, V, V4, A):
    for begin in (YP - 8, YP + Y):
        coefficient_rows(X, Y, U, A, [(4, X + 4)], begin, 8)
    for k in range(1, S):
        pieces = [(YP - 8, 16), (YP + Y - 8, 16)]
        power_rows(V, V4, A, k, [(4 + k, X + 4 - k)], pieces, 4)
    power_rows(V, V4, A, S, [(4 + S, X + 4 - S)], [(YP, 8), (YP + Y - 8, 8)], 4)


def outer_kernel(X, Y, x0, x1, c0, c1, inner_line, V_in, V4_in, A_in, U_in, V, V4, A, U, packed, Q):
    own_y = slice(YP, YP + Y)
    for pairing, (got, corner) in enumerate(((x0, c0), (x1, c1))):
        high = toward_high("gx", pairing)
        at4, at3 = jnp.where(high, X + 4, 0), jnp.where(high, X + 4, 1)
        for i in range(4):
            for f in range(RHS):
                V[0, f, at4 + i, own_y, :] = got[4 * f + i]
        for i in range(3):
            for c in range(4):
                U[c, at3 + i, own_y, :] = got[8 + 3 * c + i]
        for row, (f, x, y) in enumerate(corner_cells(X, Y, high, False)):
            if f < 2:
                V[0, f, x, y : y + 1, :] = corner[row : row + 1, :]
            else:
                U[f - 2, x, y : y + 1, :] = corner[row : row + 1, :]
    coefficient_rows(X, Y, U, A, [(1, 4), (X + 4, X + 7)], YP - 8, Y + 16)
    for k in range(1, S + 1):
        piece = (YP - 8, Y + 16) if k < S else (YP, Y)
        power_rows(V, V4, A, k, [(k, k + 4), (X + 4 - k, X + 8 - k)], [piece], 2)
    pieces = [(row, at, Y // 2) for row in (0, X - 4) for at in (0, Y // 2)]
    pieces += [(row, at, 8) for row in (4, X // 2) for at in (0, Y - 8)]
    line = local_factor(V, V4, Q, 1, 4, pieces)
    packed[...] = jnp.broadcast_to(inner_line[...] + line, packed.shape)


def fold_lanes(x):
    parts = [x[:, i : i + 128] for i in range(0, x.shape[1], 128)]
    return functools.reduce(lambda a, b: a + b, parts)


def merged_factor(gathered):
    g = gathered.T
    cols = [
        [jnp.concatenate(parts, axis=1) for parts in zip(*pair)]
        for pair in zip(unpack(g, 0), unpack(g, 1))
    ]
    R = {}
    for j in range(COLS):
        dots = []
        for k in range(j, COLS):
            p = fold_lanes(cols[j][0] * cols[k][0])
            if j >= 8:
                p = p + fold_lanes(cols[j][1] * cols[k][1])
            dots.append(total(p))
        inv = 1.0 / jnp.sqrt(dots[0])
        for k in range(j, COLS):
            R[j, k] = dots[k - j] * inv
        recip = 1.0 / dots[0]
        for k in range(j + 1, COLS):
            alpha = dots[k - j] * recip
            for part in range(len(cols[j])):
                cols[k][part] = cols[k][part] - alpha * cols[j][part]
    return R


def inverse(R):
    T = {}
    recip = [1.0 / R[j, j] for j in range(COLS)]
    for j in range(COLS):
        T[j, j] = recip[j]
        for i in range(j):
            s = T[i, i] * R[i, j]
            for k in range(i + 1, j):
                s = s + T[i, k] * R[k, j]
            T[i, j] = -s * recip[j]
    return T


def least_squares(R):
    n = RHS * S
    cols = []
    for c in range(n):
        col = []
        for i in range(c + RHS + 1):
            minus = R[i, c + RHS]
            col.append(R[i, c] - minus if i <= c else -minus)
        cols.append(col)
    upper, target = {}, {}
    recips = []

    def dot(a, b):
        terms = [x * y for x, y in zip(a, b)]
        while len(terms) > 1:
            terms = [x + y for x, y in zip(terms[::2], terms[1::2])] + (
                [terms[-1]] if len(terms) % 2 else []
            )
        return terms[0]

    for j in range(n):
        inv = 1.0 / jnp.sqrt(dot(cols[j], cols[j]))
        recips.append(inv)
        q = [v * inv for v in cols[j]]
        for c in range(j + 1, n):
            w = dot(q, cols[c])
            upper[j, c] = w
            for i in range(len(q)):
                cols[c][i] = cols[c][i] - w * q[i]
        for e in range(RHS):
            target[j, e] = dot(q, [R[i, e] for i in range(e + 1)])
    coef = {}
    for e in range(RHS):
        for j in reversed(range(n)):
            value = target[j, e]
            for later in range(j + 1, n):
                value = value - upper[j, later] * coef[later, e]
            coef[j, e] = value * recips[j]
    return coef


def final_kernel(
    X, Y, scale, gathered, V, V4, ortho, triangle, update, O, W, out_sems
):
    R = merged_factor(gathered[...])
    row = lax.broadcasted_iota(jnp.int32, (16, 128), 0)
    lane = lax.broadcasted_iota(jnp.int32, (16, 128), 1)
    tri = jnp.zeros((16, 128), F32)
    for (i, j), value in R.items():
        tri = jnp.where((row == i) & (lane == j), value * (1.0 / scale), tri)
    triangle[...] = tri[:COLS, :COLS]
    T = inverse(R)
    weights = {}
    for n, ((i, j), value) in enumerate(T.items()):
        weights[i, j] = n
        W[n] = jnp.broadcast_to(value * scale, (8, 128))
    coef = least_squares(R)
    base = len(weights)
    for n, ((k, e), value) in enumerate(coef.items()):
        weights[k, COLS + e] = base + n
        W[base + n] = jnp.broadcast_to(value, (8, 128))

    CH = 32
    XB = 2
    outs = []
    for block in range(X // XB):

        def rows(i, carry, block=block):
            x = block * XB + i
            for at in range(0, Y, CH):
                b = [basis_rows(V, V4, k, x, at, CH) for k in range(COLS)]
                for j in range(COLS + RHS):
                    value = None
                    for k in range(j + 1 if j < COLS else RHS * S):
                        w = jnp.concatenate([W[weights[k, j]]] * (CH // 8), axis=0)
                        value = w * b[k] if value is None else value + w * b[k]
                    O[j, x, pl.ds(at, CH), :] = value
            return carry

        lax.fori_loop(0, XB, rows, 0)
        here = pl.ds(block * XB, XB)
        for copy in (
            pltpu.make_async_copy(
                O.at[pl.ds(0, COLS), here], ortho.at[:, here], out_sems.at[2 * block]
            ),
            pltpu.make_async_copy(
                O.at[pl.ds(COLS, RHS), here], update.at[:, here], out_sems.at[2 * block + 1]
            ),
        ):
            copy.start()
            outs.append(copy)
    for copy in outs:
        copy.wait()


ANY = pl.BlockSpec(memory_space=pl.ANY)
VMEM = pl.BlockSpec(memory_space=pltpu.VMEM)
MIB = 1024 * 1024
PIN, BLOCK, FAR = range(3)


def call(kernel, name, inputs, outputs, scratch=(), aliases={}, limit=4):
    pin = lambda a: pltpu.with_memory_space_constraint(a, pltpu.VMEM)
    spec = lambda place: ANY if place == FAR else VMEM
    return pl.pallas_call(
        kernel,
        out_shape=tuple(
            pltpu.VMEM(o, F32) if place == PIN else jax.ShapeDtypeStruct(o, F32)
            for o, place in outputs
        ),
        in_specs=[spec(place) for _, place in inputs],
        out_specs=tuple(spec(place) for _, place in outputs),
        scratch_shapes=list(scratch),
        input_output_aliases=aliases,
        compiler_params=pltpu.CompilerParams(vmem_limit_bytes=limit * MIB),
        name=name,
    )(*(pin(a) if place == PIN else a for a, place in inputs))


def body(right_sides, diagonal, velocity):
    _, X, Y, Z = right_sides.shape
    nx, ny = lax.axis_size("gx"), lax.axis_size("gy")
    devices = nx * ny
    scale = math.sqrt(X * Y * Z * devices)
    XE, YE = X + 8, Y + 2 * YP
    inputs = [
        (pltpu.with_memory_space_constraint(a, pltpu.HBM), FAR)
        for a in (right_sides, velocity, diagonal)
    ]
    dma = pltpu.SemaphoreType.DMA

    def swap(value, axis, pairing):
        size = lax.axis_size(axis)
        pairs = [(i, i + 1) for i in range(pairing, size - 1, 2)]
        return lax.ppermute(value, axis, pairs + [(j, i) for i, j in pairs])

    v_shape, u_shape = ((S, RHS, XE, YE, Z), PIN), ((4, XE, YE, Z), PIN)
    x_slab, y_slab = ((20, Y, Z), PIN), ((24 * X, Z), PIN)
    x0, x1, y0, y1, V, U = call(
        functools.partial(pack_kernel, X, Y),
        "pack",
        inputs,
        [x_slab, x_slab, y_slab, y_slab, v_shape, u_shape],
        [dma((3,))],
    )
    x0, x1 = swap(x0, "gx", 0), swap(x1, "gx", 1)
    y1, y0 = swap(y1, "gy", 1), swap(y0, "gy", 0)
    v4_shape, a_shape = ((RHS, X, Y, Z), PIN), ((6, XE, YE, Z), PIN)
    work = pltpu.VMEM((COLS - 1, X, Y, Z), F32)
    V, V4, A, line = call(
        functools.partial(inner_kernel, X, Y),
        "inner",
        [(V, PIN), (U, PIN)],
        [v_shape, v4_shape, a_shape, ((1, 128), PIN)],
        [work],
        aliases={0: 0},
        limit=8,
    )
    strip = ((2 * CORNER_ROWS, Z), PIN)
    V, U, c0, c1 = call(
        functools.partial(place_y_kernel, X, Y),
        "place_y",
        [(y0, PIN), (y1, PIN), (V, PIN), (U, PIN)],
        [v_shape, u_shape, strip, strip],
        aliases={2: 0, 3: 1},
    )
    c0, c1 = swap(c0, "gx", 0), swap(c1, "gx", 1)
    V, V4, A = call(
        functools.partial(edge_kernel, X, Y),
        "edge",
        [(a, PIN) for a in (U, V, V4, A)],
        [v_shape, v4_shape, a_shape],
        aliases={1: 0, 2: 1, 3: 2},
    )
    V, V4, A, U, packed = call(
        functools.partial(outer_kernel, X, Y),
        "outer",
        [(a, PIN) for a in (x0, x1, c0, c1, line, V, V4, A, U)],
        [v_shape, v4_shape, a_shape, u_shape, ((devices, 128), BLOCK)],
        [work],
        aliases={5: 0, 6: 1, 7: 2, 8: 3},
        limit=8,
    )
    gathered = lax.all_to_all(packed, ("gx", "gy"), 0, 0, tiled=True)
    out = [((COLS, X, Y, Z), FAR), ((COLS, COLS), BLOCK), ((RHS, X, Y, Z), FAR)]
    ortho, triangle, update = call(
        functools.partial(final_kernel, X, Y, scale),
        "combine",
        [(gathered, BLOCK), (V, PIN), (V4, PIN)],
        out,
        [
            pltpu.VMEM((COLS + RHS, X, Y, Z), F32),
            pltpu.VMEM((71, 8, 128), F32),
            dma((X,)),
        ],
        limit=10,
    )
    return ortho, triangle, update


def solution(mesh):
    return jax.shard_map(
        body,
        mesh=mesh,
        in_specs=(P(None, "gx", "gy", None), P("gx", "gy", None), P(None, "gx", "gy", None)),
        out_specs=(P(None, "gx", "gy", None), P(), P(None, "gx", "gy", None)),
        check_vma=False,
    )
```

```python
import functools
import math

import jax
import jax.numpy as jnp
from jax import lax
from jax.experimental import pallas as pl
from jax.experimental.pallas import tpu as pltpu
from jax.sharding import PartitionSpec as P

S = 4
RHS = 2
COLS = 10
UNROLL = 4
YP = 16

F32 = jnp.float32
FIELD_CORNER = [(dx, dy) for dx in (1, 2, 3) for dy in (1, 2, 3) if dx + dy <= 4]
COEF_CORNER = [(dx, dy) for dx in (1, 2) for dy in (1, 2) if dx + dy <= 3]
CORNER_ROWS = RHS * len(FIELD_CORNER) + 4 * len(COEF_CORNER)


def slot(i, k):
    return (8 * k if k < 8 else 64 + 16 * (k - 8)) + i


def toward_high(axis, pairing):
    return lax.axis_index(axis) % 2 == pairing


def pack_kernel(X, Y, rhs, vel, diag, x0, x1, y0, y1, V, U, sems):
    own_x, own_y = pl.ds(4, X), pl.ds(YP, Y)
    copies = [
        (rhs, V.at[0, :, own_x, own_y]),
        (vel, U.at[pl.ds(0, 3), own_x, own_y]),
        (diag, U.at[3, own_x, own_y]),
    ]
    copies = [pltpu.make_async_copy(s, d, sems.at[i]) for i, (s, d) in enumerate(copies)]
    for copy in copies:
        copy.start()
    for copy in copies:
        copy.wait()
    for pairing, out in enumerate((x0, x1)):
        high = toward_high("gx", pairing)
        at4, at3 = jnp.where(high, X, 4), jnp.where(high, X + 1, 4)
        for i in range(4):
            for f in range(RHS):
                out[4 * f + i] = V[0, f, at4 + i, YP : YP + Y, :]
        for i in range(3):
            for c in range(4):
                out[8 + 3 * c + i] = U[c, at3 + i, YP : YP + Y, :]
    first_high = toward_high("gy", 0)
    for f in range(6):
        for x in range(X):
            field = V.at[0, f, 4 + x] if f < 2 else U.at[f - 2, 4 + x]
            low, high = field[YP : YP + 4, :], field[YP + Y - 4 : YP + Y, :]
            at = 4 * (f * X + x)
            y0[at : at + 4, :] = jnp.where(first_high, high, low)
            y1[at : at + 4, :] = jnp.where(first_high, low, high)


def corner_cells(X, Y, high, own):
    cells = []
    for y_low in (True, False):
        for f in range(6):
            for dx, dy in FIELD_CORNER if f < 2 else COEF_CORNER:
                if own:
                    x = jnp.where(high, X + 4 - dx, 3 + dx)
                else:
                    x = jnp.where(high, X + 3 + dx, 4 - dx)
                cells.append((f, x, YP - dy if y_low else YP + Y - 1 + dy))
    return cells


def place_y_kernel(X, Y, y0, y1, V_in, U_in, V, U, first, second):
    first_high = toward_high("gy", 0)
    for f in range(6):
        for x in range(X):
            at = 4 * (f * X + x)
            a, b = y0[at : at + 4, :], y1[at : at + 4, :]
            field = V.at[0, f, 4 + x] if f < 2 else U.at[f - 2, 4 + x]
            field[YP - 4 : YP, :] = jnp.where(first_high, b, a)
            field[YP + Y : YP + Y + 4, :] = jnp.where(first_high, a, b)
    for pairing, out in enumerate((first, second)):
        cells = corner_cells(X, Y, toward_high("gx", pairing), True)
        for row, (f, x, y) in enumerate(cells):
            out[row : row + 1, :] = (
                V[0, f, x, y : y + 1, :] if f < 2 else U[f - 2, x, y : y + 1, :]
            )


def total(x):
    return jnp.sum(jnp.sum(x, axis=0, keepdims=True), axis=1, keepdims=True)


def fold8(x):
    rows = x.shape[0]
    parts = [x[8 * i : 8 * i + 8] for i in range(rows // 8)]
    while len(parts) > 1:
        parts = [a + b for a, b in zip(parts[::2], parts[1::2])] + (
            [parts[-1]] if len(parts) % 2 else []
        )
    return parts[0]


def coefficient_rows(X, Y, U, A, rows, begin, size):
    gx, gy = lax.axis_index("gx"), lax.axis_index("gy")
    nx, ny = lax.axis_size("gx"), lax.axis_size("gy")
    here = pl.ds(begin, size)
    yi = begin + lax.broadcasted_iota(jnp.int32, (size, 128), 0)
    zi = lax.broadcasted_iota(jnp.int32, (size, 128), 1)
    y_in = ((yi >= YP) | (gy > 0)) & ((yi < Y + YP) | (gy < ny - 1))

    def one(x):
        x_in = ((x >= 4) | (gx > 0)) & ((x < X + 4) | (gx < nx - 1))
        g = jnp.where(y_in & x_in, 1.0 / (6.0 + U[3, x, here, :]), 0.0)
        for c in range(3):
            ug = U[c, x, here, :] * g
            plus, minus = g + ug, g - ug
            if c == 2:
                plus = jnp.where(zi == 0, 0.0, plus)
                minus = jnp.where(zi == 127, 0.0, minus)
            A[2 * c, x, here, :] = plus
            A[2 * c + 1, x, here, :] = minus

    for_rows(rows, one, 2)


def for_rows(rows, body, unroll):
    def run(i, carry):
        for first, last in rows:
            body(first + i)
        return carry

    lax.fori_loop(0, rows[0][1] - rows[0][0], run, 0, unroll=unroll)


def power_rows(V, V4, A, k, rows, pieces, unroll):
    def one(x):
        for begin, size in pieces:
            here = pl.ds(begin, size)
            a = [A[c, x, here, :] for c in range(6)]
            for f in range(RHS):
                centre = V[k - 1, f, x, here, :]
                value = a[4] * pltpu.roll(centre, 1, 1) + a[5] * pltpu.roll(centre, 127, 1)
                value += a[0] * V[k - 1, f, x - 1, here, :] + a[1] * V[k - 1, f, x + 1, here, :]
                value += a[2] * V[k - 1, f, x, pl.ds(begin - 1, size), :]
                value += a[3] * V[k - 1, f, x, pl.ds(begin + 1, size), :]
                if k == S:
                    V4[f, x - 4, pl.ds(begin - YP, size), :] = value
                else:
                    V[k, f, x, here, :] = value

    for_rows(rows, one, unroll)


def basis_rows(V, V4, k, x, at, size):
    if k >= RHS * S:
        return V4[k - RHS * S, x, pl.ds(at, size), :]
    return V[k // RHS, k % RHS, x + 4, pl.ds(YP + at, size), :]


def local_factor(V, V4, Q, count, pieces, before=None, packed=False):
    zero = jnp.zeros((8, 128), F32)
    top = [zero] * COLS
    if before is not None:
        first_row = lax.broadcasted_iota(jnp.int32, (8, 128), 0) == 0
        top = [jnp.where(first_row, before[k : k + 1, :], 0.0) for k in range(COLS)]

    def first_dots(i, accs):
        accs = list(accs)
        for row, at, size in pieces:
            x = row + i
            q = basis_rows(V, V4, 0, x, at, size)
            for k in range(COLS):
                accs[k] = accs[k] + fold8(q * basis_rows(V, V4, k, x, at, size))
        return tuple(accs)

    start = tuple(top[0] * t for t in top)
    accs = lax.fori_loop(0, count, first_dots, start, unroll=UNROLL)
    lane = lax.broadcasted_iota(jnp.int32, (1, 128), 1)
    lines = [jnp.zeros((1, 128), F32)] * (1 if packed else COLS)
    for j in range(COLS):
        dots = [total(a) for a in accs]
        live = dots[0] > 0.0
        length = jnp.sqrt(jnp.where(live, dots[0], 1.0))
        inv = jnp.where(live, 1.0 / length, 0.0)
        for k in range(j, COLS):
            line, at = (0, slot(j, k)) if packed else (k, j)
            lines[line] = jnp.where(lane == at, dots[k - j] * inv, lines[line])
        if j == COLS - 1:
            return lines
        recip = 1.0 / jnp.where(live, dots[0], 1.0)
        alphas = [jnp.broadcast_to(d * recip, (8, 128)) for d in dots[1:]]
        for k in range(j + 1, COLS):
            top[k] = top[k] - alphas[k - j - 1] * top[j]

        def get(k, x, at, size, j=j):
            if j == 0 or k == 0:
                return basis_rows(V, V4, k, x, at, size)
            return Q[k - 1, x, pl.ds(at, size), :]

        def sweep(i, accs, j=j, get=get, alphas=alphas):
            accs = list(accs)
            for row, at, size in pieces:
                x = row + i
                q = get(j, x, at, size)
                after = None
                for k in range(j + 1, COLS):
                    alpha = jnp.concatenate([alphas[k - j - 1]] * (size // 8), axis=0)
                    value = get(k, x, at, size) - alpha * q
                    Q[k - 1, x, pl.ds(at, size), :] = value
                    if k == j + 1:
                        after = value
                    accs[k - j - 1] = accs[k - j - 1] + fold8(after * value)
            return tuple(accs)

        start = tuple(top[j + 1] * t for t in top[j + 1 :])
        accs = lax.fori_loop(0, count, sweep, start, unroll=UNROLL)


def store_factor(out, lines):
    for k, line in enumerate(lines):
        out[k : k + 1, :] = line


def inner_kernel(X, Y, V_in, U, V, V4, A, factor, Q):
    coefficient_rows(X, Y, U, A, [(4, X + 4)], YP, Y)
    for k in range(1, S + 1):
        power_rows(V, V4, A, k, [(4 + k, X + 4 - k)], [(YP, Y)], 4)
    half = (Y - 16) // 2
    pieces = [(row, at, half) for row in (4, X // 2) for at in (8, 8 + half)]
    store_factor(factor, local_factor(V, V4, Q, X // 2 - 4, pieces))


def beside_y(Y, k):
    if k == S:
        return [(YP, 8), (YP + Y - 8, 8)]
    return [(YP - 8, 16), (YP + Y - 8, 16)]


def edge_kernel(X, Y, U, V_in, V4_in, A_in, V, V4, A):
    for begin in (YP - 8, YP + Y):
        coefficient_rows(X, Y, U, A, [(4, X + 4)], begin, 8)
    for k in range(1, S + 1):
        power_rows(V, V4, A, k, [(4 + k, X + 4 - k)], beside_y(Y, k), 7)


def near_x(X, k):
    return [(k, k + 4), (X + 4 - k, X + 8 - k)]


def face_kernel(X, Y, x0, x1, before, V_in, V4_in, A_in, U_in, V, V4, A, U, factor, Q):
    for pairing, got in enumerate((x0, x1)):
        high = toward_high("gx", pairing)
        at4, at3 = jnp.where(high, X + 4, 0), jnp.where(high, X + 4, 1)
        for i in range(4):
            for f in range(RHS):
                V[0, f, at4 + i, YP : YP + Y, :] = got[4 * f + i]
        for i in range(3):
            for c in range(4):
                U[c, at3 + i, YP : YP + Y, :] = got[8 + 3 * c + i]
    coefficient_rows(X, Y, U, A, [(1, 4), (X + 4, X + 7)], YP, Y)
    for k in range(1, S + 1):
        power_rows(V, V4, A, k, near_x(X, k), [(YP, Y)], 2)
    half = (Y - 16) // 2
    pieces = [(row, at, half) for row in (0, X - 4) for at in (8, 8 + half)]
    pieces += [(row, at, 8) for row in (4, X // 2) for at in (0, Y - 8)]
    store_factor(factor, local_factor(V, V4, Q, 4, pieces, before))


def corner_kernel(X, Y, c0, c1, before, V_in, V4_in, A_in, U_in, V, V4, A, U, packed, Q):
    for pairing, corner in enumerate((c0, c1)):
        cells = corner_cells(X, Y, toward_high("gx", pairing), False)
        for row, (f, x, y) in enumerate(cells):
            if f < 2:
                V[0, f, x, y : y + 1, :] = corner[row : row + 1, :]
            else:
                U[f - 2, x, y : y + 1, :] = corner[row : row + 1, :]
    for begin in (YP - 8, YP + Y):
        coefficient_rows(X, Y, U, A, [(1, 4), (X + 4, X + 7)], begin, 8)
    for k in range(1, S + 1):
        power_rows(V, V4, A, k, near_x(X, k), beside_y(Y, k), 4)
    pieces = [(row, at, 8) for row in (0, X - 4) for at in (0, Y - 8)]
    (line,) = local_factor(V, V4, Q, 4, pieces, before, packed=True)
    packed[...] = jnp.broadcast_to(line, packed.shape)


def fold_lanes(x):
    parts = [x[:, i : i + 128] for i in range(0, x.shape[1], 128)]
    return functools.reduce(lambda a, b: a + b, parts)


def merged_factor(gathered):
    g = gathered.T
    cols = []
    for k in range(COLS):
        at = slot(0, k)
        cols.append([g[i : i + 8] for i in range(at, at + k + 1, 8)])
    R = {}
    for j in range(COLS):
        dots = []
        for k in range(j, COLS):
            p = fold_lanes(cols[j][0] * cols[k][0])
            if j >= 8:
                p = p + fold_lanes(cols[j][1] * cols[k][1])
            dots.append(total(p))
        inv = 1.0 / jnp.sqrt(dots[0])
        for k in range(j, COLS):
            R[j, k] = dots[k - j] * inv
        recip = 1.0 / dots[0]
        for k in range(j + 1, COLS):
            alpha = dots[k - j] * recip
            for part in range(len(cols[j])):
                cols[k][part] = cols[k][part] - alpha * cols[j][part]
    return R


def inverse(R):
    T = {}
    recip = [1.0 / R[j, j] for j in range(COLS)]
    for j in range(COLS):
        T[j, j] = recip[j]
        for i in range(j):
            s = T[i, i] * R[i, j]
            for k in range(i + 1, j):
                s = s + T[i, k] * R[k, j]
            T[i, j] = -s * recip[j]
    return T


def least_squares(R):
    n = RHS * S
    cols = []
    for c in range(n):
        col = []
        for i in range(c + RHS + 1):
            minus = R[i, c + RHS]
            col.append(R[i, c] - minus if i <= c else -minus)
        cols.append(col)
    upper, target = {}, {}
    recips = []

    def dot(a, b):
        terms = [x * y for x, y in zip(a, b)]
        while len(terms) > 1:
            terms = [x + y for x, y in zip(terms[::2], terms[1::2])] + (
                [terms[-1]] if len(terms) % 2 else []
            )
        return terms[0]

    for j in range(n):
        inv = 1.0 / jnp.sqrt(dot(cols[j], cols[j]))
        recips.append(inv)
        q = [v * inv for v in cols[j]]
        for c in range(j + 1, n):
            w = dot(q, cols[c])
            upper[j, c] = w
            for i in range(len(q)):
                cols[c][i] = cols[c][i] - w * q[i]
        for e in range(RHS):
            target[j, e] = dot(q, [R[i, e] for i in range(e + 1)])
    coef = {}
    for e in range(RHS):
        for j in reversed(range(n)):
            value = target[j, e]
            for later in range(j + 1, n):
                value = value - upper[j, later] * coef[later, e]
            coef[j, e] = value * recips[j]
    return coef


def final_kernel(
    X, Y, scale, gathered, V, V4, ortho, triangle, update, O, W, out_sems
):
    R = merged_factor(gathered[...])
    row = lax.broadcasted_iota(jnp.int32, (16, 128), 0)
    lane = lax.broadcasted_iota(jnp.int32, (16, 128), 1)
    tri = jnp.zeros((16, 128), F32)
    for (i, j), value in R.items():
        tri = jnp.where((row == i) & (lane == j), value * (1.0 / scale), tri)
    triangle[...] = tri[:COLS, :COLS]
    T = inverse(R)
    weights = {}
    for n, ((i, j), value) in enumerate(T.items()):
        weights[i, j] = n
        W[n] = jnp.broadcast_to(value * scale, (8, 128))
    coef = least_squares(R)
    base = len(weights)
    for n, ((k, e), value) in enumerate(coef.items()):
        weights[k, COLS + e] = base + n
        W[base + n] = jnp.broadcast_to(value, (8, 128))

    CH = 32
    XB = 2
    outs = []
    for block in range(X // XB):

        def rows(i, carry, block=block):
            x = block * XB + i
            for at in range(0, Y, CH):
                b = [basis_rows(V, V4, k, x, at, CH) for k in range(COLS)]
                for j in range(COLS + RHS):
                    value = None
                    for k in range(j + 1 if j < COLS else RHS * S):
                        w = jnp.concatenate([W[weights[k, j]]] * (CH // 8), axis=0)
                        value = w * b[k] if value is None else value + w * b[k]
                    O[j, x, pl.ds(at, CH), :] = value
            return carry

        lax.fori_loop(0, XB, rows, 0)
        here = pl.ds(block * XB, XB)
        for copy in (
            pltpu.make_async_copy(
                O.at[pl.ds(0, COLS), here], ortho.at[:, here], out_sems.at[2 * block]
            ),
            pltpu.make_async_copy(
                O.at[pl.ds(COLS, RHS), here], update.at[:, here], out_sems.at[2 * block + 1]
            ),
        ):
            copy.start()
            outs.append(copy)
    for copy in outs:
        copy.wait()


ANY = pl.BlockSpec(memory_space=pl.ANY)
VMEM = pl.BlockSpec(memory_space=pltpu.VMEM)
MIB = 1024 * 1024
PIN, BLOCK, FAR = range(3)


def call(kernel, name, inputs, outputs, scratch=(), aliases={}, limit=4):
    pin = lambda a: pltpu.with_memory_space_constraint(a, pltpu.VMEM)
    spec = lambda place: ANY if place == FAR else VMEM
    return pl.pallas_call(
        kernel,
        out_shape=tuple(
            pltpu.VMEM(o, F32) if place == PIN else jax.ShapeDtypeStruct(o, F32)
            for o, place in outputs
        ),
        in_specs=[spec(place) for _, place in inputs],
        out_specs=tuple(spec(place) for _, place in outputs),
        scratch_shapes=list(scratch),
        input_output_aliases=aliases,
        compiler_params=pltpu.CompilerParams(vmem_limit_bytes=limit * MIB),
        name=name,
    )(*(pin(a) if place == PIN else a for a, place in inputs))


def body(right_sides, diagonal, velocity):
    _, X, Y, Z = right_sides.shape
    nx, ny = lax.axis_size("gx"), lax.axis_size("gy")
    devices = nx * ny
    scale = math.sqrt(X * Y * Z * devices)
    XE, YE = X + 8, Y + 2 * YP
    inputs = [
        (pltpu.with_memory_space_constraint(a, pltpu.HBM), FAR)
        for a in (right_sides, velocity, diagonal)
    ]
    dma = pltpu.SemaphoreType.DMA

    def swap(value, axis, pairing):
        size = lax.axis_size(axis)
        pairs = [(i, i + 1) for i in range(pairing, size - 1, 2)]
        return lax.ppermute(value, axis, pairs + [(j, i) for i, j in pairs])

    v_shape, u_shape = ((S, RHS, XE, YE, Z), PIN), ((4, XE, YE, Z), PIN)
    x_slab, y_slab = ((20, Y, Z), PIN), ((24 * X, Z), PIN)
    x0, x1, y0, y1, V, U = call(
        functools.partial(pack_kernel, X, Y),
        "pack",
        inputs,
        [x_slab, x_slab, y_slab, y_slab, v_shape, u_shape],
        [dma((3,))],
    )
    x0, x1 = swap(x0, "gx", 0), swap(x1, "gx", 1)
    y1, y0 = swap(y1, "gy", 1), swap(y0, "gy", 0)
    v4_shape, a_shape = ((RHS, X, Y, Z), PIN), ((6, XE, YE, Z), PIN)
    work = pltpu.VMEM((COLS - 1, X, Y, Z), F32)
    factor_shape = ((16, Z), PIN)
    V, V4, A, factor = call(
        functools.partial(inner_kernel, X, Y),
        "inner",
        [(V, PIN), (U, PIN)],
        [v_shape, v4_shape, a_shape, factor_shape],
        [work],
        aliases={0: 0},
        limit=8,
    )
    strip = ((2 * CORNER_ROWS, Z), PIN)
    V, U, c0, c1 = call(
        functools.partial(place_y_kernel, X, Y),
        "place_y",
        [(y0, PIN), (y1, PIN), (V, PIN), (U, PIN)],
        [v_shape, u_shape, strip, strip],
        aliases={2: 0, 3: 1},
    )
    c0, c1 = swap(c0, "gx", 0), swap(c1, "gx", 1)
    V, V4, A = call(
        functools.partial(edge_kernel, X, Y),
        "edge",
        [(a, PIN) for a in (U, V, V4, A)],
        [v_shape, v4_shape, a_shape],
        aliases={1: 0, 2: 1, 3: 2},
    )
    state = [v_shape, v4_shape, a_shape, u_shape]
    V, V4, A, U, factor = call(
        functools.partial(face_kernel, X, Y),
        "face",
        [(a, PIN) for a in (x0, x1, factor, V, V4, A, U)],
        state + [factor_shape],
        [work],
        aliases={3: 0, 4: 1, 5: 2, 6: 3},
        limit=8,
    )
    V, V4, A, U, packed = call(
        functools.partial(corner_kernel, X, Y),
        "corner",
        [(a, PIN) for a in (c0, c1, factor, V, V4, A, U)],
        state + [((devices, 128), BLOCK)],
        [work],
        aliases={3: 0, 4: 1, 5: 2, 6: 3},
        limit=8,
    )
    gathered = lax.all_to_all(packed, ("gx", "gy"), 0, 0, tiled=True)
    out = [((COLS, X, Y, Z), FAR), ((COLS, COLS), BLOCK), ((RHS, X, Y, Z), FAR)]
    ortho, triangle, update = call(
        functools.partial(final_kernel, X, Y, scale),
        "combine",
        [(gathered, BLOCK), (V, PIN), (V4, PIN)],
        out,
        [
            pltpu.VMEM((COLS + RHS, X, Y, Z), F32),
            pltpu.VMEM((71, 8, 128), F32),
            dma((X,)),
        ],
        limit=10,
    )
    return ortho, triangle, update


def solution(mesh):
    return jax.shard_map(
        body,
        mesh=mesh,
        in_specs=(P(None, "gx", "gy", None), P("gx", "gy", None), P(None, "gx", "gy", None)),
        out_specs=(P(None, "gx", "gy", None), P(), P(None, "gx", "gy", None)),
        check_vma=False,
    )
```

```python
import functools
import math

import jax
import jax.numpy as jnp
from jax import lax
from jax.experimental import pallas as pl
from jax.experimental.pallas import tpu as pltpu
from jax.sharding import PartitionSpec as P

S = 4
RHS = 2
COLS = 10
UNROLL = 4
YP = 16

F32 = jnp.float32
FIELD_CORNER = [(dx, dy) for dx in (1, 2, 3) for dy in (1, 2, 3) if dx + dy <= 4]
COEF_CORNER = [(dx, dy) for dx in (1, 2) for dy in (1, 2) if dx + dy <= 3]
CORNER_ROWS = RHS * len(FIELD_CORNER) + 4 * len(COEF_CORNER)


def slot(i, k):
    return (8 * k if k < 8 else 64 + 16 * (k - 8)) + i


def toward_high(axis, pairing):
    return lax.axis_index(axis) % 2 == pairing


def pack_kernel(X, Y, rhs, vel, diag, x0, x1, y0, y1, V, U, sems):
    own_x, own_y = pl.ds(4, X), pl.ds(YP, Y)
    copies = [
        (rhs, V.at[0, :, own_x, own_y]),
        (vel, U.at[pl.ds(0, 3), own_x, own_y]),
        (diag, U.at[3, own_x, own_y]),
    ]
    copies = [pltpu.make_async_copy(s, d, sems.at[i]) for i, (s, d) in enumerate(copies)]
    for copy in copies:
        copy.start()
    for copy in copies:
        copy.wait()
    for pairing, out in enumerate((x0, x1)):
        high = toward_high("gx", pairing)
        at3, at2 = jnp.where(high, X + 1, 4), jnp.where(high, X + 2, 4)
        for i in range(3):
            for f in range(RHS):
                out[3 * f + i] = V[0, f, at3 + i, YP : YP + Y, :]
        for i in range(2):
            for c in range(4):
                out[6 + 2 * c + i] = U[c, at2 + i, YP : YP + Y, :]
    first_high = toward_high("gy", 0)
    for f in range(6):
        for x in range(X):
            field = V.at[0, f, 4 + x] if f < 2 else U.at[f - 2, 4 + x]
            low, high = field[YP : YP + 4, :], field[YP + Y - 4 : YP + Y, :]
            at = 4 * (f * X + x)
            y0[at : at + 4, :] = jnp.where(first_high, high, low)
            y1[at : at + 4, :] = jnp.where(first_high, low, high)


def corner_cells(X, Y, high, own):
    cells = []
    for y_low in (True, False):
        for f in range(6):
            for dx, dy in FIELD_CORNER if f < 2 else COEF_CORNER:
                if own:
                    x = jnp.where(high, X + 4 - dx, 3 + dx)
                else:
                    x = jnp.where(high, X + 3 + dx, 4 - dx)
                cells.append((f, x, YP - dy if y_low else YP + Y - 1 + dy))
    return cells


def place_y_kernel(X, Y, y0, y1, A, V_in, U_in, V, U, first, second):
    first_high = toward_high("gy", 0)
    for f in range(6):
        for x in range(X):
            at = 4 * (f * X + x)
            a, b = y0[at : at + 4, :], y1[at : at + 4, :]
            field = V.at[0, f, 4 + x] if f < 2 else U.at[f - 2, 4 + x]
            field[YP - 4 : YP, :] = jnp.where(first_high, b, a)
            field[YP + Y : YP + Y + 4, :] = jnp.where(first_high, a, b)
    power_rows(V, None, A, 1, [(6, 7), (X + 1, X + 2)], [(YP, 8), (YP + Y - 8, 8)], 1)
    for pairing, out in enumerate((first, second)):
        high = toward_high("gx", pairing)
        for f in range(RHS):
            out[f * Y : (f + 1) * Y, :] = V[1, f, jnp.where(high, X + 1, 6), YP : YP + Y, :]
        for row, (f, x, y) in enumerate(corner_cells(X, Y, high, True)):
            out[RHS * Y + row : RHS * Y + row + 1, :] = (
                V[0, f, x, y : y + 1, :] if f < 2 else U[f - 2, x, y : y + 1, :]
            )


def total(x):
    return jnp.sum(jnp.sum(x, axis=0, keepdims=True), axis=1, keepdims=True)


def fold8(x):
    rows = x.shape[0]
    parts = [x[8 * i : 8 * i + 8] for i in range(rows // 8)]
    while len(parts) > 1:
        parts = [a + b for a, b in zip(parts[::2], parts[1::2])] + (
            [parts[-1]] if len(parts) % 2 else []
        )
    return parts[0]


def coefficient_rows(X, Y, U, A, rows, begin, size):
    gx, gy = lax.axis_index("gx"), lax.axis_index("gy")
    nx, ny = lax.axis_size("gx"), lax.axis_size("gy")
    here = pl.ds(begin, size)
    yi = begin + lax.broadcasted_iota(jnp.int32, (size, 128), 0)
    zi = lax.broadcasted_iota(jnp.int32, (size, 128), 1)
    y_in = ((yi >= YP) | (gy > 0)) & ((yi < Y + YP) | (gy < ny - 1))

    def one(x):
        x_in = ((x >= 4) | (gx > 0)) & ((x < X + 4) | (gx < nx - 1))
        g = jnp.where(y_in & x_in, 1.0 / (6.0 + U[3, x, here, :]), 0.0)
        for c in range(3):
            ug = U[c, x, here, :] * g
            plus, minus = g + ug, g - ug
            if c == 2:
                plus = jnp.where(zi == 0, 0.0, plus)
                minus = jnp.where(zi == 127, 0.0, minus)
            A[2 * c, x, here, :] = plus
            A[2 * c + 1, x, here, :] = minus

    for_rows(rows, one, 2)


def for_rows(rows, body, unroll):
    def run(i, carry):
        for first, last in rows:
            body(first + i)
        return carry

    lax.fori_loop(0, rows[0][1] - rows[0][0], run, 0, unroll=unroll)


def power_rows(V, V4, A, k, rows, pieces, unroll):
    def one(x):
        for begin, size in pieces:
            here = pl.ds(begin, size)
            a = [A[c, x, here, :] for c in range(6)]
            for f in range(RHS):
                centre = V[k - 1, f, x, here, :]
                value = a[4] * pltpu.roll(centre, 1, 1) + a[5] * pltpu.roll(centre, 127, 1)
                value += a[0] * V[k - 1, f, x - 1, here, :] + a[1] * V[k - 1, f, x + 1, here, :]
                value += a[2] * V[k - 1, f, x, pl.ds(begin - 1, size), :]
                value += a[3] * V[k - 1, f, x, pl.ds(begin + 1, size), :]
                if k == S:
                    V4[f, x - 4, pl.ds(begin - YP, size), :] = value
                else:
                    V[k, f, x, here, :] = value

    for_rows(rows, one, unroll)


def basis_rows(V, V4, k, x, at, size):
    if k >= RHS * S:
        return V4[k - RHS * S, x, pl.ds(at, size), :]
    return V[k // RHS, k % RHS, x + 4, pl.ds(YP + at, size), :]


def local_factor(V, V4, Q, groups, before=None, packed=False):
    def over_groups(body, accs):
        for count, pieces in groups:
            run = functools.partial(body, pieces)
            accs = lax.fori_loop(0, count, run, accs, unroll=min(count, UNROLL))
        return accs

    zero = jnp.zeros((8, 128), F32)
    top = [zero] * COLS
    if before is not None:
        first_row = lax.broadcasted_iota(jnp.int32, (8, 128), 0) == 0
        top = [jnp.where(first_row, before[k : k + 1, :], 0.0) for k in range(COLS)]

    def first_dots(pieces, i, accs):
        accs = list(accs)
        for row, at, size in pieces:
            x = row + i
            q = basis_rows(V, V4, 0, x, at, size)
            for k in range(COLS):
                accs[k] = accs[k] + fold8(q * basis_rows(V, V4, k, x, at, size))
        return tuple(accs)

    start = tuple(top[0] * t for t in top)
    accs = over_groups(first_dots, start)
    lane = lax.broadcasted_iota(jnp.int32, (1, 128), 1)
    lines = [jnp.zeros((1, 128), F32)] * (1 if packed else COLS)
    for j in range(COLS):
        dots = [total(a) for a in accs]
        live = dots[0] >= 1e-37
        length = jnp.sqrt(jnp.where(live, dots[0], 1.0))
        inv = jnp.where(live, 1.0 / length, 0.0)
        for k in range(j, COLS):
            line, at = (0, slot(j, k)) if packed else (k, j)
            lines[line] = jnp.where(lane == at, dots[k - j] * inv, lines[line])
        if j == COLS - 1:
            return lines
        recip = 1.0 / jnp.where(live, dots[0], 1.0)
        alphas = [jnp.broadcast_to(d * recip, (8, 128)) for d in dots[1:]]
        for k in range(j + 1, COLS):
            top[k] = top[k] - alphas[k - j - 1] * top[j]

        def get(k, x, at, size, j=j):
            if j == 0 or k == 0:
                return basis_rows(V, V4, k, x, at, size)
            return Q[k - 1, x, pl.ds(at, size), :]

        def sweep(pieces, i, accs, j=j, get=get, alphas=alphas):
            accs = list(accs)
            for row, at, size in pieces:
                x = row + i
                q = get(j, x, at, size)
                after = None
                for k in range(j + 1, COLS):
                    alpha = jnp.concatenate([alphas[k - j - 1]] * (size // 8), axis=0)
                    value = get(k, x, at, size) - alpha * q
                    Q[k - 1, x, pl.ds(at, size), :] = value
                    if k == j + 1:
                        after = value
                    accs[k - j - 1] = accs[k - j - 1] + fold8(after * value)
            return tuple(accs)

        start = tuple(top[j + 1] * t for t in top[j + 1 :])
        accs = over_groups(sweep, start)


def store_factor(out, lines):
    for k, line in enumerate(lines):
        out[k : k + 1, :] = line


def inner_kernel(X, Y, V_in, U, V, V4, A, factor, Q):
    coefficient_rows(X, Y, U, A, [(4, X + 4)], YP, Y)
    for k in range(1, S + 1):
        power_rows(V, V4, A, k, [(4 + k, X + 4 - k)], [(YP, Y)], 4)
    half = (Y - 16) // 2
    pieces = [(row, at, half) for row in (4, X // 2) for at in (8, 8 + half)]
    store_factor(factor, local_factor(V, V4, Q, [(X // 2 - 4, pieces)]))


def beside_y(Y, k):
    if k == S:
        return [(YP, 8), (YP + Y - 8, 8)]
    return [(YP - 8, 16), (YP + Y - 8, 16)]


def edge_kernel(X, Y, U, V_in, V4_in, A_in, V, V4, A):
    for begin in (YP - 8, YP + Y):
        coefficient_rows(X, Y, U, A, [(4, X + 4)], begin, 8)
    for k in range(1, S + 1):
        power_rows(V, V4, A, k, [(4 + k, X + 4 - k)], beside_y(Y, k), 7)


def near_x(X, k):
    return [(k + 1, k + 4), (X + 4 - k, X + 7 - k)]


def nearest_x(X, k):
    return [(k, k + 1), (X + 7 - k, X + 8 - k)]


def face_kernel(X, Y, x0, x1, before, V_in, V4_in, A_in, U_in, V, V4, A, U, factor, Q):
    for pairing, got in enumerate((x0, x1)):
        high = toward_high("gx", pairing)
        at3, at2 = jnp.where(high, X + 4, 1), jnp.where(high, X + 4, 2)
        for i in range(3):
            for f in range(RHS):
                V[0, f, at3 + i, YP : YP + Y, :] = got[3 * f + i]
        for i in range(2):
            for c in range(4):
                U[c, at2 + i, YP : YP + Y, :] = got[6 + 2 * c + i]
    coefficient_rows(X, Y, U, A, [(2, 4), (X + 4, X + 6)], YP, Y)
    for k in range(1, S + 1):
        power_rows(V, V4, A, k, near_x(X, k), [(YP, Y)], 3)
    half = (Y - 16) // 2
    faces = [(row, at, half) for row in (1, X - 4) for at in (8, 8 + half)]
    sides = [(row, at, 8) for row in (4, X // 2) for at in (0, Y - 8)]
    groups = [(3, faces), (X // 2 - 4, sides)]
    store_factor(factor, local_factor(V, V4, Q, groups, before))


def corner_kernel(X, Y, c0, c1, before, V_in, V4_in, A_in, U_in, V, V4, A, U, packed, Q):
    for pairing, got in enumerate((c0, c1)):
        high = toward_high("gx", pairing)
        for f in range(RHS):
            V[1, f, jnp.where(high, X + 6, 1), YP : YP + Y, :] = got[f * Y : (f + 1) * Y, :]
        for row, (f, x, y) in enumerate(corner_cells(X, Y, high, False)):
            value = got[RHS * Y + row : RHS * Y + row + 1, :]
            if f < 2:
                V[0, f, x, y : y + 1, :] = value
            else:
                U[f - 2, x, y : y + 1, :] = value
    for begin in (YP - 8, YP + Y):
        coefficient_rows(X, Y, U, A, [(2, 4), (X + 4, X + 6)], begin, 8)
    for k in range(1, S + 1):
        power_rows(V, V4, A, k, near_x(X, k), beside_y(Y, k), 3)
        if k > 1:
            power_rows(V, V4, A, k, nearest_x(X, k), [(YP, Y)], 1)
    ends = [(row, at, Y // 2) for row in (0, X - 1) for at in (0, Y // 2)]
    sides = [(row, at, 8) for row in (1, X - 4) for at in (0, Y - 8)]
    (line,) = local_factor(V, V4, Q, [(1, ends), (3, sides)], before, packed=True)
    packed[...] = jnp.broadcast_to(line, packed.shape)


def fold_lanes(x):
    parts = [x[:, i : i + 128] for i in range(0, x.shape[1], 128)]
    return functools.reduce(lambda a, b: a + b, parts)


def merged_factor(gathered):
    g = gathered.T
    cols = []
    for k in range(COLS):
        at = slot(0, k)
        cols.append([g[i : i + 8] for i in range(at, at + k + 1, 8)])
    R = {}
    for j in range(COLS):
        dots = []
        for k in range(j, COLS):
            p = fold_lanes(cols[j][0] * cols[k][0])
            if j >= 8:
                p = p + fold_lanes(cols[j][1] * cols[k][1])
            dots.append(total(p))
        inv = 1.0 / jnp.sqrt(dots[0])
        for k in range(j, COLS):
            R[j, k] = dots[k - j] * inv
        recip = 1.0 / dots[0]
        for k in range(j + 1, COLS):
            alpha = dots[k - j] * recip
            for part in range(len(cols[j])):
                cols[k][part] = cols[k][part] - alpha * cols[j][part]
    return R


def inverse(R):
    T = {}
    recip = [1.0 / R[j, j] for j in range(COLS)]
    for j in range(COLS):
        T[j, j] = recip[j]
        for i in range(j):
            s = T[i, i] * R[i, j]
            for k in range(i + 1, j):
                s = s + T[i, k] * R[k, j]
            T[i, j] = -s * recip[j]
    return T


def least_squares(R):
    n = RHS * S
    cols = []
    for c in range(n):
        col = []
        for i in range(c + RHS + 1):
            minus = R[i, c + RHS]
            col.append(R[i, c] - minus if i <= c else -minus)
        cols.append(col)
    upper, target = {}, {}
    recips = []

    def dot(a, b):
        terms = [x * y for x, y in zip(a, b)]
        while len(terms) > 1:
            terms = [x + y for x, y in zip(terms[::2], terms[1::2])] + (
                [terms[-1]] if len(terms) % 2 else []
            )
        return terms[0]

    for j in range(n):
        inv = 1.0 / jnp.sqrt(dot(cols[j], cols[j]))
        recips.append(inv)
        q = [v * inv for v in cols[j]]
        for c in range(j + 1, n):
            w = dot(q, cols[c])
            upper[j, c] = w
            for i in range(len(q)):
                cols[c][i] = cols[c][i] - w * q[i]
        for e in range(RHS):
            target[j, e] = dot(q, [R[i, e] for i in range(e + 1)])
    coef = {}
    for e in range(RHS):
        for j in reversed(range(n)):
            value = target[j, e]
            for later in range(j + 1, n):
                value = value - upper[j, later] * coef[later, e]
            coef[j, e] = value * recips[j]
    return coef


def final_kernel(
    X, Y, scale, gathered, V, V4, ortho, triangle, update, O, W, out_sems
):
    R = merged_factor(gathered[...])
    row = lax.broadcasted_iota(jnp.int32, (16, 128), 0)
    lane = lax.broadcasted_iota(jnp.int32, (16, 128), 1)
    tri = jnp.zeros((16, 128), F32)
    for (i, j), value in R.items():
        tri = jnp.where((row == i) & (lane == j), value * (1.0 / scale), tri)
    triangle[...] = tri[:COLS, :COLS]
    T = inverse(R)
    weights = {}
    for n, ((i, j), value) in enumerate(T.items()):
        weights[i, j] = n
        W[n] = jnp.broadcast_to(value * scale, (8, 128))
    coef = least_squares(R)
    base = len(weights)
    for n, ((k, e), value) in enumerate(coef.items()):
        weights[k, COLS + e] = base + n
        W[base + n] = jnp.broadcast_to(value, (8, 128))

    CH = 32
    XB = 2
    outs = []
    for block in range(X // XB):

        def rows(i, carry, block=block):
            x = block * XB + i
            for at in range(0, Y, CH):
                b = [basis_rows(V, V4, k, x, at, CH) for k in range(COLS)]
                for j in range(COLS + RHS):
                    value = None
                    for k in range(j + 1 if j < COLS else RHS * S):
                        w = jnp.concatenate([W[weights[k, j]]] * (CH // 8), axis=0)
                        value = w * b[k] if value is None else value + w * b[k]
                    O[j, x, pl.ds(at, CH), :] = value
            return carry

        lax.fori_loop(0, XB, rows, 0)
        here = pl.ds(block * XB, XB)
        for copy in (
            pltpu.make_async_copy(
                O.at[pl.ds(0, COLS), here], ortho.at[:, here], out_sems.at[2 * block]
            ),
            pltpu.make_async_copy(
                O.at[pl.ds(COLS, RHS), here], update.at[:, here], out_sems.at[2 * block + 1]
            ),
        ):
            copy.start()
            outs.append(copy)
    for copy in outs:
        copy.wait()


ANY = pl.BlockSpec(memory_space=pl.ANY)
VMEM = pl.BlockSpec(memory_space=pltpu.VMEM)
MIB = 1024 * 1024
PIN, BLOCK, FAR = range(3)


def call(kernel, name, inputs, outputs, scratch=(), aliases={}, limit=4):
    pin = lambda a: pltpu.with_memory_space_constraint(a, pltpu.VMEM)
    spec = lambda place: ANY if place == FAR else VMEM
    return pl.pallas_call(
        kernel,
        out_shape=tuple(
            pltpu.VMEM(o, F32) if place == PIN else jax.ShapeDtypeStruct(o, F32)
            for o, place in outputs
        ),
        in_specs=[spec(place) for _, place in inputs],
        out_specs=tuple(spec(place) for _, place in outputs),
        scratch_shapes=list(scratch),
        input_output_aliases=aliases,
        compiler_params=pltpu.CompilerParams(vmem_limit_bytes=limit * MIB),
        name=name,
    )(*(pin(a) if place == PIN else a for a, place in inputs))


def body(right_sides, diagonal, velocity):
    _, X, Y, Z = right_sides.shape
    nx, ny = lax.axis_size("gx"), lax.axis_size("gy")
    devices = nx * ny
    scale = math.sqrt(X * Y * Z * devices)
    XE, YE = X + 8, Y + 2 * YP
    inputs = [
        (pltpu.with_memory_space_constraint(a, pltpu.HBM), FAR)
        for a in (right_sides, velocity, diagonal)
    ]
    dma = pltpu.SemaphoreType.DMA

    def swap(value, axis, pairing):
        size = lax.axis_size(axis)
        pairs = [(i, i + 1) for i in range(pairing, size - 1, 2)]
        return lax.ppermute(value, axis, pairs + [(j, i) for i, j in pairs])

    v_shape, u_shape = ((S, RHS, XE, YE, Z), PIN), ((4, XE, YE, Z), PIN)
    x_slab, y_slab = ((14, Y, Z), PIN), ((24 * X, Z), PIN)
    x0, x1, y0, y1, V, U = call(
        functools.partial(pack_kernel, X, Y),
        "pack",
        inputs,
        [x_slab, x_slab, y_slab, y_slab, v_shape, u_shape],
        [dma((3,))],
    )
    x0, x1 = swap(x0, "gx", 0), swap(x1, "gx", 1)
    y1, y0 = swap(y1, "gy", 1), swap(y0, "gy", 0)
    v4_shape, a_shape = ((RHS, X, Y, Z), PIN), ((6, XE, YE, Z), PIN)
    work = pltpu.VMEM((COLS - 1, X, Y, Z), F32)
    factor_shape = ((16, Z), PIN)
    V, V4, A, factor = call(
        functools.partial(inner_kernel, X, Y),
        "inner",
        [(V, PIN), (U, PIN)],
        [v_shape, v4_shape, a_shape, factor_shape],
        [work],
        aliases={0: 0},
        limit=8,
    )
    strip = ((RHS * Y + 2 * CORNER_ROWS, Z), PIN)
    V, U, c0, c1 = call(
        functools.partial(place_y_kernel, X, Y),
        "place_y",
        [(a, PIN) for a in (y0, y1, A, V, U)],
        [v_shape, u_shape, strip, strip],
        aliases={3: 0, 4: 1},
    )
    c0, c1 = swap(c0, "gx", 0), swap(c1, "gx", 1)
    V, V4, A = call(
        functools.partial(edge_kernel, X, Y),
        "edge",
        [(a, PIN) for a in (U, V, V4, A)],
        [v_shape, v4_shape, a_shape],
        aliases={1: 0, 2: 1, 3: 2},
    )
    state = [v_shape, v4_shape, a_shape, u_shape]
    V, V4, A, U, factor = call(
        functools.partial(face_kernel, X, Y),
        "face",
        [(a, PIN) for a in (x0, x1, factor, V, V4, A, U)],
        state + [factor_shape],
        [work],
        aliases={3: 0, 4: 1, 5: 2, 6: 3},
        limit=8,
    )
    V, V4, A, U, packed = call(
        functools.partial(corner_kernel, X, Y),
        "corner",
        [(a, PIN) for a in (c0, c1, factor, V, V4, A, U)],
        state + [((devices, 128), BLOCK)],
        [work],
        aliases={3: 0, 4: 1, 5: 2, 6: 3},
        limit=8,
    )
    gathered = lax.all_to_all(packed, ("gx", "gy"), 0, 0, tiled=True)
    out = [((COLS, X, Y, Z), FAR), ((COLS, COLS), BLOCK), ((RHS, X, Y, Z), FAR)]
    ortho, triangle, update = call(
        functools.partial(final_kernel, X, Y, scale),
        "combine",
        [(gathered, BLOCK), (V, PIN), (V4, PIN)],
        out,
        [
            pltpu.VMEM((COLS + RHS, X, Y, Z), F32),
            pltpu.VMEM((71, 8, 128), F32),
            dma((X,)),
        ],
        limit=10,
    )
    return ortho, triangle, update


def solution(mesh):
    return jax.shard_map(
        body,
        mesh=mesh,
        in_specs=(P(None, "gx", "gy", None), P("gx", "gy", None), P(None, "gx", "gy", None)),
        out_specs=(P(None, "gx", "gy", None), P(), P(None, "gx", "gy", None)),
        check_vma=False,
    )
```

```python
import functools
import math

import jax
import jax.numpy as jnp
from jax import lax
from jax.experimental import pallas as pl
from jax.experimental.pallas import tpu as pltpu
from jax.sharding import PartitionSpec as P

S = 4
RHS = 2
COLS = 10
UNROLL = 4
YP = 16

F32 = jnp.float32
FIELD_CORNER = [(dx, dy) for dx in (1, 2, 3) for dy in (1, 2, 3) if dx + dy <= 4]
COEF_CORNER = [(dx, dy) for dx in (1, 2) for dy in (1, 2) if dx + dy <= 3]
CORNER_ROWS = RHS * len(FIELD_CORNER) + 4 * len(COEF_CORNER)


def slot(i, k):
    return (8 * k if k < 8 else 64 + 16 * (k - 8)) + i


def toward_high(axis, pairing):
    return lax.axis_index(axis) % 2 == pairing


def within(axis, pairing, value):
    if pairing == 0:
        return value
    i = lax.axis_index(axis)
    return jnp.where((i == 0) | (i == lax.axis_size(axis) - 1), 0.0, value)


def pack_kernel(X, Y, rhs, vel, diag, x0, x1, y0, y1, V, U, sems):
    own_x, own_y = pl.ds(4, X), pl.ds(YP, Y)
    copies = [
        (rhs, V.at[0, :, own_x, own_y]),
        (vel, U.at[pl.ds(0, 3), own_x, own_y]),
        (diag, U.at[3, own_x, own_y]),
    ]
    copies = [pltpu.make_async_copy(s, d, sems.at[i]) for i, (s, d) in enumerate(copies)]
    for copy in copies:
        copy.start()
    for copy in copies:
        copy.wait()
    for pairing, out in enumerate((x0, x1)):
        high = toward_high("gx", pairing)
        at3, at2 = jnp.where(high, X + 1, 4), jnp.where(high, X + 2, 4)
        for i in range(3):
            for f in range(RHS):
                out[3 * f + i] = V[0, f, at3 + i, YP : YP + Y, :]
        for i in range(2):
            for c in range(4):
                out[6 + 2 * c + i] = U[c, at2 + i, YP : YP + Y, :]
    first_high = toward_high("gy", 0)
    for f in range(6):
        for x in range(X):
            field = V.at[0, f, 4 + x] if f < 2 else U.at[f - 2, 4 + x]
            low, high = field[YP : YP + 4, :], field[YP + Y - 4 : YP + Y, :]
            at = 4 * (f * X + x)
            y0[at : at + 4, :] = jnp.where(first_high, high, low)
            y1[at : at + 4, :] = jnp.where(first_high, low, high)


def corner_cells(X, Y, high, own):
    cells = []
    for y_low in (True, False):
        for f in range(6):
            for dx, dy in FIELD_CORNER if f < 2 else COEF_CORNER:
                if own:
                    x = jnp.where(high, X + 4 - dx, 3 + dx)
                else:
                    x = jnp.where(high, X + 3 + dx, 4 - dx)
                cells.append((f, x, YP - dy if y_low else YP + Y - 1 + dy))
    return cells


def place_y_kernel(X, Y, y0, y1, A, V_in, U_in, V, U, first, second):
    first_high = toward_high("gy", 0)
    for f in range(6):
        for x in range(X):
            at = 4 * (f * X + x)
            a, b = y0[at : at + 4, :], within("gy", 1, y1[at : at + 4, :])
            field = V.at[0, f, 4 + x] if f < 2 else U.at[f - 2, 4 + x]
            field[YP - 4 : YP, :] = jnp.where(first_high, b, a)
            field[YP + Y : YP + Y + 4, :] = jnp.where(first_high, a, b)
    power_rows(V, None, A, 1, [(6, 7), (X + 1, X + 2)], [(YP, 8), (YP + Y - 8, 8)], 1)
    for pairing, out in enumerate((first, second)):
        high = toward_high("gx", pairing)
        for f in range(RHS):
            out[f * Y : (f + 1) * Y, :] = V[1, f, jnp.where(high, X + 1, 6), YP : YP + Y, :]
        for row, (f, x, y) in enumerate(corner_cells(X, Y, high, True)):
            out[RHS * Y + row : RHS * Y + row + 1, :] = (
                V[0, f, x, y : y + 1, :] if f < 2 else U[f - 2, x, y : y + 1, :]
            )


def total(x):
    return jnp.sum(jnp.sum(x, axis=0, keepdims=True), axis=1, keepdims=True)


def fold8(x):
    rows = x.shape[0]
    parts = [x[8 * i : 8 * i + 8] for i in range(rows // 8)]
    while len(parts) > 1:
        parts = [a + b for a, b in zip(parts[::2], parts[1::2])] + (
            [parts[-1]] if len(parts) % 2 else []
        )
    return parts[0]


def coefficient_rows(X, Y, U, A, rows, begin, size):
    gx, gy = lax.axis_index("gx"), lax.axis_index("gy")
    nx, ny = lax.axis_size("gx"), lax.axis_size("gy")
    here = pl.ds(begin, size)
    yi = begin + lax.broadcasted_iota(jnp.int32, (size, 128), 0)
    zi = lax.broadcasted_iota(jnp.int32, (size, 128), 1)
    y_in = ((yi >= YP) | (gy > 0)) & ((yi < Y + YP) | (gy < ny - 1))

    def one(x):
        x_in = ((x >= 4) | (gx > 0)) & ((x < X + 4) | (gx < nx - 1))
        g = jnp.where(y_in & x_in, 1.0 / (6.0 + U[3, x, here, :]), 0.0)
        for c in range(3):
            ug = U[c, x, here, :] * g
            plus, minus = g + ug, g - ug
            if c == 2:
                plus = jnp.where(zi == 0, 0.0, plus)
                minus = jnp.where(zi == 127, 0.0, minus)
            A[2 * c, x, here, :] = plus
            A[2 * c + 1, x, here, :] = minus

    for_rows(rows, one, 2)


def for_rows(rows, body, unroll):
    def run(i, carry):
        for first, last in rows:
            body(first + i)
        return carry

    lax.fori_loop(0, rows[0][1] - rows[0][0], run, 0, unroll=unroll)


def power_rows(V, V4, A, k, rows, pieces, unroll):
    def one(x):
        for begin, size in pieces:
            here = pl.ds(begin, size)
            a = [A[c, x, here, :] for c in range(6)]
            for f in range(RHS):
                centre = V[k - 1, f, x, here, :]
                value = a[4] * pltpu.roll(centre, 1, 1) + a[5] * pltpu.roll(centre, 127, 1)
                value += a[0] * V[k - 1, f, x - 1, here, :] + a[1] * V[k - 1, f, x + 1, here, :]
                value += a[2] * V[k - 1, f, x, pl.ds(begin - 1, size), :]
                value += a[3] * V[k - 1, f, x, pl.ds(begin + 1, size), :]
                if k == S:
                    V4[f, x - 4, pl.ds(begin - YP, size), :] = value
                else:
                    V[k, f, x, here, :] = value

    for_rows(rows, one, unroll)


def basis_rows(V, V4, k, x, at, size):
    if k >= RHS * S:
        return V4[k - RHS * S, x, pl.ds(at, size), :]
    return V[k // RHS, k % RHS, x + 4, pl.ds(YP + at, size), :]


def local_factor(V, V4, Q, groups, before=None, packed=False):
    def over_groups(body, accs):
        for count, pieces in groups:
            run = functools.partial(body, pieces)
            accs = lax.fori_loop(0, count, run, accs, unroll=min(count, UNROLL))
        return accs

    zero = jnp.zeros((8, 128), F32)
    top = [zero] * COLS
    if before is not None:
        first_row = lax.broadcasted_iota(jnp.int32, (8, 128), 0) == 0
        top = [jnp.where(first_row, before[k : k + 1, :], 0.0) for k in range(COLS)]

    def first_dots(pieces, i, accs):
        accs = list(accs)
        for row, at, size in pieces:
            x = row + i
            q = basis_rows(V, V4, 0, x, at, size)
            for k in range(COLS):
                accs[k] = accs[k] + fold8(q * basis_rows(V, V4, k, x, at, size))
        return tuple(accs)

    start = tuple(top[0] * t for t in top)
    accs = over_groups(first_dots, start)
    lane = lax.broadcasted_iota(jnp.int32, (1, 128), 1)
    lines = [jnp.zeros((1, 128), F32)] * (1 if packed else COLS)
    for j in range(COLS):
        dots = [total(a) for a in accs]
        live = dots[0] >= 1e-37
        length = jnp.sqrt(jnp.where(live, dots[0], 1.0))
        inv = jnp.where(live, 1.0 / length, 0.0)
        for k in range(j, COLS):
            line, at = (0, slot(j, k)) if packed else (k, j)
            lines[line] = jnp.where(lane == at, dots[k - j] * inv, lines[line])
        if j == COLS - 1:
            return lines
        recip = 1.0 / jnp.where(live, dots[0], 1.0)
        alphas = [jnp.broadcast_to(d * recip, (8, 128)) for d in dots[1:]]
        for k in range(j + 1, COLS):
            top[k] = top[k] - alphas[k - j - 1] * top[j]

        def get(k, x, at, size, j=j):
            if j == 0 or k == 0:
                return basis_rows(V, V4, k, x, at, size)
            return Q[k - 1, x, pl.ds(at, size), :]

        def sweep(pieces, i, accs, j=j, get=get, alphas=alphas):
            accs = list(accs)
            for row, at, size in pieces:
                x = row + i
                q = get(j, x, at, size)
                after = None
                for k in range(j + 1, COLS):
                    alpha = jnp.concatenate([alphas[k - j - 1]] * (size // 8), axis=0)
                    value = get(k, x, at, size) - alpha * q
                    Q[k - 1, x, pl.ds(at, size), :] = value
                    if k == j + 1:
                        after = value
                    accs[k - j - 1] = accs[k - j - 1] + fold8(after * value)
            return tuple(accs)

        start = tuple(top[j + 1] * t for t in top[j + 1 :])
        accs = over_groups(sweep, start)


def store_factor(out, lines):
    for k, line in enumerate(lines):
        out[k : k + 1, :] = line


def inner_kernel(X, Y, V_in, U, V, V4, A, factor, Q):
    coefficient_rows(X, Y, U, A, [(4, X + 4)], YP, Y)
    for k in range(1, S + 1):
        power_rows(V, V4, A, k, [(4 + k, X + 4 - k)], [(YP, Y)], 4)
    half = (Y - 16) // 2
    pieces = [(row, at, half) for row in (4, X // 2) for at in (8, 8 + half)]
    store_factor(factor, local_factor(V, V4, Q, [(X // 2 - 4, pieces)]))


def beside_y(Y, k):
    if k == S:
        return [(YP, 8), (YP + Y - 8, 8)]
    return [(YP - 8, 16), (YP + Y - 8, 16)]


def edge_kernel(X, Y, U, V_in, V4_in, A_in, V, V4, A):
    for begin in (YP - 8, YP + Y):
        coefficient_rows(X, Y, U, A, [(4, X + 4)], begin, 8)
    for k in range(1, S + 1):
        power_rows(V, V4, A, k, [(4 + k, X + 4 - k)], beside_y(Y, k), 7)


def near_x(X, k):
    return [(k + 1, k + 4), (X + 4 - k, X + 7 - k)]


def nearest_x(X, k):
    return [(k, k + 1), (X + 7 - k, X + 8 - k)]


def face_kernel(X, Y, x0, x1, before, V_in, V4_in, A_in, U_in, V, V4, A, U, factor, Q):
    for pairing, got in enumerate((x0, x1)):
        high = toward_high("gx", pairing)
        at3, at2 = jnp.where(high, X + 4, 1), jnp.where(high, X + 4, 2)
        for i in range(3):
            for f in range(RHS):
                V[0, f, at3 + i, YP : YP + Y, :] = within("gx", pairing, got[3 * f + i])
        for i in range(2):
            for c in range(4):
                U[c, at2 + i, YP : YP + Y, :] = got[6 + 2 * c + i]
    coefficient_rows(X, Y, U, A, [(2, 4), (X + 4, X + 6)], YP, Y)
    for k in range(1, S + 1):
        power_rows(V, V4, A, k, near_x(X, k), [(YP, Y)], 3)
    half = (Y - 16) // 2
    faces = [(row, at, half) for row in (1, X - 4) for at in (8, 8 + half)]
    sides = [(row, at, 8) for row in (4, X // 2) for at in (0, Y - 8)]
    groups = [(3, faces), (X // 2 - 4, sides)]
    store_factor(factor, local_factor(V, V4, Q, groups, before))


def corner_kernel(X, Y, c0, c1, before, V_in, V4_in, A_in, U_in, V, V4, A, U, packed, Q):
    for pairing, got in enumerate((c0, c1)):
        high = toward_high("gx", pairing)
        for f in range(RHS):
            third = within("gx", pairing, got[f * Y : (f + 1) * Y, :])
            V[1, f, jnp.where(high, X + 6, 1), YP : YP + Y, :] = third
        for row, (f, x, y) in enumerate(corner_cells(X, Y, high, False)):
            value = within("gx", pairing, got[RHS * Y + row : RHS * Y + row + 1, :])
            if f < 2:
                V[0, f, x, y : y + 1, :] = value
            else:
                U[f - 2, x, y : y + 1, :] = value
    for begin in (YP - 8, YP + Y):
        coefficient_rows(X, Y, U, A, [(2, 4), (X + 4, X + 6)], begin, 8)
    for k in range(1, S + 1):
        power_rows(V, V4, A, k, near_x(X, k), beside_y(Y, k), 3)
        if k > 1:
            power_rows(V, V4, A, k, nearest_x(X, k), [(YP, Y)], 1)
    ends = [(row, at, Y // 2) for row in (0, X - 1) for at in (0, Y // 2)]
    sides = [(row, at, 8) for row in (1, X - 4) for at in (0, Y - 8)]
    (line,) = local_factor(V, V4, Q, [(1, ends), (3, sides)], before, packed=True)
    packed[...] = jnp.broadcast_to(line, packed.shape)


def fold_lanes(x):
    parts = [x[:, i : i + 128] for i in range(0, x.shape[1], 128)]
    return functools.reduce(lambda a, b: a + b, parts)


def merged_factor(gathered):
    g = gathered.T
    cols = []
    for k in range(COLS):
        at = slot(0, k)
        cols.append([g[i : i + 8] for i in range(at, at + k + 1, 8)])
    R = {}
    for j in range(COLS):
        dots = []
        for k in range(j, COLS):
            p = fold_lanes(cols[j][0] * cols[k][0])
            if j >= 8:
                p = p + fold_lanes(cols[j][1] * cols[k][1])
            dots.append(total(p))
        inv = 1.0 / jnp.sqrt(dots[0])
        for k in range(j, COLS):
            R[j, k] = dots[k - j] * inv
        recip = 1.0 / dots[0]
        for k in range(j + 1, COLS):
            alpha = dots[k - j] * recip
            for part in range(len(cols[j])):
                cols[k][part] = cols[k][part] - alpha * cols[j][part]
    return R


def inverse(R):
    T = {}
    recip = [1.0 / R[j, j] for j in range(COLS)]
    for j in range(COLS):
        T[j, j] = recip[j]
        for i in range(j):
            s = T[i, i] * R[i, j]
            for k in range(i + 1, j):
                s = s + T[i, k] * R[k, j]
            T[i, j] = -s * recip[j]
    return T


def least_squares(R):
    n = RHS * S
    cols = []
    for c in range(n):
        col = []
        for i in range(c + RHS + 1):
            minus = R[i, c + RHS]
            col.append(R[i, c] - minus if i <= c else -minus)
        cols.append(col)
    upper, target = {}, {}
    recips = []

    def dot(a, b):
        terms = [x * y for x, y in zip(a, b)]
        while len(terms) > 1:
            terms = [x + y for x, y in zip(terms[::2], terms[1::2])] + (
                [terms[-1]] if len(terms) % 2 else []
            )
        return terms[0]

    for j in range(n):
        inv = 1.0 / jnp.sqrt(dot(cols[j], cols[j]))
        recips.append(inv)
        q = [v * inv for v in cols[j]]
        for c in range(j + 1, n):
            w = dot(q, cols[c])
            upper[j, c] = w
            for i in range(len(q)):
                cols[c][i] = cols[c][i] - w * q[i]
        for e in range(RHS):
            target[j, e] = dot(q, [R[i, e] for i in range(e + 1)])
    coef = {}
    for e in range(RHS):
        for j in reversed(range(n)):
            value = target[j, e]
            for later in range(j + 1, n):
                value = value - upper[j, later] * coef[later, e]
            coef[j, e] = value * recips[j]
    return coef


def final_kernel(
    X, Y, scale, gathered, V, V4, ortho, triangle, update, O, W, out_sems
):
    R = merged_factor(gathered[...])
    row = lax.broadcasted_iota(jnp.int32, (16, 128), 0)
    lane = lax.broadcasted_iota(jnp.int32, (16, 128), 1)
    tri = jnp.zeros((16, 128), F32)
    for (i, j), value in R.items():
        tri = jnp.where((row == i) & (lane == j), value * (1.0 / scale), tri)
    triangle[...] = tri[:COLS, :COLS]
    T = inverse(R)
    weights = {}
    for n, ((i, j), value) in enumerate(T.items()):
        weights[i, j] = n
        W[n] = jnp.broadcast_to(value * scale, (8, 128))
    coef = least_squares(R)
    base = len(weights)
    for n, ((k, e), value) in enumerate(coef.items()):
        weights[k, COLS + e] = base + n
        W[base + n] = jnp.broadcast_to(value, (8, 128))

    CH = 32
    XB = 2
    outs = []
    for block in range(X // XB):

        def rows(i, carry, block=block):
            x = block * XB + i
            for at in range(0, Y, CH):
                b = [basis_rows(V, V4, k, x, at, CH) for k in range(COLS)]
                for j in range(COLS + RHS):
                    value = None
                    for k in range(j + 1 if j < COLS else RHS * S):
                        w = jnp.concatenate([W[weights[k, j]]] * (CH // 8), axis=0)
                        value = w * b[k] if value is None else value + w * b[k]
                    O[j, x, pl.ds(at, CH), :] = value
            return carry

        lax.fori_loop(0, XB, rows, 0)
        here = pl.ds(block * XB, XB)
        for copy in (
            pltpu.make_async_copy(
                O.at[pl.ds(0, COLS), here], ortho.at[:, here], out_sems.at[2 * block]
            ),
            pltpu.make_async_copy(
                O.at[pl.ds(COLS, RHS), here], update.at[:, here], out_sems.at[2 * block + 1]
            ),
        ):
            copy.start()
            outs.append(copy)
    for copy in outs:
        copy.wait()


ANY = pl.BlockSpec(memory_space=pl.ANY)
VMEM = pl.BlockSpec(memory_space=pltpu.VMEM)
MIB = 1024 * 1024
PIN, BLOCK, FAR = range(3)


def call(kernel, name, inputs, outputs, scratch=(), aliases={}, limit=4):
    pin = lambda a: pltpu.with_memory_space_constraint(a, pltpu.VMEM)
    spec = lambda place: ANY if place == FAR else VMEM
    return pl.pallas_call(
        kernel,
        out_shape=tuple(
            pltpu.VMEM(o, F32) if place == PIN else jax.ShapeDtypeStruct(o, F32)
            for o, place in outputs
        ),
        in_specs=[spec(place) for _, place in inputs],
        out_specs=tuple(spec(place) for _, place in outputs),
        scratch_shapes=list(scratch),
        input_output_aliases=aliases,
        compiler_params=pltpu.CompilerParams(vmem_limit_bytes=limit * MIB),
        name=name,
    )(*(pin(a) if place == PIN else a for a, place in inputs))


def body(right_sides, diagonal, velocity):
    _, X, Y, Z = right_sides.shape
    nx, ny = lax.axis_size("gx"), lax.axis_size("gy")
    devices = nx * ny
    scale = math.sqrt(X * Y * Z * devices)
    XE, YE = X + 8, Y + 2 * YP
    inputs = [
        (pltpu.with_memory_space_constraint(a, pltpu.HBM), FAR)
        for a in (right_sides, velocity, diagonal)
    ]
    dma = pltpu.SemaphoreType.DMA

    def swap(value, axis, pairing):
        size = lax.axis_size(axis)
        pairs = [(i, (i + 1) % size) for i in range(pairing, size, 2)]
        return lax.ppermute(value, axis, pairs + [(j, i) for i, j in pairs])

    v_shape, u_shape = ((S, RHS, XE, YE, Z), PIN), ((4, XE, YE, Z), PIN)
    x_slab, y_slab = ((14, Y, Z), PIN), ((24 * X, Z), PIN)
    x0, x1, y0, y1, V, U = call(
        functools.partial(pack_kernel, X, Y),
        "pack",
        inputs,
        [x_slab, x_slab, y_slab, y_slab, v_shape, u_shape],
        [dma((3,))],
    )
    x0, x1 = swap(x0, "gx", 0), swap(x1, "gx", 1)
    y1, y0 = swap(y1, "gy", 1), swap(y0, "gy", 0)
    v4_shape, a_shape = ((RHS, X, Y, Z), PIN), ((6, XE, YE, Z), PIN)
    work = pltpu.VMEM((COLS - 1, X, Y, Z), F32)
    factor_shape = ((16, Z), PIN)
    V, V4, A, factor = call(
        functools.partial(inner_kernel, X, Y),
        "inner",
        [(V, PIN), (U, PIN)],
        [v_shape, v4_shape, a_shape, factor_shape],
        [work],
        aliases={0: 0},
        limit=8,
    )
    strip = ((RHS * Y + 2 * CORNER_ROWS, Z), PIN)
    V, U, c0, c1 = call(
        functools.partial(place_y_kernel, X, Y),
        "place_y",
        [(a, PIN) for a in (y0, y1, A, V, U)],
        [v_shape, u_shape, strip, strip],
        aliases={3: 0, 4: 1},
    )
    c0, c1 = swap(c0, "gx", 0), swap(c1, "gx", 1)
    V, V4, A = call(
        functools.partial(edge_kernel, X, Y),
        "edge",
        [(a, PIN) for a in (U, V, V4, A)],
        [v_shape, v4_shape, a_shape],
        aliases={1: 0, 2: 1, 3: 2},
    )
    state = [v_shape, v4_shape, a_shape, u_shape]
    V, V4, A, U, factor = call(
        functools.partial(face_kernel, X, Y),
        "face",
        [(a, PIN) for a in (x0, x1, factor, V, V4, A, U)],
        state + [factor_shape],
        [work],
        aliases={3: 0, 4: 1, 5: 2, 6: 3},
        limit=8,
    )
    V, V4, A, U, packed = call(
        functools.partial(corner_kernel, X, Y),
        "corner",
        [(a, PIN) for a in (c0, c1, factor, V, V4, A, U)],
        state + [((devices, 128), BLOCK)],
        [work],
        aliases={3: 0, 4: 1, 5: 2, 6: 3},
        limit=8,
    )
    gathered = lax.all_to_all(packed, ("gx", "gy"), 0, 0, tiled=True)
    out = [((COLS, X, Y, Z), FAR), ((COLS, COLS), BLOCK), ((RHS, X, Y, Z), FAR)]
    ortho, triangle, update = call(
        functools.partial(final_kernel, X, Y, scale),
        "combine",
        [(gathered, BLOCK), (V, PIN), (V4, PIN)],
        out,
        [
            pltpu.VMEM((COLS + RHS, X, Y, Z), F32),
            pltpu.VMEM((71, 8, 128), F32),
            dma((X,)),
        ],
        limit=10,
    )
    return ortho, triangle, update


def solution(mesh):
    return jax.shard_map(
        body,
        mesh=mesh,
        in_specs=(P(None, "gx", "gy", None), P("gx", "gy", None), P(None, "gx", "gy", None)),
        out_specs=(P(None, "gx", "gy", None), P(), P(None, "gx", "gy", None)),
        check_vma=False,
    )
```

```python
import functools
import math

import jax
import jax.numpy as jnp
from jax import lax
from jax.experimental import pallas as pl
from jax.experimental.pallas import tpu as pltpu
from jax.sharding import PartitionSpec as P

S = 4
RHS = 2
COLS = 10
UNROLL = 4
YP = 16

F32 = jnp.float32
FIELD_CORNER = [(dx, dy) for dx in (1, 2, 3) for dy in (1, 2, 3) if dx + dy <= 4]
COEF_CORNER = [(dx, dy) for dx in (1, 2) for dy in (1, 2) if dx + dy <= 3]
CORNER_ROWS = RHS * len(FIELD_CORNER) + 4 * len(COEF_CORNER)


def slot(i, k):
    return (8 * k if k < 8 else 64 + 16 * (k - 8)) + i


def toward_high(axis, pairing):
    return lax.axis_index(axis) % 2 == pairing


def within(axis, pairing, value):
    if pairing == 0:
        return value
    i = lax.axis_index(axis)
    return jnp.where((i == 0) | (i == lax.axis_size(axis) - 1), 0.0, value)


def pack_kernel(X, Y, rhs, vel, diag, x0, x1, y0, y1, V, U, sems):
    own_x, own_y = pl.ds(4, X), pl.ds(YP, Y)
    copies = [
        (rhs, V.at[0, :, own_x, own_y]),
        (vel, U.at[pl.ds(0, 3), own_x, own_y]),
        (diag, U.at[3, own_x, own_y]),
    ]
    copies = [pltpu.make_async_copy(s, d, sems.at[i]) for i, (s, d) in enumerate(copies)]
    for copy in copies:
        copy.start()
    for copy in copies:
        copy.wait()
    for pairing, out in enumerate((x0, x1)):
        high = toward_high("gx", pairing)
        at3, at2 = jnp.where(high, X + 1, 4), jnp.where(high, X + 2, 4)
        for i in range(3):
            for f in range(RHS):
                out[3 * f + i] = V[0, f, at3 + i, YP : YP + Y, :]
        for i in range(2):
            for c in range(4):
                out[6 + 2 * c + i] = U[c, at2 + i, YP : YP + Y, :]
    first_high = toward_high("gy", 0)
    for f in range(6):
        for x in range(X):
            field = V.at[0, f, 4 + x] if f < 2 else U.at[f - 2, 4 + x]
            low, high = field[YP : YP + 4, :], field[YP + Y - 4 : YP + Y, :]
            at = 4 * (f * X + x)
            y0[at : at + 4, :] = jnp.where(first_high, high, low)
            y1[at : at + 4, :] = jnp.where(first_high, low, high)


def corner_cells(X, Y, high, own):
    cells = []
    for y_low in (True, False):
        for f in range(6):
            for dx, dy in FIELD_CORNER if f < 2 else COEF_CORNER:
                if own:
                    x = jnp.where(high, X + 4 - dx, 3 + dx)
                else:
                    x = jnp.where(high, X + 3 + dx, 4 - dx)
                cells.append((f, x, YP - dy if y_low else YP + Y - 1 + dy))
    return cells


def place_y_kernel(X, Y, y0, y1, A, V_in, U_in, V, U, first, second):
    first_high = toward_high("gy", 0)
    for f in range(6):
        for x in range(X):
            at = 4 * (f * X + x)
            a, b = y0[at : at + 4, :], within("gy", 1, y1[at : at + 4, :])
            field = V.at[0, f, 4 + x] if f < 2 else U.at[f - 2, 4 + x]
            field[YP - 4 : YP, :] = jnp.where(first_high, b, a)
            field[YP + Y : YP + Y + 4, :] = jnp.where(first_high, a, b)
    power_rows(V, None, A, 1, [(6, 7), (X + 1, X + 2)], [(YP, 8), (YP + Y - 8, 8)], 1)
    for pairing, out in enumerate((first, second)):
        high = toward_high("gx", pairing)
        for f in range(RHS):
            out[f * Y : (f + 1) * Y, :] = V[1, f, jnp.where(high, X + 1, 6), YP : YP + Y, :]
        for row, (f, x, y) in enumerate(corner_cells(X, Y, high, True)):
            out[RHS * Y + row : RHS * Y + row + 1, :] = (
                V[0, f, x, y : y + 1, :] if f < 2 else U[f - 2, x, y : y + 1, :]
            )


def total(x):
    return jnp.sum(jnp.sum(x, axis=0, keepdims=True), axis=1, keepdims=True)


def fold8(x):
    rows = x.shape[0]
    parts = [x[8 * i : 8 * i + 8] for i in range(rows // 8)]
    while len(parts) > 1:
        parts = [a + b for a, b in zip(parts[::2], parts[1::2])] + (
            [parts[-1]] if len(parts) % 2 else []
        )
    return parts[0]


def coefficient_rows(X, Y, U, A, rows, begin, size):
    gx, gy = lax.axis_index("gx"), lax.axis_index("gy")
    nx, ny = lax.axis_size("gx"), lax.axis_size("gy")
    here = pl.ds(begin, size)
    yi = begin + lax.broadcasted_iota(jnp.int32, (size, 128), 0)
    zi = lax.broadcasted_iota(jnp.int32, (size, 128), 1)
    y_in = ((yi >= YP) | (gy > 0)) & ((yi < Y + YP) | (gy < ny - 1))

    def one(x):
        x_in = ((x >= 4) | (gx > 0)) & ((x < X + 4) | (gx < nx - 1))
        g = jnp.where(y_in & x_in, 1.0 / (6.0 + U[3, x, here, :]), 0.0)
        for c in range(3):
            ug = U[c, x, here, :] * g
            plus, minus = g + ug, g - ug
            if c == 2:
                plus = jnp.where(zi == 0, 0.0, plus)
                minus = jnp.where(zi == 127, 0.0, minus)
            A[2 * c, x, here, :] = plus
            A[2 * c + 1, x, here, :] = minus

    for_rows(rows, one, 2)


def for_rows(rows, body, unroll):
    def run(i, carry):
        for first, last in rows:
            body(first + i)
        return carry

    lax.fori_loop(0, rows[0][1] - rows[0][0], run, 0, unroll=unroll)


def power_rows(V, V4, A, k, rows, pieces, unroll):
    def one(x):
        for begin, size in pieces:
            here = pl.ds(begin, size)
            a = [A[c, x, here, :] for c in range(6)]
            for f in range(RHS):
                centre = V[k - 1, f, x, here, :]
                value = a[4] * pltpu.roll(centre, 1, 1) + a[5] * pltpu.roll(centre, 127, 1)
                value += a[0] * V[k - 1, f, x - 1, here, :] + a[1] * V[k - 1, f, x + 1, here, :]
                value += a[2] * V[k - 1, f, x, pl.ds(begin - 1, size), :]
                value += a[3] * V[k - 1, f, x, pl.ds(begin + 1, size), :]
                if k == S:
                    V4[f, x - 4, pl.ds(begin - YP, size), :] = value
                else:
                    V[k, f, x, here, :] = value

    for_rows(rows, one, unroll)


def basis_rows(V, V4, k, x, at, size):
    if k >= RHS * S:
        return V4[k - RHS * S, x, pl.ds(at, size), :]
    return V[k // RHS, k % RHS, x + 4, pl.ds(YP + at, size), :]


def local_factor(V, V4, Q, groups, before=None, packed=False):
    def over_groups(body, accs):
        for count, pieces in groups:
            run = functools.partial(body, pieces)
            accs = lax.fori_loop(0, count, run, accs, unroll=min(count, UNROLL))
        return accs

    zero = jnp.zeros((8, 128), F32)
    top = [zero] * COLS
    if before is not None:
        first_row = lax.broadcasted_iota(jnp.int32, (8, 128), 0) == 0
        top = [jnp.where(first_row, before[k : k + 1, :], 0.0) for k in range(COLS)]

    def first_dots(pieces, i, accs):
        accs = list(accs)
        for row, at, size in pieces:
            x = row + i
            q = basis_rows(V, V4, 0, x, at, size)
            for k in range(COLS):
                accs[k] = accs[k] + fold8(q * basis_rows(V, V4, k, x, at, size))
        return tuple(accs)

    start = tuple(top[0] * t for t in top)
    accs = over_groups(first_dots, start)
    lane = lax.broadcasted_iota(jnp.int32, (1, 128), 1)
    lines = [jnp.zeros((1, 128), F32)] * (1 if packed else COLS)
    for j in range(COLS):
        dots = [total(a) for a in accs]
        live = dots[0] >= 1e-37
        length = jnp.sqrt(jnp.where(live, dots[0], 1.0))
        inv = jnp.where(live, 1.0 / length, 0.0)
        for k in range(j, COLS):
            line, at = (0, slot(j, k)) if packed else (k, j)
            lines[line] = jnp.where(lane == at, dots[k - j] * inv, lines[line])
        if j == COLS - 1:
            return lines
        recip = 1.0 / jnp.where(live, dots[0], 1.0)
        alphas = [jnp.broadcast_to(d * recip, (8, 128)) for d in dots[1:]]
        for k in range(j + 1, COLS):
            top[k] = top[k] - alphas[k - j - 1] * top[j]

        def get(k, x, at, size, j=j):
            if j == 0 or k == 0:
                return basis_rows(V, V4, k, x, at, size)
            return Q[k - 1, x, pl.ds(at, size), :]

        def sweep(pieces, i, accs, j=j, get=get, alphas=alphas):
            accs = list(accs)
            for row, at, size in pieces:
                x = row + i
                q = get(j, x, at, size)
                after = None
                for k in range(j + 1, COLS):
                    alpha = jnp.concatenate([alphas[k - j - 1]] * (size // 8), axis=0)
                    value = get(k, x, at, size) - alpha * q
                    Q[k - 1, x, pl.ds(at, size), :] = value
                    if k == j + 1:
                        after = value
                    accs[k - j - 1] = accs[k - j - 1] + fold8(after * value)
            return tuple(accs)

        start = tuple(top[j + 1] * t for t in top[j + 1 :])
        accs = over_groups(sweep, start)


def store_factor(out, lines):
    for k, line in enumerate(lines):
        out[k : k + 1, :] = line


def inner_kernel(X, Y, V_in, U, V, V4, A, factor, Q):
    coefficient_rows(X, Y, U, A, [(4, X + 4)], YP, Y)
    for k in range(1, S + 1):
        power_rows(V, V4, A, k, [(4 + k, X + 4 - k)], [(YP, Y)], 4)
    half = (Y - 16) // 2
    pieces = [(row, at, half) for row in (4, X // 2) for at in (8, 8 + half)]
    store_factor(factor, local_factor(V, V4, Q, [(X // 2 - 4, pieces)]))


def beside_y(Y, k):
    if k == S:
        return [(YP, 8), (YP + Y - 8, 8)]
    return [(YP - 8, 16), (YP + Y - 8, 16)]


def edge_kernel(X, Y, U, V_in, V4_in, A_in, V, V4, A):
    for begin in (YP - 8, YP + Y):
        coefficient_rows(X, Y, U, A, [(4, X + 4)], begin, 8)
    for k in range(1, S + 1):
        power_rows(V, V4, A, k, [(4 + k, X + 4 - k)], beside_y(Y, k), 7)


def near_x(X, k):
    return [(k + 1, k + 4), (X + 4 - k, X + 7 - k)]


def nearest_x(X, k):
    return [(k, k + 1), (X + 7 - k, X + 8 - k)]


def face_kernel(X, Y, x0, x1, before, V_in, V4_in, A_in, U_in, V, V4, A, U, factor, Q):
    for pairing, got in enumerate((x0, x1)):
        high = toward_high("gx", pairing)
        at3, at2 = jnp.where(high, X + 4, 1), jnp.where(high, X + 4, 2)
        for i in range(3):
            for f in range(RHS):
                V[0, f, at3 + i, YP : YP + Y, :] = within("gx", pairing, got[3 * f + i])
        for i in range(2):
            for c in range(4):
                U[c, at2 + i, YP : YP + Y, :] = got[6 + 2 * c + i]
    coefficient_rows(X, Y, U, A, [(2, 4), (X + 4, X + 6)], YP, Y)
    for k in range(1, S + 1):
        power_rows(V, V4, A, k, near_x(X, k), [(YP, Y)], 3)
    half = (Y - 16) // 2
    faces = [(row, at, half) for row in (1, X - 4) for at in (8, 8 + half)]
    sides = [(row, at, 8) for row in (4, X // 2) for at in (0, Y - 8)]
    groups = [(3, faces), (X // 2 - 4, sides)]
    store_factor(factor, local_factor(V, V4, Q, groups, before))


def corner_kernel(X, Y, c0, c1, before, V_in, V4_in, A_in, U_in, V, V4, A, U, packed, Q):
    for pairing, got in enumerate((c0, c1)):
        high = toward_high("gx", pairing)
        for f in range(RHS):
            third = within("gx", pairing, got[f * Y : (f + 1) * Y, :])
            V[1, f, jnp.where(high, X + 6, 1), YP : YP + Y, :] = third
        for row, (f, x, y) in enumerate(corner_cells(X, Y, high, False)):
            value = within("gx", pairing, got[RHS * Y + row : RHS * Y + row + 1, :])
            if f < 2:
                V[0, f, x, y : y + 1, :] = value
            else:
                U[f - 2, x, y : y + 1, :] = value
    for begin in (YP - 8, YP + Y):
        coefficient_rows(X, Y, U, A, [(2, 4), (X + 4, X + 6)], begin, 8)
    for k in range(1, S + 1):
        power_rows(V, V4, A, k, near_x(X, k), beside_y(Y, k), 3)
        if k > 1:
            power_rows(V, V4, A, k, nearest_x(X, k), [(YP, Y)], 1)
    ends = [(row, at, Y // 2) for row in (0, X - 1) for at in (0, Y // 2)]
    sides = [(row, at, 8) for row in (1, X - 4) for at in (0, Y - 8)]
    (line,) = local_factor(V, V4, Q, [(1, ends), (3, sides)], before, packed=True)
    packed[...] = jnp.broadcast_to(line, packed.shape)


def fold_lanes(x):
    parts = [x[:, i : i + 128] for i in range(0, x.shape[1], 128)]
    return functools.reduce(lambda a, b: a + b, parts)


def merged_factor(gathered):
    g = gathered.T
    cols = []
    for k in range(COLS):
        at = slot(0, k)
        cols.append([g[i : i + 8] for i in range(at, at + k + 1, 8)])
    R = {}
    for j in range(COLS):
        dots = []
        for k in range(j, COLS):
            p = fold_lanes(cols[j][0] * cols[k][0])
            if j >= 8:
                p = p + fold_lanes(cols[j][1] * cols[k][1])
            dots.append(total(p))
        inv = 1.0 / jnp.sqrt(dots[0])
        for k in range(j, COLS):
            R[j, k] = dots[k - j] * inv
        recip = 1.0 / dots[0]
        for k in range(j + 1, COLS):
            alpha = dots[k - j] * recip
            for part in range(len(cols[j])):
                cols[k][part] = cols[k][part] - alpha * cols[j][part]
    return R


def inverse(R):
    T = {}
    recip = [1.0 / R[j, j] for j in range(COLS)]
    for j in range(COLS):
        T[j, j] = recip[j]
        for i in range(j):
            s = T[i, i] * R[i, j]
            for k in range(i + 1, j):
                s = s + T[i, k] * R[k, j]
            T[i, j] = -s * recip[j]
    return T


def least_squares(R):
    n = RHS * S
    cols = []
    for c in range(n):
        col = []
        for i in range(c + RHS + 1):
            minus = R[i, c + RHS]
            col.append(R[i, c] - minus if i <= c else -minus)
        cols.append(col)
    upper, target = {}, {}
    recips = []

    def dot(a, b):
        terms = [x * y for x, y in zip(a, b)]
        while len(terms) > 1:
            terms = [x + y for x, y in zip(terms[::2], terms[1::2])] + (
                [terms[-1]] if len(terms) % 2 else []
            )
        return terms[0]

    for j in range(n):
        inv = 1.0 / jnp.sqrt(dot(cols[j], cols[j]))
        recips.append(inv)
        q = [v * inv for v in cols[j]]
        for c in range(j + 1, n):
            w = dot(q, cols[c])
            upper[j, c] = w
            for i in range(len(q)):
                cols[c][i] = cols[c][i] - w * q[i]
        for e in range(RHS):
            target[j, e] = dot(q, [R[i, e] for i in range(e + 1)])
    coef = {}
    for e in range(RHS):
        for j in reversed(range(n)):
            value = target[j, e]
            for later in range(j + 1, n):
                value = value - upper[j, later] * coef[later, e]
            coef[j, e] = value * recips[j]
    return coef


def final_kernel(
    X, Y, scale, gathered, V, V4, ortho, triangle, update, O, W, out_sems
):
    R = merged_factor(gathered[...])
    row = lax.broadcasted_iota(jnp.int32, (16, 128), 0)
    lane = lax.broadcasted_iota(jnp.int32, (16, 128), 1)
    tri = jnp.zeros((16, 128), F32)
    for (i, j), value in R.items():
        tri = jnp.where((row == i) & (lane == j), value * (1.0 / scale), tri)
    triangle[...] = tri[:COLS, :COLS]
    T = inverse(R)
    weights = {}
    for n, ((i, j), value) in enumerate(T.items()):
        weights[i, j] = n
        W[n] = jnp.broadcast_to(value * scale, (8, 128))
    coef = least_squares(R)
    base = len(weights)
    for n, ((k, e), value) in enumerate(coef.items()):
        weights[k, COLS + e] = base + n
        W[base + n] = jnp.broadcast_to(value, (8, 128))

    CH = 32
    XB = 2
    outs = []
    for block in range(X // XB):

        def rows(i, carry, block=block):
            x = block * XB + i
            for at in range(0, Y, CH):
                b = [basis_rows(V, V4, k, x, at, CH) for k in range(COLS)]
                for j in range(COLS + RHS):
                    value = None
                    for k in range(j + 1 if j < COLS else RHS * S):
                        w = jnp.concatenate([W[weights[k, j]]] * (CH // 8), axis=0)
                        value = w * b[k] if value is None else value + w * b[k]
                    O[j, x, pl.ds(at, CH), :] = value
            return carry

        lax.fori_loop(0, XB, rows, 0)
        here = pl.ds(block * XB, XB)
        for copy in (
            pltpu.make_async_copy(
                O.at[pl.ds(0, COLS), here], ortho.at[:, here], out_sems.at[2 * block]
            ),
            pltpu.make_async_copy(
                O.at[pl.ds(COLS, RHS), here], update.at[:, here], out_sems.at[2 * block + 1]
            ),
        ):
            copy.start()
            outs.append(copy)
    for copy in outs:
        copy.wait()


ANY = pl.BlockSpec(memory_space=pl.ANY)
VMEM = pl.BlockSpec(memory_space=pltpu.VMEM)
MIB = 1024 * 1024
PIN, BLOCK, FAR = range(3)


def call(kernel, name, inputs, outputs, scratch=(), aliases={}, limit=4):
    pin = lambda a: pltpu.with_memory_space_constraint(a, pltpu.VMEM)
    spec = lambda place: ANY if place == FAR else VMEM
    return pl.pallas_call(
        kernel,
        out_shape=tuple(
            pltpu.VMEM(o, F32) if place == PIN else jax.ShapeDtypeStruct(o, F32)
            for o, place in outputs
        ),
        in_specs=[spec(place) for _, place in inputs],
        out_specs=tuple(spec(place) for _, place in outputs),
        scratch_shapes=list(scratch),
        input_output_aliases=aliases,
        compiler_params=pltpu.CompilerParams(vmem_limit_bytes=limit * MIB),
        name=name,
    )(*(pin(a) if place == PIN else a for a, place in inputs))


def body(right_sides, diagonal, velocity):
    _, X, Y, Z = right_sides.shape
    nx, ny = lax.axis_size("gx"), lax.axis_size("gy")
    devices = nx * ny
    scale = math.sqrt(X * Y * Z * devices)
    XE, YE = X + 8, Y + 2 * YP
    inputs = [
        (pltpu.with_memory_space_constraint(a, pltpu.HBM), FAR)
        for a in (right_sides, velocity, diagonal)
    ]
    dma = pltpu.SemaphoreType.DMA

    def swap(value, axis, pairing):
        size = lax.axis_size(axis)
        pairs = [(i, i + 1) for i in range(pairing, size - 1, 2)]
        ends = [(0, 0), (size - 1, size - 1)] if pairing else []
        return lax.ppermute(value, axis, pairs + [(j, i) for i, j in pairs] + ends)

    v_shape, u_shape = ((S, RHS, XE, YE, Z), PIN), ((4, XE, YE, Z), PIN)
    x_slab, y_slab = ((14, Y, Z), PIN), ((24 * X, Z), PIN)
    x0, x1, y0, y1, V, U = call(
        functools.partial(pack_kernel, X, Y),
        "pack",
        inputs,
        [x_slab, x_slab, y_slab, y_slab, v_shape, u_shape],
        [dma((3,))],
    )
    x0, x1 = swap(x0, "gx", 0), swap(x1, "gx", 1)
    y1, y0 = swap(y1, "gy", 1), swap(y0, "gy", 0)
    v4_shape, a_shape = ((RHS, X, Y, Z), PIN), ((6, XE, YE, Z), PIN)
    work = pltpu.VMEM((COLS - 1, X, Y, Z), F32)
    factor_shape = ((16, Z), PIN)
    V, V4, A, factor = call(
        functools.partial(inner_kernel, X, Y),
        "inner",
        [(V, PIN), (U, PIN)],
        [v_shape, v4_shape, a_shape, factor_shape],
        [work],
        aliases={0: 0},
        limit=8,
    )
    strip = ((RHS * Y + 2 * CORNER_ROWS, Z), PIN)
    V, U, c0, c1 = call(
        functools.partial(place_y_kernel, X, Y),
        "place_y",
        [(a, PIN) for a in (y0, y1, A, V, U)],
        [v_shape, u_shape, strip, strip],
        aliases={3: 0, 4: 1},
    )
    c0, c1 = swap(c0, "gx", 0), swap(c1, "gx", 1)
    V, V4, A = call(
        functools.partial(edge_kernel, X, Y),
        "edge",
        [(a, PIN) for a in (U, V, V4, A)],
        [v_shape, v4_shape, a_shape],
        aliases={1: 0, 2: 1, 3: 2},
    )
    state = [v_shape, v4_shape, a_shape, u_shape]
    V, V4, A, U, factor = call(
        functools.partial(face_kernel, X, Y),
        "face",
        [(a, PIN) for a in (x0, x1, factor, V, V4, A, U)],
        state + [factor_shape],
        [work],
        aliases={3: 0, 4: 1, 5: 2, 6: 3},
        limit=8,
    )
    V, V4, A, U, packed = call(
        functools.partial(corner_kernel, X, Y),
        "corner",
        [(a, PIN) for a in (c0, c1, factor, V, V4, A, U)],
        state + [((devices, 128), BLOCK)],
        [work],
        aliases={3: 0, 4: 1, 5: 2, 6: 3},
        limit=8,
    )
    gathered = lax.all_to_all(packed, ("gx", "gy"), 0, 0, tiled=True)
    out = [((COLS, X, Y, Z), FAR), ((COLS, COLS), BLOCK), ((RHS, X, Y, Z), FAR)]
    ortho, triangle, update = call(
        functools.partial(final_kernel, X, Y, scale),
        "combine",
        [(gathered, BLOCK), (V, PIN), (V4, PIN)],
        out,
        [
            pltpu.VMEM((COLS + RHS, X, Y, Z), F32),
            pltpu.VMEM((71, 8, 128), F32),
            dma((X,)),
        ],
        limit=10,
    )
    return ortho, triangle, update


def solution(mesh):
    return jax.shard_map(
        body,
        mesh=mesh,
        in_specs=(P(None, "gx", "gy", None), P("gx", "gy", None), P(None, "gx", "gy", None)),
        out_specs=(P(None, "gx", "gy", None), P(), P(None, "gx", "gy", None)),
        check_vma=False,
    )
```

```python
import functools
import math

import jax
import jax.numpy as jnp
from jax import lax
from jax.experimental import pallas as pl
from jax.experimental.pallas import tpu as pltpu
from jax.sharding import PartitionSpec as P

S = 4
RHS = 2
COLS = 10
UNROLL = 4
YP = 16

F32 = jnp.float32
FIELD_CORNER = [(dx, dy) for dx in (1, 2, 3) for dy in (1, 2, 3) if dx + dy <= 4]
COEF_CORNER = [(dx, dy) for dx in (1, 2) for dy in (1, 2) if dx + dy <= 3]
CORNER_ROWS = RHS * len(FIELD_CORNER) + 4 * len(COEF_CORNER)


def slot(i, k):
    return (8 * k if k < 8 else 64 + 16 * (k - 8)) + i


def toward_high(axis, pairing):
    return lax.axis_index(axis) % 2 == pairing


def within(axis, pairing, value):
    if pairing == 0:
        return value
    i = lax.axis_index(axis)
    return jnp.where((i == 0) | (i == lax.axis_size(axis) - 1), 0.0, value)


def pack_kernel(X, Y, rhs, vel, diag, x0, x1, y0, y1, V, U, sems):
    own_x, own_y = pl.ds(4, X), pl.ds(YP, Y)
    copies = [
        (rhs, V.at[0, :, own_x, own_y]),
        (vel, U.at[pl.ds(0, 3), own_x, own_y]),
        (diag, U.at[3, own_x, own_y]),
    ]
    copies = [pltpu.make_async_copy(s, d, sems.at[i]) for i, (s, d) in enumerate(copies)]
    for copy in copies:
        copy.start()
    for copy in copies:
        copy.wait()
    for pairing, out in enumerate((x0, x1)):
        high = toward_high("gx", pairing)
        at3, at2 = jnp.where(high, X + 1, 4), jnp.where(high, X + 2, 4)
        for i in range(3):
            for f in range(RHS):
                out[3 * f + i] = V[0, f, at3 + i, YP : YP + Y, :]
        for i in range(2):
            for c in range(4):
                out[6 + 2 * c + i] = U[c, at2 + i, YP : YP + Y, :]
    first_high = toward_high("gy", 0)
    for f in range(6):
        for x in range(X):
            field = V.at[0, f, 4 + x] if f < 2 else U.at[f - 2, 4 + x]
            low, high = field[YP : YP + 4, :], field[YP + Y - 4 : YP + Y, :]
            at = 4 * (f * X + x)
            y0[at : at + 4, :] = jnp.where(first_high, high, low)
            y1[at : at + 4, :] = jnp.where(first_high, low, high)


def corner_cells(X, Y, high, own):
    cells = []
    for y_low in (True, False):
        for f in range(6):
            for dx, dy in FIELD_CORNER if f < 2 else COEF_CORNER:
                if own:
                    x = jnp.where(high, X + 4 - dx, 3 + dx)
                else:
                    x = jnp.where(high, X + 3 + dx, 4 - dx)
                cells.append((f, x, YP - dy if y_low else YP + Y - 1 + dy))
    return cells


def place_y_kernel(X, Y, y0, y1, A, V_in, U_in, V, U, first, second):
    first_high = toward_high("gy", 0)
    for f in range(6):
        for x in range(X):
            at = 4 * (f * X + x)
            a, b = y0[at : at + 4, :], within("gy", 1, y1[at : at + 4, :])
            field = V.at[0, f, 4 + x] if f < 2 else U.at[f - 2, 4 + x]
            field[YP - 4 : YP, :] = jnp.where(first_high, b, a)
            field[YP + Y : YP + Y + 4, :] = jnp.where(first_high, a, b)
    power_rows(V, None, A, 1, [(6, 7), (X + 1, X + 2)], [(YP, 8), (YP + Y - 8, 8)], 1)
    for pairing, out in enumerate((first, second)):
        high = toward_high("gx", pairing)
        for f in range(RHS):
            out[f * Y : (f + 1) * Y, :] = V[1, f, jnp.where(high, X + 1, 6), YP : YP + Y, :]
        for row, (f, x, y) in enumerate(corner_cells(X, Y, high, True)):
            out[RHS * Y + row : RHS * Y + row + 1, :] = (
                V[0, f, x, y : y + 1, :] if f < 2 else U[f - 2, x, y : y + 1, :]
            )


def total(x):
    return jnp.sum(jnp.sum(x, axis=0, keepdims=True), axis=1, keepdims=True)


def fold8(x):
    rows = x.shape[0]
    parts = [x[8 * i : 8 * i + 8] for i in range(rows // 8)]
    while len(parts) > 1:
        parts = [a + b for a, b in zip(parts[::2], parts[1::2])] + (
            [parts[-1]] if len(parts) % 2 else []
        )
    return parts[0]


def coefficient_rows(X, Y, U, A, rows, begin, size):
    gx, gy = lax.axis_index("gx"), lax.axis_index("gy")
    nx, ny = lax.axis_size("gx"), lax.axis_size("gy")
    here = pl.ds(begin, size)
    yi = begin + lax.broadcasted_iota(jnp.int32, (size, 128), 0)
    zi = lax.broadcasted_iota(jnp.int32, (size, 128), 1)
    y_in = ((yi >= YP) | (gy > 0)) & ((yi < Y + YP) | (gy < ny - 1))

    def one(x):
        x_in = ((x >= 4) | (gx > 0)) & ((x < X + 4) | (gx < nx - 1))
        g = jnp.where(y_in & x_in, 1.0 / (6.0 + U[3, x, here, :]), 0.0)
        for c in range(3):
            ug = U[c, x, here, :] * g
            plus, minus = g + ug, g - ug
            if c == 2:
                plus = jnp.where(zi == 0, 0.0, plus)
                minus = jnp.where(zi == 127, 0.0, minus)
            A[2 * c, x, here, :] = plus
            A[2 * c + 1, x, here, :] = minus

    for_rows(rows, one, 2)


def for_rows(rows, body, unroll):
    def run(i, carry):
        for first, last in rows:
            body(first + i)
        return carry

    lax.fori_loop(0, rows[0][1] - rows[0][0], run, 0, unroll=unroll)


def power_rows(V, V4, A, k, rows, pieces, unroll):
    def one(x):
        for begin, size in pieces:
            here = pl.ds(begin, size)
            a = [A[c, x, here, :] for c in range(6)]
            for f in range(RHS):
                centre = V[k - 1, f, x, here, :]
                value = a[4] * pltpu.roll(centre, 1, 1) + a[5] * pltpu.roll(centre, 127, 1)
                value += a[0] * V[k - 1, f, x - 1, here, :] + a[1] * V[k - 1, f, x + 1, here, :]
                value += a[2] * V[k - 1, f, x, pl.ds(begin - 1, size), :]
                value += a[3] * V[k - 1, f, x, pl.ds(begin + 1, size), :]
                if k == S:
                    V4[f, x - 4, pl.ds(begin - YP, size), :] = value
                else:
                    V[k, f, x, here, :] = value

    for_rows(rows, one, unroll)


def basis_rows(V, V4, k, x, at, size):
    if k >= RHS * S:
        return V4[k - RHS * S, x, pl.ds(at, size), :]
    return V[k // RHS, k % RHS, x + 4, pl.ds(YP + at, size), :]


def local_factor(V, V4, Q, groups, before=None, packed=False):
    def over_groups(body, accs):
        for count, pieces in groups:
            run = functools.partial(body, pieces)
            accs = lax.fori_loop(0, count, run, accs, unroll=min(count, UNROLL))
        return accs

    zero = jnp.zeros((8, 128), F32)
    top = [zero] * COLS
    if before is not None:
        first_row = lax.broadcasted_iota(jnp.int32, (8, 128), 0) == 0
        top = [jnp.where(first_row, before[k : k + 1, :], 0.0) for k in range(COLS)]

    def first_dots(pieces, i, accs):
        accs = list(accs)
        for row, at, size in pieces:
            x = row + i
            q = basis_rows(V, V4, 0, x, at, size)
            for k in range(COLS):
                accs[k] = accs[k] + fold8(q * basis_rows(V, V4, k, x, at, size))
        return tuple(accs)

    start = tuple(top[0] * t for t in top)
    accs = over_groups(first_dots, start)
    lane = lax.broadcasted_iota(jnp.int32, (1, 128), 1)
    lines = [jnp.zeros((1, 128), F32)] * (1 if packed else COLS)
    for j in range(COLS):
        dots = [total(a) for a in accs]
        live = dots[0] >= 1e-37
        length = jnp.sqrt(jnp.where(live, dots[0], 1.0))
        inv = jnp.where(live, 1.0 / length, 0.0)
        for k in range(j, COLS):
            line, at = (0, slot(j, k)) if packed else (k, j)
            lines[line] = jnp.where(lane == at, dots[k - j] * inv, lines[line])
        if j == COLS - 1:
            return lines
        recip = 1.0 / jnp.where(live, dots[0], 1.0)
        alphas = [jnp.broadcast_to(d * recip, (8, 128)) for d in dots[1:]]
        for k in range(j + 1, COLS):
            top[k] = top[k] - alphas[k - j - 1] * top[j]

        def get(k, x, at, size, j=j):
            if j == 0 or k == 0:
                return basis_rows(V, V4, k, x, at, size)
            return Q[k - 1, x, pl.ds(at, size), :]

        def sweep(pieces, i, accs, j=j, get=get, alphas=alphas):
            accs = list(accs)
            for row, at, size in pieces:
                x = row + i
                q = get(j, x, at, size)
                after = None
                for k in range(j + 1, COLS):
                    alpha = jnp.concatenate([alphas[k - j - 1]] * (size // 8), axis=0)
                    value = get(k, x, at, size) - alpha * q
                    Q[k - 1, x, pl.ds(at, size), :] = value
                    if k == j + 1:
                        after = value
                    accs[k - j - 1] = accs[k - j - 1] + fold8(after * value)
            return tuple(accs)

        start = tuple(top[j + 1] * t for t in top[j + 1 :])
        accs = over_groups(sweep, start)


def store_factor(out, lines):
    for k, line in enumerate(lines):
        out[k : k + 1, :] = line


def inner_kernel(X, Y, V_in, U, V, V4, A, factor, Q):
    coefficient_rows(X, Y, U, A, [(4, X + 4)], YP, Y)
    for k in range(1, S + 1):
        power_rows(V, V4, A, k, [(4 + k, X + 4 - k)], [(YP, Y)], 4)
    half = (Y - 16) // 2
    pieces = [(row, at, half) for row in (4, X // 2) for at in (8, 8 + half)]
    store_factor(factor, local_factor(V, V4, Q, [(X // 2 - 4, pieces)]))


def beside_y(Y, k):
    if k == S:
        return [(YP, 8), (YP + Y - 8, 8)]
    return [(YP - 8, 16), (YP + Y - 8, 16)]


def edge_kernel(X, Y, U, V_in, V4_in, A_in, V, V4, A):
    for begin in (YP - 8, YP + Y):
        coefficient_rows(X, Y, U, A, [(4, X + 4)], begin, 8)
    for k in range(1, S + 1):
        power_rows(V, V4, A, k, [(4 + k, X + 4 - k)], beside_y(Y, k), 7)


def near_x(X, k):
    return [(k + 1, k + 4), (X + 4 - k, X + 7 - k)]


def nearest_x(X, k):
    return [(k, k + 1), (X + 7 - k, X + 8 - k)]


def face_kernel(X, Y, x0, x1, before, V_in, V4_in, A_in, U_in, V, V4, A, U, factor, Q):
    for pairing, got in enumerate((x0, x1)):
        high = toward_high("gx", pairing)
        at3, at2 = jnp.where(high, X + 4, 1), jnp.where(high, X + 4, 2)
        for i in range(3):
            for f in range(RHS):
                V[0, f, at3 + i, YP : YP + Y, :] = within("gx", pairing, got[3 * f + i])
        for i in range(2):
            for c in range(4):
                U[c, at2 + i, YP : YP + Y, :] = got[6 + 2 * c + i]
    coefficient_rows(X, Y, U, A, [(2, 4), (X + 4, X + 6)], YP, Y)
    for k in range(1, S + 1):
        power_rows(V, V4, A, k, near_x(X, k), [(YP, Y)], 3)
    half = (Y - 16) // 2
    faces = [(row, at, half) for row in (1, X - 4) for at in (8, 8 + half)]
    sides = [(row, at, 8) for row in (4, X // 2) for at in (0, Y - 8)]
    groups = [(3, faces), (X // 2 - 4, sides)]
    store_factor(factor, local_factor(V, V4, Q, groups, before))


def corner_kernel(X, Y, c0, c1, before, V_in, V4_in, A_in, U_in, V, V4, A, U, packed, Q):
    for pairing, got in enumerate((c0, c1)):
        high = toward_high("gx", pairing)
        for f in range(RHS):
            third = within("gx", pairing, got[f * Y : (f + 1) * Y, :])
            V[1, f, jnp.where(high, X + 6, 1), YP : YP + Y, :] = third
        for row, (f, x, y) in enumerate(corner_cells(X, Y, high, False)):
            value = within("gx", pairing, got[RHS * Y + row : RHS * Y + row + 1, :])
            if f < 2:
                V[0, f, x, y : y + 1, :] = value
            else:
                U[f - 2, x, y : y + 1, :] = value
    for begin in (YP - 8, YP + Y):
        coefficient_rows(X, Y, U, A, [(2, 4), (X + 4, X + 6)], begin, 8)
    for k in range(1, S + 1):
        power_rows(V, V4, A, k, near_x(X, k), beside_y(Y, k), 3)
        if k > 1:
            power_rows(V, V4, A, k, nearest_x(X, k), [(YP, Y)], 1)
    ends = [(row, at, Y // 2) for row in (0, X - 1) for at in (0, Y // 2)]
    sides = [(row, at, 8) for row in (1, X - 4) for at in (0, Y - 8)]
    (line,) = local_factor(V, V4, Q, [(1, ends), (3, sides)], before, packed=True)
    packed[...] = jnp.broadcast_to(line, packed.shape)


def fold_lanes(x):
    parts = [x[:, i : i + 128] for i in range(0, x.shape[1], 128)]
    return functools.reduce(lambda a, b: a + b, parts)


def merged_factor(gathered):
    g = gathered.T
    cols = []
    for k in range(COLS):
        at = slot(0, k)
        cols.append([g[i : i + 8] for i in range(at, at + k + 1, 8)])
    R = {}
    for j in range(COLS):
        dots = []
        for k in range(j, COLS):
            p = fold_lanes(cols[j][0] * cols[k][0])
            if j >= 8:
                p = p + fold_lanes(cols[j][1] * cols[k][1])
            dots.append(total(p))
        inv = 1.0 / jnp.sqrt(dots[0])
        for k in range(j, COLS):
            R[j, k] = dots[k - j] * inv
        recip = 1.0 / dots[0]
        for k in range(j + 1, COLS):
            alpha = dots[k - j] * recip
            for part in range(len(cols[j])):
                cols[k][part] = cols[k][part] - alpha * cols[j][part]
    return R


def inverse(R):
    T = {}
    recip = [1.0 / R[j, j] for j in range(COLS)]
    for j in range(COLS):
        T[j, j] = recip[j]
        for i in range(j):
            s = T[i, i] * R[i, j]
            for k in range(i + 1, j):
                s = s + T[i, k] * R[k, j]
            T[i, j] = -s * recip[j]
    return T


def least_squares(R):
    n = RHS * S
    cols = []
    for c in range(n):
        col = []
        for i in range(c + RHS + 1):
            minus = R[i, c + RHS]
            col.append(R[i, c] - minus if i <= c else -minus)
        cols.append(col)
    upper, target = {}, {}
    recips = []

    def dot(a, b):
        terms = [x * y for x, y in zip(a, b)]
        while len(terms) > 1:
            terms = [x + y for x, y in zip(terms[::2], terms[1::2])] + (
                [terms[-1]] if len(terms) % 2 else []
            )
        return terms[0]

    for j in range(n):
        inv = 1.0 / jnp.sqrt(dot(cols[j], cols[j]))
        recips.append(inv)
        q = [v * inv for v in cols[j]]
        for c in range(j + 1, n):
            w = dot(q, cols[c])
            upper[j, c] = w
            for i in range(len(q)):
                cols[c][i] = cols[c][i] - w * q[i]
        for e in range(RHS):
            target[j, e] = dot(q, [R[i, e] for i in range(e + 1)])
    coef = {}
    for e in range(RHS):
        for j in reversed(range(n)):
            value = target[j, e]
            for later in range(j + 1, n):
                value = value - upper[j, later] * coef[later, e]
            coef[j, e] = value * recips[j]
    return coef


def final_kernel(
    X, Y, scale, gathered, V, V4, ortho, triangle, update, O, W, out_sems
):
    R = merged_factor(gathered[...])
    row = lax.broadcasted_iota(jnp.int32, (16, 128), 0)
    lane = lax.broadcasted_iota(jnp.int32, (16, 128), 1)
    tri = jnp.zeros((16, 128), F32)
    for (i, j), value in R.items():
        tri = jnp.where((row == i) & (lane == j), value * (1.0 / scale), tri)
    triangle[...] = tri[:COLS, :COLS]
    T = inverse(R)
    weights = {}
    for n, ((i, j), value) in enumerate(T.items()):
        weights[i, j] = n
        W[n] = jnp.broadcast_to(value * scale, (8, 128))
    coef = least_squares(R)
    base = len(weights)
    for n, ((k, e), value) in enumerate(coef.items()):
        weights[k, COLS + e] = base + n
        W[base + n] = jnp.broadcast_to(value, (8, 128))

    CH = 32
    XB = 2
    outs = []
    for block in range(X // XB):

        def rows(i, carry, block=block):
            x = block * XB + i
            for at in range(0, Y, CH):
                b = [basis_rows(V, V4, k, x, at, CH) for k in range(COLS)]
                for j in range(COLS + RHS):
                    value = None
                    for k in range(j + 1 if j < COLS else RHS * S):
                        w = jnp.concatenate([W[weights[k, j]]] * (CH // 8), axis=0)
                        value = w * b[k] if value is None else value + w * b[k]
                    O[j, x, pl.ds(at, CH), :] = value
            return carry

        lax.fori_loop(0, XB, rows, 0)
        here = pl.ds(block * XB, XB)
        for copy in (
            pltpu.make_async_copy(
                O.at[pl.ds(0, COLS), here], ortho.at[:, here], out_sems.at[2 * block]
            ),
            pltpu.make_async_copy(
                O.at[pl.ds(COLS, RHS), here], update.at[:, here], out_sems.at[2 * block + 1]
            ),
        ):
            copy.start()
            outs.append(copy)
    for copy in outs:
        copy.wait()


ANY = pl.BlockSpec(memory_space=pl.ANY)
VMEM = pl.BlockSpec(memory_space=pltpu.VMEM)
MIB = 1024 * 1024
PIN, BLOCK, FAR = range(3)


def call(kernel, name, inputs, outputs, scratch=(), aliases={}, limit=4):
    pin = lambda a: pltpu.with_memory_space_constraint(a, pltpu.VMEM)
    spec = lambda place: ANY if place == FAR else VMEM
    return pl.pallas_call(
        kernel,
        out_shape=tuple(
            pltpu.VMEM(o, F32) if place == PIN else jax.ShapeDtypeStruct(o, F32)
            for o, place in outputs
        ),
        in_specs=[spec(place) for _, place in inputs],
        out_specs=tuple(spec(place) for _, place in outputs),
        scratch_shapes=list(scratch),
        input_output_aliases=aliases,
        compiler_params=pltpu.CompilerParams(vmem_limit_bytes=limit * MIB),
        name=name,
    )(*(pin(a) if place == PIN else a for a, place in inputs))


def body(right_sides, diagonal, velocity):
    _, X, Y, Z = right_sides.shape
    nx, ny = lax.axis_size("gx"), lax.axis_size("gy")
    devices = nx * ny
    scale = math.sqrt(X * Y * Z * devices)
    XE, YE = X + 8, Y + 2 * YP
    inputs = [
        (pltpu.with_memory_space_constraint(a, pltpu.HBM), FAR)
        for a in (right_sides, velocity, diagonal)
    ]
    dma = pltpu.SemaphoreType.DMA

    def swap(value, axis, pairing):
        size = lax.axis_size(axis)
        pairs = [(i, (i + 1) % size) for i in range(pairing, size, 2)]
        if axis == "gx" and pairing == 1:
            pairs = [(i * ny + j, (i + 1) * ny + j) for i in range(1, nx - 1, 2) for j in range(ny)]
            pairs += [(i * ny + j, i * ny + j + 1) for i in (0, nx - 1) for j in range(0, ny, 2)]
            axis = ("gx", "gy")
        return lax.ppermute(value, axis, pairs + [(j, i) for i, j in pairs])

    v_shape, u_shape = ((S, RHS, XE, YE, Z), PIN), ((4, XE, YE, Z), PIN)
    x_slab, y_slab = ((14, Y, Z), PIN), ((24 * X, Z), PIN)
    x0, x1, y0, y1, V, U = call(
        functools.partial(pack_kernel, X, Y),
        "pack",
        inputs,
        [x_slab, x_slab, y_slab, y_slab, v_shape, u_shape],
        [dma((3,))],
    )
    x0, x1 = swap(x0, "gx", 0), swap(x1, "gx", 1)
    y1, y0 = swap(y1, "gy", 1), swap(y0, "gy", 0)
    v4_shape, a_shape = ((RHS, X, Y, Z), PIN), ((6, XE, YE, Z), PIN)
    work = pltpu.VMEM((COLS - 1, X, Y, Z), F32)
    factor_shape = ((16, Z), PIN)
    V, V4, A, factor = call(
        functools.partial(inner_kernel, X, Y),
        "inner",
        [(V, PIN), (U, PIN)],
        [v_shape, v4_shape, a_shape, factor_shape],
        [work],
        aliases={0: 0},
        limit=8,
    )
    strip = ((RHS * Y + 2 * CORNER_ROWS, Z), PIN)
    V, U, c0, c1 = call(
        functools.partial(place_y_kernel, X, Y),
        "place_y",
        [(a, PIN) for a in (y0, y1, A, V, U)],
        [v_shape, u_shape, strip, strip],
        aliases={3: 0, 4: 1},
    )
    c0, c1 = swap(c0, "gx", 0), swap(c1, "gx", 1)
    V, V4, A = call(
        functools.partial(edge_kernel, X, Y),
        "edge",
        [(a, PIN) for a in (U, V, V4, A)],
        [v_shape, v4_shape, a_shape],
        aliases={1: 0, 2: 1, 3: 2},
    )
    state = [v_shape, v4_shape, a_shape, u_shape]
    V, V4, A, U, factor = call(
        functools.partial(face_kernel, X, Y),
        "face",
        [(a, PIN) for a in (x0, x1, factor, V, V4, A, U)],
        state + [factor_shape],
        [work],
        aliases={3: 0, 4: 1, 5: 2, 6: 3},
        limit=8,
    )
    V, V4, A, U, packed = call(
        functools.partial(corner_kernel, X, Y),
        "corner",
        [(a, PIN) for a in (c0, c1, factor, V, V4, A, U)],
        state + [((devices, 128), BLOCK)],
        [work],
        aliases={3: 0, 4: 1, 5: 2, 6: 3},
        limit=8,
    )
    gathered = lax.all_to_all(packed, ("gx", "gy"), 0, 0, tiled=True)
    out = [((COLS, X, Y, Z), FAR), ((COLS, COLS), BLOCK), ((RHS, X, Y, Z), FAR)]
    ortho, triangle, update = call(
        functools.partial(final_kernel, X, Y, scale),
        "combine",
        [(gathered, BLOCK), (V, PIN), (V4, PIN)],
        out,
        [
            pltpu.VMEM((COLS + RHS, X, Y, Z), F32),
            pltpu.VMEM((71, 8, 128), F32),
            dma((X,)),
        ],
        limit=10,
    )
    return ortho, triangle, update


def solution(mesh):
    return jax.shard_map(
        body,
        mesh=mesh,
        in_specs=(P(None, "gx", "gy", None), P("gx", "gy", None), P(None, "gx", "gy", None)),
        out_specs=(P(None, "gx", "gy", None), P(), P(None, "gx", "gy", None)),
        check_vma=False,
    )
```
